32 devices in a mesh: dp: 8 (over y, x, core), mp: 4 (over z).
Axes of the slice: x: 2, y: 2, z: 4, core: 2. Of those that a mesh axis runs over, the one named last changes fastest.
Arguments:
- tokens: bfloat16 [8192, 768], P(('dp', 'mp')), may hold values from -6 to 6
- segment_ids: int32 [8, 1024], P('dp'), may hold values from 0 to 8, as said below
- pair_doc: int32 [8, 4], P('dp'), may hold values from 0 to 31
- slot_of: int32 [8], replicated, may hold values from 0 to 15, as said below
- master: float32 [16, 768, 3072], P('dp', None, 'mp')
- first_moment: float32 [16, 768, 3072], P('dp', None, 'mp'), may hold values from -1 to 1
- second_moment: float32 [16, 768, 3072], P('dp', None, 'mp'), may hold values from 0.0005 to 0.002
- norm_params: float32 [2, 4, 768], replicated
- norm_first: float32 [2, 4, 768], replicated, may hold values from -1 to 1
- norm_second: float32 [2, 4, 768], replicated, may hold values from 0.0005 to 0.002
Outputs:
- loss_total: float32 [], replicated
- token_grad: float32 [8192, 768], P(('dp', 'mp'))
- new_master: float32 [16, 768, 3072], P('dp', None, 'mp')
- new_first: float32 [16, 768, 3072], P('dp', None, 'mp')
- new_second: float32 [16, 768, 3072], P('dp', None, 'mp')
- weight_copy: bfloat16 [16, 768, 3072], P('dp', None, 'mp')
- new_norm: float32 [2, 4, 768], replicated
- new_norm_first: float32 [2, 4, 768], replicated
- new_norm_second: float32 [2, 4, 768], replicated
The draws below stay inside these ranges and needn't reach their ends.
Inputs may be any that keep to these rules, and one draw needn't show every extreme that they name: `segment_ids`: in each row: ids never fall and each id 0 to 8 appears; ids below 4 are queries of 1 to 32 tokens, the next 4 ids are documents, one of exactly 768 tokens, and the last id is padding of 1 to 32 tokens. Distinct values; matrix m (layer m // 4, kind m % 4) lives on dp index slot_of[m] // 2 in local slot slot_of[m] % 2; some dp index owns 2 matrices.
All inputs are finite; a program needn't handle non-finite values.
Results may differ from the reference program's by a relative error of at most 0.02.
The reference program's roundings to bfloat16 on the way count: a program that leaves them out, or rounds other values in their place, can miss the bound.
Values may be sent and summed in bfloat16 or wider, within the bound.
No kernel may reach another device: no remote copies, remote signals or barrier semaphores. Data moves between devices by JAX's collectives and lax.ppermute only.
A program may use at most 192 MiB of HBM per device.

```python
import math
import jax
import jax.numpy as jnp
from jax import lax

HEADS = 12
HEAD_DIM = 64
D = 768
FF = 3072
LAYERS = 2
TOK_DEV = 1024
QRY_DEV = 4
DOC_DEV = 4
OWN_MAX = 2
STEP = 7
QLEN_MAX = 32
DOC_MAX = 768
SEGS = 9
MATS = 8
SLOTS = 16
DOCS = 32
TOKENS = 8192
N_DP = 8
N_MP = 4


def owner_slots(key):
    key = jax.random.fold_in(key, 101)
    key_list = jax.random.split(key, 3)
    devices = jax.random.permutation(key_list[0], N_DP).astype(jnp.int32)
    mat_order = jax.random.permutation(key_list[1], MATS).astype(jnp.int32)
    sub_slot = jax.random.randint(key_list[2], (MATS,), 0, OWN_MAX).astype(jnp.int32)
    rank_list = jnp.arange(MATS, dtype=jnp.int32)
    host_device = devices[jnp.maximum(rank_list - 1, 0)]
    slot_pick = jnp.where(rank_list == 0, 0, jnp.where(rank_list == 1, 1, sub_slot))
    slot_list = (host_device * OWN_MAX + slot_pick).astype(jnp.int32)
    return jnp.zeros((MATS,), jnp.int32).at[mat_order].set(slot_list)


def draw_slot_of(key, part):
    slot_list = owner_slots(key)
    return slot_list


def draw_master(key, part):
    slot_list = owner_slots(key)
    key = jax.random.fold_in(key, 3)
    every_slot = jnp.arange(N_DP * OWN_MAX, dtype=jnp.int32)
    attention_kind = jnp.arange(MATS, dtype=jnp.int32) % 4 == 0
    holds_attention = jnp.any((slot_list[None, :] == every_slot[:, None]) & attention_kind[None, :], axis=1)
    column = jnp.arange(FF, dtype=jnp.int32)
    out_part = column % (FF // N_MP) >= 3 * (D // N_MP)
    scale_map = jnp.where(holds_attention[:, None, None] & out_part[None, None, :], 4.0, 1.0) * D ** (-0.5)
    shape_all = (N_DP * OWN_MAX, D, FF)
    values = jax.random.normal(key, shape_all, jnp.float32)
    return (values * scale_map).astype(jnp.float32)


def draw_norm_params(key, part):
    key = jax.random.fold_in(key, 5)
    key_list = jax.random.split(key, 2)
    shape_all = (LAYERS, 4, D)
    gain_rows = jnp.arange(4) % 2 == 0
    gains = jnp.exp(jax.random.uniform(key_list[0], shape_all, jnp.float32, -0.5, 0.45))
    shifts = 0.05 * jax.random.normal(key_list[1], shape_all, jnp.float32)
    return jnp.where(gain_rows[None, :, None], gains, shifts).astype(jnp.float32)


def draw_segment_ids(key, part):
    key = jax.random.fold_in(key, 7)

    def one_row(row_key):
        key_list = jax.random.split(row_key, 4)
        query_len = jax.random.randint(key_list[0], (QRY_DEV,), 1, QLEN_MAX + 1).astype(jnp.int32)
        pad_len = jax.random.randint(key_list[1], (1,), 1, QLEN_MAX + 1).astype(jnp.int32)
        weight = jax.random.randint(key_list[2], (DOC_DEV - 1,), 1, 9).astype(jnp.int32) ** 3
        remaining = TOK_DEV - jnp.sum(query_len) - pad_len[0] - DOC_MAX - (DOC_DEV - 1)
        extra_len = remaining * weight // jnp.sum(weight)
        others = 1 + extra_len
        others = others.at[0].add(remaining - jnp.sum(extra_len))
        long_at = jax.random.randint(key_list[3], (), 0, DOC_DEV).astype(jnp.int32)
        doc_index = jnp.arange(DOC_DEV, dtype=jnp.int32)
        source = jnp.clip(doc_index - (doc_index > long_at).astype(jnp.int32), 0, DOC_DEV - 2)
        doc_lengths = jnp.where(doc_index == long_at, DOC_MAX, others[source])
        lengths = jnp.concatenate([query_len, doc_lengths, pad_len]).astype(jnp.int32)
        seg_ends = jnp.cumsum(lengths)
        place_ids = jnp.arange(TOK_DEV, dtype=jnp.int32)
        return jnp.sum((place_ids[:, None] >= seg_ends[None, :]).astype(jnp.int32), axis=1)
    return jax.vmap(one_row)(jax.random.split(key, N_DP)).astype(jnp.int32)


def place_ends(entries, stream_key, smallest, top_value):
    extent = entries.shape
    place = [jax.random.randint(jax.random.fold_in(stream_key, axis), (), 0, extent[axis]) for axis in range(len(extent))]
    entries = entries.at[tuple(place)].set(smallest)
    longest = extent.index(max(extent))
    place[longest] = (place[longest] + 1) % extent[longest]
    return entries.at[tuple(place)].set(top_value)


def levels(rng, shape, cuts, low, largest):
    gain, own = 1.0, jax.random.fold_in(rng, 6)
    for axis_at, blocks in cuts:
        draws = jnp.exp(jax.random.uniform(jax.random.fold_in(own, axis_at), (blocks,), jnp.float32, low / len(cuts), largest / len(cuts)))
        gain = gain * jnp.repeat(draws, shape[axis_at] // blocks).reshape([-1 if axis == axis_at else 1 for axis in range(len(shape))])
    return gain


def gaussian(rng, extent, width, most, shards=(), held_as=jnp.bfloat16):
    entries = jax.random.normal(rng, extent, jnp.float32) * width
    if len(shards) > 0:
        entries = levels(rng, extent, shards, -0.22, 0.18) * entries
    return jnp.clip(entries, min=-most, max=most).astype(held_as)


def setup_inputs(seed: int = 0) -> dict:
    keys = jax.random.split(jax.random.key(seed), 11)
    return {
        "tokens": gaussian(keys[0], (TOKENS, D), 1.0, 6.0, ((0, 32),)),
        "segment_ids": draw_segment_ids(jax.random.fold_in(keys[10], 71), 0),
        "pair_doc": place_ends(jax.random.randint(keys[2], (N_DP, QRY_DEV), 0, DOCS), jax.random.fold_in(keys[2], 1), 0, DOCS - 1).astype(jnp.int32),
        "slot_of": draw_slot_of(jax.random.fold_in(keys[10], 71), 0),
        "master": draw_master(jax.random.fold_in(keys[10], 71), 0),
        "first_moment": gaussian(keys[5], (SLOTS, D, FF), (0.11 * (16.0 * N_DP * QRY_DEV / TOK_DEV) ** 0.5), 1.0, ((0, 8), (2, 4)), jnp.float32),
        "second_moment": jnp.clip(jnp.exp(math.log(0.002) - 1.3862944 * jax.random.uniform(keys[6], (SLOTS, D, FF), jnp.float32) ** levels(keys[6], (SLOTS, D, FF), ((0, 8), (2, 4)), -0.2, 0.2)), 0.0005, 0.002),
        "norm_params": draw_norm_params(jax.random.fold_in(keys[10], 71), 0),
        "norm_first": gaussian(keys[8], (LAYERS, 4, D), (0.11 * (16.0 * N_DP * QRY_DEV / TOK_DEV) ** 0.5), 1.0, (), jnp.float32),
        "norm_second": jnp.clip(jnp.exp(jax.random.uniform(keys[9], (LAYERS, 4, D), jnp.float32, math.log(0.0005), math.log(0.002))), 0.0005, 0.002),
    }


BETA_ONE = 0.9
BETA_TWO = 0.999
LEARN_RATE = 0.02
NORM_RATE = 0.4
WEIGHT_DECAY = 0.5
ADAM_EPSILON = 1e-08
NORM_EPSILON = 1e-05
SOFTMAX_DIVISOR = 0.01
EXACT_ARITHMETIC = lax.Precision.HIGHEST

@jax.custom_vjp
def narrow_convert(v):
    return lax.optimization_barrier(v.astype(jnp.bfloat16)).astype(jnp.float32)

@jax.custom_vjp
def low_back(v):
    return v

def low_keep(v):
    return (narrow_convert(v), None)

def low_pass(kept, grad):
    return (grad,)

def back_keep(v):
    return (v, None)

def back_low(kept, grad):
    return (narrow_convert(grad),)
narrow_convert.defvjp(low_keep, low_pass)
low_back.defvjp(back_keep, back_low)

def layer_norm(inputs, norm_gain, norm_shift):
    centered = inputs - lax.optimization_barrier(jnp.mean(inputs, axis=-1, keepdims=True))
    variance = lax.optimization_barrier(jnp.mean(centered * centered, axis=-1, keepdims=True))
    return centered * lax.rsqrt(variance + NORM_EPSILON) * norm_gain + norm_shift

def segment_layout(seg_row, seg_count):
    length = seg_row.shape[0]
    place_ids = jnp.arange(length, dtype=jnp.int32)
    member = seg_row[:, None] == jnp.arange(seg_count, dtype=jnp.int32)[None, :]
    starts = lax.optimization_barrier(jnp.min(jnp.where(member, place_ids[:, None], length), axis=0))
    counts = lax.optimization_barrier(jnp.sum(member.astype(jnp.int32), axis=0))
    positions = place_ids - lax.optimization_barrier(jnp.sum(jnp.where(member, starts[None, :], 0), axis=1))
    return (member, positions, counts)

def rope_tables(positions, head_dim):
    half_dim = head_dim // 2
    inverse = 1000.0 ** (-(jnp.arange(half_dim, dtype=jnp.float32) * 2.0 / head_dim))
    angles = positions.astype(jnp.float32)[:, None] * inverse[None, :]
    cosine = jnp.concatenate([jnp.cos(angles), jnp.cos(angles)], axis=1)
    sine_table = jnp.concatenate([jnp.sin(angles), jnp.sin(angles)], axis=1)
    return (cosine, sine_table)

def rotate(values, cosine, sine_table):
    half_dim = values.shape[-1] // 2
    turned = jnp.concatenate([-values[..., half_dim:], values[..., :half_dim]], axis=-1)
    return values * cosine[:, None, :] + turned * sine_table[:, None, :]

def adam_update(weight, first_state, second_state, gradient, step_rate):
    first_new = BETA_ONE * first_state + (1.0 - BETA_ONE) * gradient
    second_new = BETA_TWO * second_state + (1.0 - BETA_TWO) * gradient * gradient
    first_hat = first_new / (1.0 - BETA_ONE ** STEP)
    second_hat = second_new / (1.0 - BETA_TWO ** STEP)
    weight_new = weight - step_rate * (first_hat / (jnp.sqrt(second_hat) + ADAM_EPSILON) + WEIGHT_DECAY * weight)
    return (weight_new, first_new, second_new)

def attention_rows(query_rot, key_rot, value_rows, seg_row):
    length = seg_row.shape[0]
    block_rows = min(512, length)
    block_count = length // block_rows
    scale_value = HEAD_DIM ** (-0.5)

    def one_block(inputs_blk):
        query_blk, seg_blk = inputs_blk
        scores = jnp.einsum('qhd,khd->hqk', query_blk, key_rot, precision=EXACT_ARITHMETIC) * scale_value
        scores = low_back(scores)
        same_doc = seg_blk[:, None] == seg_row[None, :]
        scores = jnp.where(same_doc[None], scores, -1e+30)
        row_top = lax.optimization_barrier(jnp.max(scores, axis=-1, keepdims=True))
        weights = jnp.exp(scores - row_top)
        softmax_rows = weights / lax.optimization_barrier(jnp.sum(weights, axis=-1, keepdims=True))
        return jnp.einsum('hqk,khd->qhd', narrow_convert(softmax_rows), value_rows, precision=EXACT_ARITHMETIC)
    heads_here = query_rot.shape[1]
    blocks = lax.map(jax.checkpoint(one_block), (query_rot.reshape(block_count, block_rows, heads_here, HEAD_DIM), seg_row.reshape(block_count, block_rows)))
    return blocks.reshape(length, heads_here * HEAD_DIM)

def forward_layer(hidden, weights, norms, layer_index, seg_row, cosine, sine_table):
    length = hidden.shape[0]
    part_width = D // N_MP
    attn_block = weights[4 * layer_index].reshape(D, N_MP, 4, part_width)
    w_query = attn_block[:, :, 0, :].reshape(D, D)
    w_key = attn_block[:, :, 1, :].reshape(D, D)
    w_value = attn_block[:, :, 2, :].reshape(D, D)
    w_out_t = attn_block[:, :, 3, :].reshape(D, D)
    w_gate = weights[4 * layer_index + 1]
    w_up = weights[4 * layer_index + 2]
    w_down_t = weights[4 * layer_index + 3]
    norm_set = norms[layer_index]
    tokens_in = narrow_convert(hidden)
    query_pre = low_back(jnp.dot(tokens_in, w_query, precision=EXACT_ARITHMETIC)).reshape(length, HEADS, HEAD_DIM)
    key_pre = low_back(jnp.dot(tokens_in, w_key, precision=EXACT_ARITHMETIC)).reshape(length, HEADS, HEAD_DIM)
    query_rot = low_back(narrow_convert(rotate(query_pre, cosine, sine_table)))
    key_rot = low_back(narrow_convert(rotate(key_pre, cosine, sine_table)))
    value_rows = low_back(narrow_convert(jnp.dot(tokens_in, w_value, precision=EXACT_ARITHMETIC))).reshape(length, HEADS, HEAD_DIM)
    context = low_back(narrow_convert(attention_rows(query_rot, key_rot, value_rows, seg_row)))
    attn_out = low_back(jnp.dot(context, w_out_t.T, precision=EXACT_ARITHMETIC))
    normed = layer_norm(hidden + attn_out, norm_set[0], norm_set[1])
    normed_in = narrow_convert(normed)
    gate_rows = low_back(jnp.dot(normed_in, w_gate, precision=EXACT_ARITHMETIC))
    up_rows = low_back(jnp.dot(normed_in, w_up, precision=EXACT_ARITHMETIC))
    hidden_units = narrow_convert(jax.nn.silu(gate_rows) * up_rows)
    mlp_out = low_back(jnp.dot(hidden_units, w_down_t.T, precision=EXACT_ARITHMETIC))
    return layer_norm(normed + mlp_out, norm_set[2], norm_set[3])

def group_embed(hidden, seg_row, weights, norms):
    member, positions, counts = segment_layout(seg_row, SEGS)
    cosine, sine_table = rope_tables(positions, HEAD_DIM)
    for layer_index in range(LAYERS):
        hidden = forward_layer(hidden, weights, norms, layer_index, seg_row, cosine, sine_table)
    pooled = jnp.dot(member[:, :SEGS - 1].astype(jnp.float32).T, hidden, precision=EXACT_ARITHMETIC)
    pooled = pooled / counts[:SEGS - 1].astype(jnp.float32)[:, None]
    return pooled * lax.rsqrt(lax.optimization_barrier(jnp.sum(pooled * pooled, axis=1, keepdims=True)) + 1e-06)

def reference(tokens, segment_ids, pair_doc, slot_of, master, first_moment, second_moment, norm_params, norm_first, norm_second):
    weights = master[slot_of].astype(jnp.bfloat16).astype(jnp.float32)
    groups = tokens.astype(jnp.float32).reshape(N_DP, TOK_DEV, D)
    targets = pair_doc.reshape(-1)

    def total_loss(group_rows, weight_set, norm_set):

        def one_group(group_pair):
            return group_embed(group_pair[0], group_pair[1], weight_set, norm_set)
        embeds = lax.map(jax.checkpoint(one_group), (group_rows, segment_ids))
        question_group = embeds[:, :QRY_DEV].reshape(-1, D)
        passage_group = embeds[:, QRY_DEV:].reshape(-1, D)
        pairwise_match_scores = jnp.dot(narrow_convert(question_group), narrow_convert(passage_group).T, precision=EXACT_ARITHMETIC) / SOFTMAX_DIVISOR
        row_top = lax.optimization_barrier(jnp.max(pairwise_match_scores, axis=1, keepdims=True))
        log_totals = row_top[:, 0] + jnp.log(lax.optimization_barrier(jnp.sum(jnp.exp(pairwise_match_scores - row_top), axis=1)))
        target_map = targets[:, None] == jnp.arange(passage_group.shape[0], dtype=jnp.int32)[None, :]
        chosen = lax.optimization_barrier(jnp.sum(jnp.where(target_map, pairwise_match_scores, 0.0), axis=1))
        return jnp.sum(log_totals - chosen)
    loss_total, pullback = jax.vjp(total_loss, groups, weights, norm_params)
    grad_groups, grad_weights, grad_norms = pullback(jnp.ones((), jnp.float32))
    slot_count = master.shape[0]
    owned_map = (slot_of[None, :] == jnp.arange(slot_count, dtype=jnp.int32)[:, None]).astype(jnp.float32)
    slot_grads = jnp.einsum('sm,mdf->sdf', owned_map, grad_weights, precision=EXACT_ARITHMETIC)
    in_use = (lax.optimization_barrier(jnp.sum(owned_map, axis=1)) > 0)[:, None, None]
    new_master, new_first, new_second = adam_update(master, first_moment, second_moment, slot_grads, LEARN_RATE)
    new_master = jnp.where(in_use, new_master, master)
    new_first = jnp.where(in_use, new_first, first_moment)
    new_second = jnp.where(in_use, new_second, second_moment)
    new_norm, new_norm_first, new_norm_second = adam_update(norm_params, norm_first, norm_second, grad_norms, NORM_RATE)
    token_grad = grad_groups.reshape(N_DP * TOK_DEV, D)
    return (loss_total, token_grad, new_master, new_first, new_second, new_master.astype(jnp.bfloat16), new_norm, new_norm_first, new_norm_second)
```

```python
import jax
import jax.numpy as jnp
from jax import lax
from jax.sharding import Mesh
from jax.sharding import PartitionSpec as P

HEAD_DIM = 64
LAYERS = 2
QRY_DEV = 4
OWN_MAX = 2
STEP = 7
SEGS = 9
MATS = 8


BETA_ONE = 0.9
BETA_TWO = 0.999
LEARN_RATE = 0.02
NORM_RATE = 0.4
WEIGHT_DECAY = 0.5
ADAM_EPSILON = 1e-08
NORM_EPSILON = 1e-05
SOFTMAX_DIVISOR = 0.01
EXACT_ARITHMETIC = lax.Precision.HIGHEST


def layer_norm(inputs, norm_gain, norm_shift):
    centered = inputs - jnp.mean(inputs, axis=-1, keepdims=True)
    variance = jnp.mean(centered * centered, axis=-1, keepdims=True)
    return centered * lax.rsqrt(variance + NORM_EPSILON) * norm_gain + norm_shift


def segment_layout(seg_row, seg_count):
    length = seg_row.shape[0]
    place_ids = jnp.arange(length, dtype=jnp.int32)
    member = seg_row[:, None] == jnp.arange(seg_count, dtype=jnp.int32)[None, :]
    starts = jnp.min(jnp.where(member, place_ids[:, None], length), axis=0)
    counts = jnp.sum(member.astype(jnp.int32), axis=0)
    positions = place_ids - jnp.sum(jnp.where(member, starts[None, :], 0), axis=1)
    return (member, positions, counts)


def rope_tables(positions, head_dim):
    half_dim = head_dim // 2
    inverse = 1000.0 ** (-(jnp.arange(half_dim, dtype=jnp.float32) * 2.0 / head_dim))
    angles = positions.astype(jnp.float32)[:, None] * inverse[None, :]
    cosine = jnp.concatenate([jnp.cos(angles), jnp.cos(angles)], axis=1)
    sine_table = jnp.concatenate([jnp.sin(angles), jnp.sin(angles)], axis=1)
    return (cosine, sine_table)


def rotate(values, cosine, sine_table):
    half_dim = values.shape[-1] // 2
    turned = jnp.concatenate([-values[..., half_dim:], values[..., :half_dim]], axis=-1)
    return values * cosine[:, None, :] + turned * sine_table[:, None, :]


def rotate_back(gradient, cosine, sine_table):
    half_dim = gradient.shape[-1] // 2
    scaled = gradient * sine_table[:, None, :]
    turned = jnp.concatenate([scaled[..., half_dim:], -scaled[..., :half_dim]], axis=-1)
    return gradient * cosine[:, None, :] + turned


def adam_update(weight, first_state, second_state, gradient, step_rate):
    first_new = BETA_ONE * first_state + (1.0 - BETA_ONE) * gradient
    second_new = BETA_TWO * second_state + (1.0 - BETA_TWO) * gradient * gradient
    first_hat = first_new / (1.0 - BETA_ONE**STEP)
    second_hat = second_new / (1.0 - BETA_TWO**STEP)
    weight_new = weight - step_rate * (
        first_hat / (jnp.sqrt(second_hat) + ADAM_EPSILON) + WEIGHT_DECAY * weight
    )
    return (weight_new, first_new, second_new)


def product_against_flipped(left_side, right_side):
    return lax.dot_general(
        left_side, right_side, (((1,), (1,)), ((), ())), preferred_element_type=jnp.float32
    )


def contract_rows(left_side, right_side):
    return lax.dot_general(
        left_side, right_side, (((0,), (0,)), ((), ())), preferred_element_type=jnp.float32
    )


def contract_exact(left_side, right_side):
    return lax.dot_general(
        left_side, right_side, (((0,), (0,)), ((), ())), precision=EXACT_ARITHMETIC
    )


def attend(query_rot, key_rot, value_rows, seg_row):
    length = seg_row.shape[0]
    block_rows = min(512, length)
    block_count = length // block_rows
    heads_here = query_rot.shape[1]
    scale_value = HEAD_DIM ** (-0.5)

    def one_block(inputs_blk):
        query_blk, seg_blk = inputs_blk
        scores = (
            jnp.einsum("qhd,khd->hqk", query_blk, key_rot, preferred_element_type=jnp.float32)
            * scale_value
        )
        same_doc = seg_blk[:, None] == seg_row[None, :]
        scores = jnp.where(same_doc[None], scores, -1e30)
        row_top = jnp.max(scores, axis=-1, keepdims=True)
        weights = jnp.exp(scores - row_top)
        totals = jnp.sum(weights, axis=-1, keepdims=True)
        softmax_rows = (weights / totals).astype(jnp.bfloat16)
        context = jnp.einsum(
            "hqk,khd->qhd", softmax_rows, value_rows, preferred_element_type=jnp.float32
        )
        return (context, (row_top + jnp.log(totals))[..., 0])

    contexts, log_totals = lax.map(
        one_block,
        (
            query_rot.reshape(block_count, block_rows, heads_here, HEAD_DIM),
            seg_row.reshape(block_count, block_rows),
        ),
    )
    return (contexts.reshape(length, heads_here * HEAD_DIM), log_totals)


def attend_back(query_rot, key_rot, value_rows, seg_row, log_totals, grad_context):
    length = seg_row.shape[0]
    block_rows = min(512, length)
    block_count = length // block_rows
    heads_here = query_rot.shape[1]
    scale_value = HEAD_DIM ** (-0.5)

    def one_block(running, inputs_blk):
        grad_key, grad_value = running
        query_blk, seg_blk, total_blk, grad_blk = inputs_blk
        scores = (
            jnp.einsum("qhd,khd->hqk", query_blk, key_rot, preferred_element_type=jnp.float32)
            * scale_value
        )
        same_doc = seg_blk[:, None] == seg_row[None, :]
        softmax_rows = jnp.where(same_doc[None], jnp.exp(scores - total_blk[..., None]), 0.0)
        grad_probs = jnp.einsum(
            "qhd,khd->hqk", grad_blk, value_rows, preferred_element_type=jnp.float32
        )
        inner_sum = jnp.sum(softmax_rows * grad_probs, axis=-1, keepdims=True)
        grad_scores = (softmax_rows * (grad_probs - inner_sum)).astype(jnp.bfloat16)
        grad_query = (
            jnp.einsum("hqk,khd->qhd", grad_scores, key_rot, preferred_element_type=jnp.float32)
            * scale_value
        )
        grad_key = (
            grad_key
            + jnp.einsum("hqk,qhd->khd", grad_scores, query_blk, preferred_element_type=jnp.float32)
            * scale_value
        )
        grad_value = grad_value + jnp.einsum(
            "hqk,qhd->khd",
            softmax_rows.astype(jnp.bfloat16),
            grad_blk,
            preferred_element_type=jnp.float32,
        )
        return ((grad_key, grad_value), grad_query)

    zeros_init = jnp.zeros((length, heads_here, HEAD_DIM), jnp.float32)
    inputs_all = (
        query_rot.reshape(block_count, block_rows, heads_here, HEAD_DIM),
        seg_row.reshape(block_count, block_rows),
        log_totals,
        grad_context.reshape(block_count, block_rows, heads_here, HEAD_DIM),
    )
    (grad_key, grad_value), grad_query = lax.scan(one_block, (zeros_init, zeros_init), inputs_all)
    return (grad_query.reshape(length, heads_here, HEAD_DIM), grad_key, grad_value)


AXES = ("g", "c", "zp", "a")


def hop(value, move):
    columns = lax.axis_size("g")
    pairs = []
    for column in range(columns):
        for core in range(2):
            for z in range(4):
                to_column, to_core, to_z = move(column, core, z)
                pairs.append(((column * 2 + core) * 4 + z, (to_column * 2 + to_core) * 4 + to_z))
    return lax.ppermute(value, AXES, pairs)


def swap_core(value):
    return hop(value, lambda g, c, z: (g, 1 - c, z))


def swap_near(value):
    return hop(value, lambda g, c, z: (g, c, z ^ 1))


def swap_far(value):
    return hop(value, lambda g, c, z: (g, c, z ^ 2))


def turn(value):
    return hop(value, lambda g, c, z: (g, z // 2, 2 * c + z % 2))


def gather_rows(own):
    near = swap_near(own)
    local = jnp.concatenate([own, swap_core(own)], axis=0)
    remote = jnp.concatenate([near, swap_core(near)], axis=0)
    return (local, remote)


def fold_rows(local, remote):
    rows = local.shape[0] // 2
    near = remote[:rows] + swap_core(remote[rows:].astype(jnp.bfloat16)).astype(jnp.float32)
    near = swap_near(near.astype(jnp.bfloat16)).astype(jnp.float32)
    own = local[:rows] + swap_core(local[rows:].astype(jnp.bfloat16)).astype(jnp.float32)
    return own + near


def both(function, *pairs):
    return tuple(function(*parts) for parts in zip(*pairs))


def contract_both(left, right):
    return contract_rows(left[0], right[0]) + contract_rows(left[1], right[1])


def gather_weights(pieces):
    core = lax.axis_index("c")
    first = hop(pieces, lambda g, c, z: (g, 0, z) if c == 1 else (g, 1, z ^ 2))
    second = hop(pieces, lambda g, c, z: (g, 1, z ^ 2) if c == 1 else (g, 0, z))
    upper = jnp.where(core == 0, pieces, first)
    lower = jnp.where(core == 0, first, second)
    rows = jnp.concatenate([upper, lower], axis=1)
    return lax.all_gather(rows, "g", axis=1, tiled=True)


def scatter_grads(stacked):
    core = lax.axis_index("c")
    rows = lax.psum_scatter(stacked, "g", scatter_dimension=1, tiled=True)
    half = rows.shape[1] // 2
    upper, lower = rows[:, :half], rows[:, half:]
    first = hop(
        jnp.where(core == 0, lower, upper),
        lambda g, c, z: (g, 1, z) if c == 0 else (g, 0, z ^ 2),
    )
    second = hop(lower, lambda g, c, z: (g, 1, z ^ 2) if c == 1 else (g, 0, z))
    mine = jnp.where(core == 0, upper, second).astype(jnp.float32)
    return mine + first.astype(jnp.float32)


def layer_forward(hidden, matrices, norm_set, seg_row, cosine, sine_table):
    attn_block, w_gate, w_up, w_down_t = matrices
    part_width = attn_block.shape[1] // 4
    heads_here = part_width // HEAD_DIM
    tokens_all = gather_rows(hidden.astype(jnp.bfloat16))
    projected = jnp.concatenate(
        both(
            lambda rows: jnp.dot(
                rows, attn_block[:, : 3 * part_width], preferred_element_type=jnp.float32
            ),
            tokens_all,
        ),
        axis=0,
    )
    length = projected.shape[0]
    query_rot = rotate(
        projected[:, :part_width].reshape(length, heads_here, HEAD_DIM), cosine, sine_table
    ).astype(jnp.bfloat16)
    key_rot = rotate(
        projected[:, part_width : 2 * part_width].reshape(length, heads_here, HEAD_DIM),
        cosine,
        sine_table,
    ).astype(jnp.bfloat16)
    value_rows = (
        projected[:, 2 * part_width :].reshape(length, heads_here, HEAD_DIM).astype(jnp.bfloat16)
    )
    context, log_totals = attend(query_rot, key_rot, value_rows, seg_row)
    context = context.astype(jnp.bfloat16)
    context = (context[: length // 2], context[length // 2 :])
    w_out_t = attn_block[:, 3 * part_width :]
    residual_one = hidden + fold_rows(
        *both(lambda rows: product_against_flipped(rows, w_out_t), context)
    )
    normed = layer_norm(residual_one, norm_set[0], norm_set[1])
    normed_all = gather_rows(normed.astype(jnp.bfloat16))
    gate_rows = both(
        lambda rows: jnp.dot(rows, w_gate, preferred_element_type=jnp.float32), normed_all
    )
    up_rows = both(
        lambda rows: jnp.dot(rows, w_up, preferred_element_type=jnp.float32), normed_all
    )
    hidden_units = both(
        lambda gate, up: (jax.nn.silu(gate) * up).astype(jnp.bfloat16), gate_rows, up_rows
    )
    residual_two = normed + fold_rows(
        *both(lambda rows: product_against_flipped(rows, w_down_t), hidden_units)
    )
    output = layer_norm(residual_two, norm_set[2], norm_set[3])
    kept = (
        tokens_all,
        query_rot,
        key_rot,
        value_rows,
        log_totals,
        context,
        residual_one,
        normed_all,
        gate_rows,
        up_rows,
        hidden_units,
        residual_two,
    )
    return (output, kept)


def layer_backward(kept, grad_output, matrices, norm_set, seg_row, cosine, sine_table):
    (
        tokens_all,
        query_rot,
        key_rot,
        value_rows,
        log_totals,
        context,
        residual_one,
        normed_all,
        gate_rows,
        up_rows,
        hidden_units,
        residual_two,
    ) = kept
    attn_block, w_gate, w_up, w_down_t = matrices
    part_width = attn_block.shape[1] // 4
    heads_here = part_width // HEAD_DIM
    length = query_rot.shape[0]
    _, second_pull = jax.vjp(layer_norm, residual_two, norm_set[2], norm_set[3])
    grad_two, grad_gain_two, grad_shift_two = second_pull(grad_output)
    grad_mlp = gather_rows(grad_two.astype(jnp.bfloat16))

    def unit_grads(rows, gate, up):
        grad_units = jnp.dot(rows, w_down_t, preferred_element_type=jnp.float32)
        _, unit_pull = jax.vjp(lambda gate_in, up_in: jax.nn.silu(gate_in) * up_in, gate, up)
        grad_gate, grad_up = unit_pull(grad_units)
        return (grad_gate.astype(jnp.bfloat16), grad_up.astype(jnp.bfloat16))

    unit_halves = both(unit_grads, grad_mlp, gate_rows, up_rows)
    grad_gate = tuple(half[0] for half in unit_halves)
    grad_up = tuple(half[1] for half in unit_halves)
    grad_normed = grad_two + fold_rows(
        *both(
            lambda gate, up: product_against_flipped(gate, w_gate)
            + product_against_flipped(up, w_up),
            grad_gate,
            grad_up,
        )
    )
    grad_down_t = contract_both(grad_mlp, hidden_units)
    grad_gate_w = contract_both(normed_all, grad_gate)
    grad_up_w = contract_both(normed_all, grad_up)
    _, first_pull = jax.vjp(layer_norm, residual_one, norm_set[0], norm_set[1])
    grad_one, grad_gain_one, grad_shift_one = first_pull(grad_normed)
    grad_attn = gather_rows(grad_one.astype(jnp.bfloat16))
    w_out_t = attn_block[:, 3 * part_width :]
    grad_context = jnp.concatenate(
        both(
            lambda rows: jnp.dot(rows, w_out_t, preferred_element_type=jnp.float32).astype(
                jnp.bfloat16
            ),
            grad_attn,
        ),
        axis=0,
    )
    grad_out_t = contract_both(grad_attn, context)
    grad_query, grad_key, grad_value = attend_back(
        query_rot,
        key_rot,
        value_rows,
        seg_row,
        log_totals,
        grad_context.reshape(length, heads_here, HEAD_DIM),
    )
    grad_query_pre = (
        rotate_back(grad_query.astype(jnp.bfloat16), cosine, sine_table)
        .astype(jnp.bfloat16)
        .reshape(length, part_width)
    )
    grad_key_pre = (
        rotate_back(grad_key.astype(jnp.bfloat16), cosine, sine_table)
        .astype(jnp.bfloat16)
        .reshape(length, part_width)
    )
    grad_value_low = grad_value.astype(jnp.bfloat16).reshape(length, part_width)
    grad_projected = jnp.concatenate([grad_query_pre, grad_key_pre, grad_value_low], axis=1)
    grad_projected = (grad_projected[: length // 2], grad_projected[length // 2 :])
    grad_hidden = grad_one + fold_rows(
        *both(
            lambda rows: product_against_flipped(rows, attn_block[:, : 3 * part_width]),
            grad_projected,
        )
    )
    grad_attn_block = jnp.concatenate(
        [contract_both(tokens_all, grad_projected), grad_out_t], axis=1
    )
    block_grads = (grad_attn_block, grad_gate_w, grad_up_w, grad_down_t)
    norm_grads = jnp.stack([grad_gain_one, grad_shift_one, grad_gain_two, grad_shift_two])
    return (grad_hidden, block_grads, norm_grads)


def per_device(
    tokens,
    segment_ids,
    pair_doc,
    slot_of,
    master,
    first_moment,
    second_moment,
    norm_params,
    norm_first,
    norm_second,
):
    columns = lax.axis_size("g")
    owners = 2 * columns
    column = lax.axis_index("g")
    core = lax.axis_index("c")
    z_pair = lax.axis_index("zp")
    near_bit = lax.axis_index("a")
    width = master.shape[1]
    shard_rows = tokens.shape[0]
    straight = core == z_pair
    seg_row = jnp.where(straight, segment_ids, swap_core(segment_ids))[0]
    targets = jnp.where(straight, pair_doc, swap_core(pair_doc))[0]
    member, positions, counts = segment_layout(seg_row, SEGS)
    chunk = near_bit + 2 * core
    chunk_order = [chunk, chunk ^ 2, chunk ^ 1, chunk ^ 3]

    def in_order(values):
        return jnp.concatenate(
            [
                lax.dynamic_slice_in_dim(values, index * shard_rows, shard_rows, 0)
                for index in chunk_order
            ],
            axis=0,
        )

    cosine, sine_table = rope_tables(in_order(positions), HEAD_DIM)
    seg_local = in_order(seg_row)
    my_member = lax.dynamic_slice_in_dim(member, chunk * shard_rows, shard_rows, 0)[
        :, : SEGS - 1
    ].astype(jnp.float32)
    outgoing = master.astype(jnp.bfloat16).reshape(OWN_MAX, owners, width // owners, width)
    incoming = lax.all_to_all(
        outgoing.transpose(1, 0, 2, 3), ("g", "c"), split_axis=0, concat_axis=0, tiled=True
    ).reshape(OWN_MAX * owners, width // owners, width)
    pieces = jnp.stack(
        [
            lax.dynamic_index_in_dim(incoming, slot_of[matrix], 0, keepdims=False)
            for matrix in range(MATS)
        ]
    )
    layer_matrices = []
    for layer_index in range(LAYERS):
        attn = gather_weights(pieces[4 * layer_index : 4 * layer_index + 1])
        rest = gather_weights(pieces[4 * layer_index + 1 : 4 * layer_index + 4])
        layer_matrices.append((attn[0], rest[0], rest[1], rest[2]))
    hidden = turn(tokens).astype(jnp.float32)
    kept_list = []
    for layer_index in range(LAYERS):
        hidden, kept = layer_forward(
            hidden,
            layer_matrices[layer_index],
            norm_params[layer_index],
            seg_local,
            cosine,
            sine_table,
        )
        kept_list.append(kept)
    pooled_sum = contract_exact(my_member, hidden)
    pooled_sum = pooled_sum + swap_core(pooled_sum)
    pooled_sum = pooled_sum + swap_near(pooled_sum)
    lengths = counts[: SEGS - 1].astype(jnp.float32)[:, None]

    def embed_rows(summed_rows):
        pooled = summed_rows / lengths
        return pooled * lax.rsqrt(jnp.sum(pooled * pooled, axis=1, keepdims=True) + 1e-06)

    embeds, embed_pull = jax.vjp(embed_rows, pooled_sum)
    sent = jnp.concatenate(
        [
            embeds.astype(jnp.bfloat16),
            jnp.pad(targets.astype(jnp.bfloat16)[None, :], ((0, 7), (0, width - QRY_DEV))),
        ],
        axis=0,
    )
    every = lax.all_gather(sent, ("g", "zp"), axis=0)
    questions = every[:, :QRY_DEV].reshape(-1, width)
    passages = every[:, QRY_DEV : SEGS - 1].reshape(-1, width)
    all_targets = every[:, SEGS - 1, :QRY_DEV].astype(jnp.int32).reshape(-1)
    scores = product_against_flipped(questions, passages) / SOFTMAX_DIVISOR
    row_top = jnp.max(scores, axis=1, keepdims=True)
    log_totals = row_top[:, 0] + jnp.log(jnp.sum(jnp.exp(scores - row_top), axis=1))
    target_map = (
        all_targets[:, None] == jnp.arange(passages.shape[0], dtype=jnp.int32)[None, :]
    )
    chosen = jnp.sum(jnp.where(target_map, scores, 0.0), axis=1)
    loss_total = jnp.sum(log_totals - chosen)
    grad_logits = (
        jnp.exp(scores - log_totals[:, None]) - target_map.astype(jnp.float32)
    ) / SOFTMAX_DIVISOR
    group = 2 * column + z_pair
    my_rows = lax.dynamic_slice_in_dim(grad_logits, group * QRY_DEV, QRY_DEV, 0)
    doc_count = SEGS - 1 - QRY_DEV
    my_columns = lax.dynamic_slice_in_dim(grad_logits, group * doc_count, doc_count, 1)
    grad_query_emb = jnp.dot(my_rows, passages.astype(jnp.float32), precision=EXACT_ARITHMETIC)
    grad_doc_emb = contract_exact(my_columns, questions.astype(jnp.float32))
    (grad_pooled,) = embed_pull(jnp.concatenate([grad_query_emb, grad_doc_emb], axis=0))
    gradient = jnp.dot(my_member, grad_pooled, precision=EXACT_ARITHMETIC)
    norm_list = [None] * LAYERS
    piece_list = [None] * MATS
    for layer_index in reversed(range(LAYERS)):
        gradient, block_grads, norm_grads = layer_backward(
            kept_list[layer_index],
            gradient,
            layer_matrices[layer_index],
            norm_params[layer_index],
            seg_local,
            cosine,
            sine_table,
        )
        norm_list[layer_index] = norm_grads
        rest = scatter_grads(jnp.stack([grad.astype(jnp.bfloat16) for grad in block_grads[1:]]))
        attn = scatter_grads(block_grads[0].astype(jnp.bfloat16)[None])
        piece_list[4 * layer_index] = attn[0]
        for matrix in range(3):
            piece_list[4 * layer_index + 1 + matrix] = rest[matrix]
    token_grad = turn(gradient.astype(jnp.bfloat16)).astype(jnp.float32)
    outgoing = jnp.zeros((OWN_MAX * owners, width // owners, width), jnp.bfloat16)
    for matrix in range(MATS):
        outgoing = lax.dynamic_update_index_in_dim(
            outgoing, piece_list[matrix].astype(jnp.bfloat16), slot_of[matrix], 0
        )
    incoming = lax.all_to_all(
        outgoing.reshape(owners, OWN_MAX, width // owners, width),
        ("g", "c"),
        split_axis=0,
        concat_axis=0,
        tiled=True,
    )
    my_grads = (
        incoming.transpose(1, 0, 2, 3).reshape(OWN_MAX, width, width).astype(jnp.float32)
    )
    norm_total = jnp.stack(norm_list).reshape(-1, width)
    norm_total = norm_total + swap_core(norm_total)
    norm_total = norm_total + swap_near(norm_total)
    norm_total = norm_total + swap_far(norm_total)
    norm_total = jnp.sum(lax.all_gather(norm_total, "g", axis=0), axis=0)
    norm_total = norm_total.reshape(norm_params.shape)
    slot_ids = (2 * column + core) * OWN_MAX + jnp.arange(OWN_MAX, dtype=jnp.int32)
    in_use = jnp.any(slot_of[None, :] == slot_ids[:, None], axis=1)[:, None, None]
    new_master, new_first, new_second = adam_update(
        master, first_moment, second_moment, my_grads, LEARN_RATE
    )
    new_master = jnp.where(in_use, new_master, master)
    new_first = jnp.where(in_use, new_first, first_moment)
    new_second = jnp.where(in_use, new_second, second_moment)
    new_norm, new_norm_first, new_norm_second = adam_update(
        norm_params, norm_first, norm_second, norm_total, NORM_RATE
    )
    return (
        loss_total,
        token_grad,
        new_master,
        new_first,
        new_second,
        new_master.astype(jnp.bfloat16),
        new_norm,
        new_norm_first,
        new_norm_second,
    )


def solution(mesh):
    owners, model_parts = mesh.devices.shape
    work_mesh = Mesh(mesh.devices.reshape(owners // 2, 2, model_parts // 2, 2), AXES)
    dp, mp = ("g", "c"), ("zp", "a")
    in_specs = (
        P(AXES, None),
        P(dp, None),
        P(dp, None),
        P(),
        P(dp, None, mp),
        P(dp, None, mp),
        P(dp, None, mp),
        P(),
        P(),
        P(),
    )
    out_specs = (
        P(),
        P(AXES, None),
        P(dp, None, mp),
        P(dp, None, mp),
        P(dp, None, mp),
        P(dp, None, mp),
        P(),
        P(),
        P(),
    )
    return jax.shard_map(
        per_device, mesh=work_mesh, in_specs=in_specs, out_specs=out_specs, check_vma=False
    )
```

```python
import functools

import jax
import jax.numpy as jnp
from jax import lax
from jax.experimental import pallas as pl
from jax.experimental.pallas import tpu as pltpu
from jax.sharding import Mesh
from jax.sharding import PartitionSpec as P

HEAD_DIM = 64
LAYERS = 2
QRY_DEV = 4
OWN_MAX = 2
STEP = 7
SEGS = 9
MATS = 8


BETA_ONE = 0.9
BETA_TWO = 0.999
LEARN_RATE = 0.02
NORM_RATE = 0.4
WEIGHT_DECAY = 0.5
ADAM_EPSILON = 1e-08
NORM_EPSILON = 1e-05
SOFTMAX_DIVISOR = 0.01
EXACT_ARITHMETIC = lax.Precision.HIGHEST


def segment_layout(seg_row, seg_count):
    length = seg_row.shape[0]
    place_ids = jnp.arange(length, dtype=jnp.int32)
    member = seg_row[:, None] == jnp.arange(seg_count, dtype=jnp.int32)[None, :]
    starts = jnp.min(jnp.where(member, place_ids[:, None], length), axis=0)
    counts = jnp.sum(member.astype(jnp.int32), axis=0)
    positions = place_ids - jnp.sum(jnp.where(member, starts[None, :], 0), axis=1)
    return (member, positions, counts)


def rope_tables(positions, head_dim):
    half_dim = head_dim // 2
    inverse = 1000.0 ** (-(jnp.arange(half_dim, dtype=jnp.float32) * 2.0 / head_dim))
    angles = positions.astype(jnp.float32)[:, None] * inverse[None, :]
    cosine = jnp.concatenate([jnp.cos(angles), jnp.cos(angles)], axis=1)
    sine_table = jnp.concatenate([jnp.sin(angles), jnp.sin(angles)], axis=1)
    return (cosine, sine_table)


def adam_update(weight, first_state, second_state, gradient, step_rate):
    first_new = BETA_ONE * first_state + (1.0 - BETA_ONE) * gradient
    second_new = BETA_TWO * second_state + (1.0 - BETA_TWO) * gradient * gradient
    first_hat = first_new / (1.0 - BETA_ONE**STEP)
    second_hat = second_new / (1.0 - BETA_TWO**STEP)
    weight_new = weight - step_rate * (
        first_hat / (jnp.sqrt(second_hat) + ADAM_EPSILON) + WEIGHT_DECAY * weight
    )
    return (weight_new, first_new, second_new)


def contract_exact(left_side, right_side):
    return lax.dot_general(
        left_side, right_side, (((0,), (0,)), ((), ())), precision=EXACT_ARITHMETIC
    )


def spread_map(heads):
    width = heads * HEAD_DIM
    half = HEAD_DIM // 2
    row = jnp.arange(3 * width, dtype=jnp.int32)[:, None]
    column = jnp.arange(6 * width, dtype=jnp.int32)[None, :]
    kind = column // (2 * width)
    head = column % (2 * width) // (2 * HEAD_DIM)
    lane = column % (2 * HEAD_DIM)
    base = kind * width + head * HEAD_DIM
    within = lane % HEAD_DIM
    plain = (row == base + within) & (lane < HEAD_DIM)
    turned = (lane >= HEAD_DIM) & (kind < 2)
    minus = turned & (within < half) & (row == base + within + half)
    plus = turned & (within >= half) & (row == base + within - half)
    return (plain.astype(jnp.float32) + plus - minus.astype(jnp.float32)).astype(jnp.bfloat16)


def unspread_map(heads):
    width = heads * HEAD_DIM
    half = HEAD_DIM // 2
    row = jnp.arange(4 * width, dtype=jnp.int32)[:, None]
    column = jnp.arange(2 * width, dtype=jnp.int32)[None, :]
    base = (column // HEAD_DIM) * 2 * HEAD_DIM
    within = column % HEAD_DIM
    plain = (row == base + within).astype(jnp.float32)
    plus = ((within < half) & (row == base + within + half)).astype(jnp.float32)
    minus = ((within >= half) & (row == base + within - half)).astype(jnp.float32)
    return jnp.stack([plain, plus - minus]).astype(jnp.bfloat16)


def flipped(left_side, right_side):
    return lax.dot_general(
        left_side, right_side, (((1,), (1,)), ((), ())), preferred_element_type=jnp.float32
    )


def straight(left_side, right_side):
    return jnp.dot(left_side, right_side, preferred_element_type=jnp.float32)


def over_rows(left_side, right_side):
    return lax.dot_general(
        left_side, right_side, (((0,), (0,)), ((), ())), preferred_element_type=jnp.float32
    )


def call(body, outputs, operands, scratch=(), mebibytes=16, name=None):
    out_shape = tuple(jax.ShapeDtypeStruct(shape, dtype) for shape, dtype in outputs)
    return pl.pallas_call(
        body,
        out_shape=out_shape,
        scratch_shapes=list(scratch),
        compiler_params=pltpu.CompilerParams(vmem_limit_bytes=mebibytes * 2**20),
        cost_estimate=pl.CostEstimate(flops=10**6, bytes_accessed=10**5, transcendentals=0),
        name=name,
    )(*operands)


def attend_block(
    heads, chunk, rows, query_ref, key_ref, value_ref, seg_col_ref, seg_row_ref
):
    pad = 2 * HEAD_DIM
    span = slice(chunk * rows, (chunk + 1) * rows)
    bias = jnp.where(seg_col_ref[span, :] == seg_row_ref[...], 0.0, -1e30)
    lanes = lax.broadcasted_iota(jnp.int32, (rows, pad), 1)
    totals_all = jnp.zeros((rows, pad), jnp.float32)
    pieces = []
    for head in range(heads):
        cols = slice(head * pad, (head + 1) * pad)
        scores = flipped(query_ref[span, cols], key_ref[:, cols]) + bias
        row_top = jnp.max(scores, axis=-1, keepdims=True)
        weights = jnp.exp(scores - row_top)
        totals = jnp.sum(weights, axis=-1, keepdims=True)
        probs = (weights * (1.0 / totals)).astype(jnp.bfloat16)
        context = straight(probs, value_ref[:, cols])
        pieces.append(context[:, :HEAD_DIM].astype(jnp.bfloat16))
        totals_all = jnp.where(lanes == head, row_top + jnp.log(totals), totals_all)
    return (jnp.concatenate(pieces, axis=1), totals_all)


def attend_first_kernel(heads, *refs):
    chunk_refs, refs = refs[:4], refs[4:]
    weight_ref, map_ref, table_ref, seg_col_ref, seg_row_ref = refs[:5]
    query_ref, key_ref, value_ref, context_ref, total_ref, keep_ref, send_ref = refs[5:]
    width = heads * HEAD_DIM
    pad = 2 * HEAD_DIM
    rows = chunk_refs[0].shape[0]
    weights = straight(weight_ref[:, : 3 * width], map_ref[...]).astype(jnp.bfloat16)
    for chunk in range(4):
        span = slice(chunk * rows, (chunk + 1) * rows)
        projected = straight(chunk_refs[chunk][...], weights)
        table = table_ref[span, :]
        for head in range(heads):
            for base, ref, scale in ((0, query_ref, 0.0625), (heads * pad, key_ref, 1.0)):
                lanes = slice(base + head * pad, base + (head + 1) * pad)
                turned = projected[:, lanes] * table
                turned = turned + pltpu.roll(turned, HEAD_DIM, 1)
                ref[span, head * pad : (head + 1) * pad] = (turned * scale).astype(jnp.bfloat16)
        value_ref[span, :] = projected[:, 2 * heads * pad :].astype(jnp.bfloat16)
    out_weights = weight_ref[:, 3 * width :]
    for place, out_ref in enumerate((keep_ref, send_ref)):
        span = slice(place * rows, (place + 1) * rows)
        context, totals = attend_block(
            heads, 2 + place, rows, query_ref, key_ref, value_ref, seg_col_ref, seg_row_ref
        )
        context_ref[span, :] = context
        total_ref[span, :] = totals
        out_ref[...] = flipped(context, out_weights).astype(out_ref.dtype)


def attend_second_kernel(heads, *refs):
    weight_ref, seg_col_ref, seg_row_ref, query_ref, key_ref, value_ref = refs[:6]
    context_ref, total_ref, keep_ref, send_ref = refs[6:]
    rows = keep_ref.shape[0]
    out_weights = weight_ref[:, 3 * heads * HEAD_DIM :]
    for place, out_ref in enumerate((keep_ref, send_ref)):
        span = slice(place * rows, (place + 1) * rows)
        context, totals = attend_block(
            heads, place, rows, query_ref, key_ref, value_ref, seg_col_ref, seg_row_ref
        )
        context_ref[span, :] = context
        total_ref[span, :] = totals
        out_ref[...] = flipped(context, out_weights).astype(out_ref.dtype)


def attend_first(chunks, attn_block, mapping, table, seg_col, seg_row):
    width = attn_block.shape[0]
    part = attn_block.shape[1] // 4
    rows = chunks[0].shape[0]
    length = 4 * rows
    return call(
        functools.partial(attend_first_kernel, part // HEAD_DIM),
        [((length, 2 * part), jnp.bfloat16)] * 3
        + [
            ((2 * rows, part), jnp.bfloat16),
            ((2 * rows, 2 * HEAD_DIM), jnp.float32),
            ((rows, width), jnp.float32),
            ((rows, width), jnp.bfloat16),
        ],
        (*chunks, attn_block, mapping, table, seg_col, seg_row),
        mebibytes=28,
        name="attend_first",
    )


def attend_second(attn_block, seg_col, seg_row, query, key, value):
    width = attn_block.shape[0]
    part = attn_block.shape[1] // 4
    rows = query.shape[0] // 4
    return call(
        functools.partial(attend_second_kernel, part // HEAD_DIM),
        [
            ((2 * rows, part), jnp.bfloat16),
            ((2 * rows, 2 * HEAD_DIM), jnp.float32),
            ((rows, width), jnp.float32),
            ((rows, width), jnp.bfloat16),
        ],
        (attn_block, seg_col, seg_row, query, key, value),
        mebibytes=28,
        name="attend_second",
    )


def attend_back_kernel(heads, *refs):
    chunk_refs, refs = refs[:4], refs[4:]
    weight_ref, map_ref, cos_ref, sin_ref, seg_col_ref, seg_row_ref = refs[:6]
    query_ref, key_ref, value_ref, local_total_ref, remote_total_ref = refs[6:11]
    projected_ref, own_ref, sibling_ref, near_ref, across_ref = refs[11:16]
    grad_query, grad_key, grad_value = refs[16:]
    width = heads * HEAD_DIM
    pad = 2 * HEAD_DIM
    rows = chunk_refs[0].shape[0]
    out_weights = weight_ref[:, 3 * width :]
    empty = jnp.zeros((out_weights.shape[0], HEAD_DIM), jnp.bfloat16)
    wide = []
    for head in range(heads):
        wide += [out_weights[:, head * HEAD_DIM : (head + 1) * HEAD_DIM], empty]
    wide = jnp.concatenate(wide, axis=1)
    for chunk in range(4):
        span = slice(chunk * rows, (chunk + 1) * rows)
        grads_all = straight(chunk_refs[chunk][...], wide).astype(jnp.bfloat16)
        total_ref = local_total_ref if chunk < 2 else remote_total_ref
        total_span = slice(chunk % 2 * rows, (chunk % 2 + 1) * rows)
        bias = jnp.where(seg_col_ref[span, :] == seg_row_ref[...], 0.0, -1e30)
        for head in range(heads):
            cols = slice(head * pad, (head + 1) * pad)
            query = query_ref[span, cols]
            key = key_ref[:, cols]
            grads = grads_all[:, cols]
            scores = flipped(query, key) + bias
            probs = jnp.exp(scores - total_ref[total_span, head : head + 1])
            grad_probs = flipped(grads, value_ref[:, cols])
            inner = jnp.sum(probs * grad_probs, axis=-1, keepdims=True)
            grad_scores = (probs * (grad_probs - inner)).astype(jnp.bfloat16)
            grad_query[span, cols] = (straight(grad_scores, key) * 0.125).astype(jnp.bfloat16)
            key_part = straight(query.T, grad_scores)
            value_part = straight(grads.T, probs.astype(jnp.bfloat16))
            if chunk == 0:
                grad_key[cols, :] = key_part
                grad_value[cols, :] = value_part
            else:
                grad_key[cols, :] += key_part
                grad_value[cols, :] += value_part
    for chunk, out_ref in enumerate((own_ref, sibling_ref, near_ref, across_ref)):
        span = slice(chunk * rows, (chunk + 1) * rows)
        grad_k = (grad_key[:, span] * 2.0).astype(jnp.bfloat16).T
        grad_v = grad_value[:, span].astype(jnp.bfloat16).T
        both = jnp.concatenate([grad_query[span, :], grad_k], axis=1)
        plain = straight(both, map_ref[0])
        turned = straight(both, map_ref[1])
        cosine = jnp.concatenate([cos_ref[span, :]] * heads, axis=1)
        sine = jnp.concatenate([sin_ref[span, :]] * heads, axis=1)
        turned = (plain * cosine + turned * sine).astype(jnp.bfloat16)
        grad_v = [grad_v[:, head * pad : head * pad + HEAD_DIM] for head in range(heads)]
        projected = jnp.concatenate([turned, *grad_v], axis=1)
        projected_ref[span, :] = projected
        out_ref[...] = flipped(projected, weight_ref[:, : 3 * width]).astype(out_ref.dtype)


def attend_back(chunks, attn_block, mapping, cosine, sine, seg_col, seg_row, kept):
    width = attn_block.shape[0]
    part = attn_block.shape[1] // 4
    rows = chunks[0].shape[0]
    length = 4 * rows
    return call(
        functools.partial(attend_back_kernel, part // HEAD_DIM),
        [((length, 3 * part), jnp.bfloat16)]
        + [((rows, width), jnp.float32), ((rows, width), jnp.bfloat16)] * 2,
        (*chunks, attn_block, mapping, cosine, sine, seg_col, seg_row, *kept),
        mebibytes=28,
        scratch=[
            pltpu.VMEM((length, 2 * part), jnp.bfloat16),
            pltpu.VMEM((2 * part, length), jnp.float32),
            pltpu.VMEM((2 * part, length), jnp.float32),
        ],
        name="attend_back",
    )


def units_kernel(*refs):
    chunk_refs, (weight_ref, keep_ref, send_ref) = refs[:2], refs[2:]
    units = weight_ref.shape[1] // 3
    for chunk_ref, out_ref in zip(chunk_refs, (keep_ref, send_ref)):
        tokens = chunk_ref[...]
        gate = straight(tokens, weight_ref[:, :units])
        up = straight(tokens, weight_ref[:, units : 2 * units])
        hidden = (gate / (1.0 + jnp.exp(-gate)) * up).astype(jnp.bfloat16)
        out_ref[...] = flipped(hidden, weight_ref[:, 2 * units :]).astype(out_ref.dtype)


def hidden_units(chunks, weights):
    rows, width = chunks[0].shape
    return call(
        units_kernel,
        [((rows, width), jnp.float32), ((rows, width), jnp.bfloat16)],
        (*chunks, weights),
        name="hidden_units",
    )


def units_back_kernel(*refs):
    token_refs, chunk_refs, weight_ref = refs[:2], refs[2:4], refs[4]
    grad_ref, hidden_ref, keep_ref, send_ref = refs[5:]
    rows, width = chunk_refs[0].shape
    units = weight_ref.shape[1] // 3
    for place, out_ref in enumerate((keep_ref, send_ref)):
        span = slice(place * rows, (place + 1) * rows)
        tokens = token_refs[place][...]
        gate = straight(tokens, weight_ref[:, :units])
        up = straight(tokens, weight_ref[:, units : 2 * units])
        grad_hidden = straight(chunk_refs[place][...], weight_ref[:, 2 * units :])
        share = 1.0 / (1.0 + jnp.exp(-gate))
        silu = gate * share
        hidden_ref[span, :] = (silu * up).astype(jnp.bfloat16)
        grad_up = (grad_hidden * silu).astype(jnp.bfloat16)
        slope = share + silu * (1.0 - share)
        grad_gate = (grad_hidden * up * slope).astype(jnp.bfloat16)
        grad_ref[span, :units] = grad_gate
        grad_ref[span, units:] = grad_up
        result = flipped(grad_gate, weight_ref[:, :units])
        result = result + flipped(grad_up, weight_ref[:, units : 2 * units])
        out_ref[...] = result.astype(out_ref.dtype)


def units_back(tokens, chunks, weights):
    rows, width = chunks[0].shape
    units = weights.shape[1] // 3
    return call(
        units_back_kernel,
        [
            ((2 * rows, 2 * units), jnp.bfloat16),
            ((2 * rows, units), jnp.bfloat16),
            ((rows, width), jnp.float32),
            ((rows, width), jnp.bfloat16),
        ],
        (*tokens, *chunks, weights),
        mebibytes=24,
        name="units_back",
    )


def units_weights_kernel(*refs):
    token_refs, grad_refs, refs = refs[:4], refs[4:8], refs[8:]
    local_pair_ref, remote_pair_ref, local_hidden_ref, remote_hidden_ref, out_ref = refs
    rows, width = token_refs[0].shape
    units = local_hidden_ref.shape[1]
    for tile in range(0, width, 256):
        cols = slice(tile, tile + 256)
        pair, down = 0.0, 0.0
        for chunk in range(4):
            span = slice(chunk % 2 * rows, (chunk % 2 + 1) * rows)
            pair_ref = local_pair_ref if chunk < 2 else remote_pair_ref
            hidden_ref = local_hidden_ref if chunk < 2 else remote_hidden_ref
            pair = pair + over_rows(token_refs[chunk][:, cols], pair_ref[span, :])
            down = down + over_rows(grad_refs[chunk][:, cols], hidden_ref[span, :])
        out_ref[cols, : 2 * units] = pair.astype(jnp.bfloat16)
        out_ref[cols, 2 * units :] = down.astype(jnp.bfloat16)


def units_weights(tokens, grads, pairs, hidden):
    rows, width = tokens[0].shape
    units = hidden[0].shape[1]
    return call(
        units_weights_kernel,
        [((width, 3 * units), jnp.bfloat16)],
        (*tokens, *grads, *pairs, *hidden),
        name="units_weights",
    )[0]


def attend_weights_kernel(*refs):
    token_refs, grad_refs, refs = refs[:4], refs[4:8], refs[8:]
    projected_ref, local_context_ref, remote_context_ref, out_ref = refs
    rows, width = token_refs[0].shape
    for tile in range(0, width, 256):
        cols = slice(tile, tile + 256)
        left, right = 0.0, 0.0
        for chunk in range(4):
            span = slice(chunk % 2 * rows, (chunk % 2 + 1) * rows)
            context_ref = local_context_ref if chunk < 2 else remote_context_ref
            projected = projected_ref[chunk * rows : (chunk + 1) * rows, :]
            left = left + over_rows(token_refs[chunk][:, cols], projected)
            right = right + over_rows(grad_refs[chunk][:, cols], context_ref[span, :])
        both = jnp.concatenate([left, right], axis=1)
        out_ref[cols, :] = both.astype(jnp.bfloat16)


def attend_weights(tokens, grads, projected, context):
    rows, width = tokens[0].shape
    part = context[0].shape[1]
    return call(
        attend_weights_kernel,
        [((width, 4 * part), jnp.bfloat16)],
        (*tokens, *grads, projected, *context),
        name="attend_weights",
    )[0]


def norm_kernel(*refs):
    base_ref, keep_ref, sibling_ref, near_ref, norm_ref = refs[:5]
    residual_ref, normed_ref, low_ref = refs[5:]
    residual = base_ref[...] + keep_ref[...] + sibling_ref[...].astype(jnp.float32)
    residual = residual + near_ref[...].astype(jnp.float32)
    residual_ref[...] = residual
    centered = residual - jnp.mean(residual, axis=-1, keepdims=True)
    variance = jnp.mean(centered * centered, axis=-1, keepdims=True)
    normed = centered * lax.rsqrt(variance + NORM_EPSILON) * norm_ref[0:1, :] + norm_ref[1:2, :]
    normed_ref[...] = normed
    low_ref[...] = normed.astype(jnp.bfloat16)


def add_and_norm(base, keep, sibling, near, norm_pair):
    shape = base.shape
    return call(
        norm_kernel,
        [(shape, jnp.float32), (shape, jnp.float32), (shape, jnp.bfloat16)],
        (base, keep, sibling, near, norm_pair),
        name="add_and_norm",
    )


def norm_back_rows(grad, residual, gain):
    centered = residual - jnp.mean(residual, axis=-1, keepdims=True)
    variance = jnp.mean(centered * centered, axis=-1, keepdims=True)
    inverse = lax.rsqrt(variance + NORM_EPSILON)
    scaled = centered * inverse
    wide = grad * gain
    inner = jnp.mean(wide * scaled, axis=-1, keepdims=True)
    result = inverse * (wide - jnp.mean(wide, axis=-1, keepdims=True) - scaled * inner)
    gain_grad = jnp.sum(grad * scaled, axis=0, keepdims=True)
    return (result, jnp.concatenate([gain_grad, jnp.sum(grad, axis=0, keepdims=True)], axis=0))


def norm_back_kernel(*refs):
    part_refs, (residual_ref, norm_ref, out_ref, low_ref, params_ref) = refs[:-5], refs[-5:]
    grad = part_refs[0][...]
    for part_ref in part_refs[1:]:
        grad = grad + part_ref[...].astype(jnp.float32)
    result, params = norm_back_rows(grad, residual_ref[...], norm_ref[0:1, :])
    out_ref[...] = result
    low_ref[...] = result.astype(jnp.bfloat16)
    params_ref[...] = params


def norm_back(parts, residual, norm_pair):
    shape = residual.shape
    return call(
        norm_back_kernel,
        [(shape, jnp.float32), (shape, jnp.bfloat16), ((2, shape[1]), jnp.float32)],
        (*parts, residual, norm_pair),
        name="norm_back",
    )


def embed_kernel(sum_ref, near_ref, length_ref, target_ref, total_ref, out_ref):
    total = sum_ref[...] + near_ref[...]
    total_ref[...] = total
    pooled = total / length_ref[...]
    embeds = pooled * lax.rsqrt(jnp.sum(pooled * pooled, axis=1, keepdims=True) + 1e-06)
    out_ref[...] = jnp.concatenate([embeds, target_ref[...]], axis=1).astype(jnp.bfloat16)


def embed(pool_part, near_part, lengths, targets):
    rows, width = pool_part.shape
    return call(
        embed_kernel,
        [
            ((rows, width), jnp.float32),
            ((rows, width + targets.shape[1]), jnp.bfloat16),
        ],
        (pool_part, near_part, lengths, targets),
        name="embed",
    )


def loss_kernel(*refs):
    every_ref, sum_ref, length_ref, member_ref, group_ref, residual_ref, norm_ref = refs[:7]
    loss_ref, out_ref, low_ref, params_ref = refs[7:]
    width = sum_ref.shape[1]
    rows = SEGS - 1
    docs = rows - QRY_DEV
    total = every_ref.shape[0]
    vectors = every_ref[:, :width]
    targets = every_ref[:, width : width + 1].astype(jnp.float32)
    scores = flipped(vectors, vectors) / SOFTMAX_DIVISOR
    row = lax.broadcasted_iota(jnp.int32, (total, total), 0)
    column = lax.broadcasted_iota(jnp.int32, (total, total), 1)
    place = column % rows
    is_doc = place >= QRY_DEV
    doc = column // rows * docs + place - QRY_DEV
    is_query = row % rows < QRY_DEV
    hit = is_doc & (doc.astype(jnp.float32) == targets)
    masked = jnp.where(is_doc, scores, -1e30)
    row_top = jnp.max(masked, axis=1, keepdims=True)
    log_totals = row_top + jnp.log(jnp.sum(jnp.exp(masked - row_top), axis=1, keepdims=True))
    chosen = jnp.sum(jnp.where(hit, scores, 0.0), axis=1, keepdims=True)
    losses = jnp.where(is_query[:, :1], log_totals - chosen, 0.0)
    loss_ref[...] = jnp.sum(losses, axis=0, keepdims=True)
    logits = (jnp.exp(masked - log_totals) - hit.astype(jnp.float32)) / SOFTMAX_DIVISOR
    logits = jnp.where(is_query & is_doc, logits, 0.0)
    wide = vectors.astype(jnp.float32)
    embed_grads = exact(logits, wide) + exact(logits.T, wide)
    mine = lax.broadcasted_iota(jnp.int32, (rows, total), 1) - group_ref[...] * rows
    mine = (mine == lax.broadcasted_iota(jnp.int32, (rows, total), 0)).astype(jnp.float32)
    embed_grads = exact(mine, embed_grads)
    pooled = sum_ref[...] / length_ref[...]
    inverse = lax.rsqrt(jnp.sum(pooled * pooled, axis=1, keepdims=True) + 1e-06)
    inner = jnp.sum(embed_grads * pooled, axis=1, keepdims=True)
    pooled_grads = embed_grads * inverse - pooled * (inverse * inverse * inverse * inner)
    grad = exact(member_ref[...], pooled_grads / length_ref[...])
    result, params = norm_back_rows(grad, residual_ref[...], norm_ref[0:1, :])
    out_ref[...] = result
    low_ref[...] = result.astype(jnp.bfloat16)
    params_ref[...] = params


def exact(left_side, right_side):
    return lax.dot_general(
        left_side,
        right_side,
        (((1,), (0,)), ((), ())),
        precision=EXACT_ARITHMETIC,
        preferred_element_type=jnp.float32,
    )


def loss_and_back(every, pooled_sum, lengths, member, group, residual, norm_pair):
    shape = residual.shape
    return call(
        loss_kernel,
        [
            ((1, 1), jnp.float32),
            (shape, jnp.float32),
            (shape, jnp.bfloat16),
            ((2, shape[1]), jnp.float32),
        ],
        (every, pooled_sum, lengths, member, group, residual, norm_pair),
        name="loss_and_back",
    )


AXES = ("g", "c", "zp", "a")


def hop(value, move):
    columns = lax.axis_size("g")
    pairs = []
    for column in range(columns):
        for core in range(2):
            for z in range(4):
                to_column, to_core, to_z = move(column, core, z)
                pairs.append(((column * 2 + core) * 4 + z, (to_column * 2 + to_core) * 4 + to_z))
    return lax.ppermute(value, AXES, pairs)


def swap_core(value):
    return hop(value, lambda g, c, z: (g, 1 - c, z))


def swap_near(value):
    return hop(value, lambda g, c, z: (g, c, z ^ 1))


def swap_far(value):
    return hop(value, lambda g, c, z: (g, c, z ^ 2))


def turn(value):
    return hop(value, lambda g, c, z: (g, z // 2, 2 * c + z % 2))


def gather_rows(own):
    near = swap_near(own)
    return (own, swap_core(own), near, swap_core(near))


def fold_remote(keep, send):
    return (keep + swap_core(send).astype(jnp.float32)).astype(jnp.bfloat16)


def after(value, *others):
    return lax.optimization_barrier((value, *others))[0]


def swap_x(value):
    return hop(value, lambda g, c, z: (g ^ 1, c, z))


def swap_y(value):
    return hop(value, lambda g, c, z: (g ^ 2, c, z))


def ordered(bit, mine, other, axis):
    low = jnp.where(bit == 0, mine, other)
    return jnp.stack([low, jnp.where(bit == 0, other, mine)], axis=axis)


def to_working_block(piece):
    core = lax.axis_index("c")
    first = hop(piece, lambda g, c, z: (g, 0, z) if c == 1 else (g, 1, z ^ 2))
    second = hop(piece, lambda g, c, z: (g, 1, z ^ 2) if c == 1 else (g, 0, z))
    return (jnp.where(core == 0, piece, first), jnp.where(core == 0, first, second))


def from_working_block(upper, lower):
    core = lax.axis_index("c")
    first = hop(
        jnp.where(core == 0, lower, upper),
        lambda g, c, z: (g, 1, z) if c == 0 else (g, 0, z ^ 2),
    )
    second = hop(lower, lambda g, c, z: (g, 1, z ^ 2) if c == 1 else (g, 0, z))
    mine = jnp.where(core == 0, upper, second).astype(jnp.float32)
    return mine + first.astype(jnp.float32)


def gather_rows_of(upper, lower):
    return lax.all_gather(jnp.concatenate([upper, lower], axis=0), "g", axis=0, tiled=True)


def gather_half(upper, lower):
    if lax.axis_size("g") != 4:
        return (upper, lower)
    column = lax.axis_index("g")
    return (
        ordered(column % 2, upper, swap_x(upper), 0),
        ordered(column // 2, lower, swap_y(lower), 0),
    )


def gather_rest(upper, lower):
    if lax.axis_size("g") != 4:
        return gather_rows_of(upper, lower)
    column = lax.axis_index("g")
    upper_all = ordered(column // 2, upper, swap_y(upper), 0)
    lower_all = ordered(column % 2, lower, swap_x(lower), 1)
    return jnp.stack([upper_all, lower_all], axis=2).reshape(-1, upper.shape[2])


def scatter_rows_of(partial):
    rows = lax.psum_scatter(partial, "g", scatter_dimension=0, tiled=True)
    half = rows.shape[0] // 2
    return (rows[:half], rows[half:])


def split_halves(values, bit, axis):
    low = lax.index_in_dim(values, 0, axis, keepdims=False)
    high = lax.index_in_dim(values, 1, axis, keepdims=False)
    mine = jnp.where(bit == 0, low, high).astype(jnp.float32)
    return (mine, jnp.where(bit == 0, high, low).astype(jnp.bfloat16))


def scatter_half(partial):
    if lax.axis_size("g") != 4:
        return scatter_rows_of(partial)
    column = lax.axis_index("g")
    blocks = partial.reshape(2, 2, 2, partial.shape[0] // 8, partial.shape[1])
    upper, upper_sent = split_halves(blocks[:, :, 0], column % 2, 1)
    lower, lower_sent = split_halves(blocks[:, :, 1], column // 2, 0)
    return (
        upper + swap_x(upper_sent).astype(jnp.float32),
        lower + swap_y(lower_sent).astype(jnp.float32),
    )


def scatter_rest(upper, lower):
    if lax.axis_size("g") != 4:
        return (upper, lower)
    column = lax.axis_index("g")
    upper, upper_sent = split_halves(upper, column // 2, 0)
    lower, lower_sent = split_halves(lower, column % 2, 0)
    upper = upper + swap_y(upper_sent).astype(jnp.float32)
    lower = lower + swap_x(lower_sent).astype(jnp.float32)
    return (upper.astype(jnp.bfloat16), lower.astype(jnp.bfloat16))


def heads_forward(hidden, tokens, attn_block, norm_pair, layout, maps, tables):
    query, key, value, remote_context, remote_totals, keep, send = attend_first(
        tokens, attn_block, maps[0], tables[0], *layout
    )
    leaving, query = lax.optimization_barrier((fold_remote(keep, send), query))
    near = swap_near(leaving)
    local_context, local_totals, keep, send = attend_second(attn_block, *layout, query, key, value)
    residual, normed, low = add_and_norm(hidden, keep, swap_core(send), near, norm_pair)
    kept = (
        tokens,
        (query, key, value, local_totals, remote_totals),
        (local_context, remote_context),
        residual,
    )
    return (normed, low, kept)


def units_forward(normed, low, unit_block, norm_pair):
    normed_all = gather_rows(low)
    local_keep, local_send = hidden_units(normed_all[:2], unit_block)
    sibling = swap_core(local_send)
    keep, send = hidden_units(normed_all[2:], unit_block)
    near = swap_near(fold_remote(keep, send))
    residual, output, low = add_and_norm(normed, local_keep, sibling, near, norm_pair)
    return (output, low, (normed_all, residual))


def units_backward(kept, grad_two, low, unit_block, norm_pair):
    residual_one, normed_all = kept[3:5]
    grad_mlp = gather_rows(low)
    local_pair, local_hidden, local_keep, local_send = units_back(
        normed_all[:2], grad_mlp[:2], unit_block
    )
    sibling = swap_core(local_send)
    remote_pair, remote_hidden, keep, send = units_back(normed_all[2:], grad_mlp[2:], unit_block)
    near = swap_near(fold_remote(keep, send))
    hidden = (local_hidden, remote_hidden)
    unit_grads = units_weights(normed_all, grad_mlp, (local_pair, remote_pair), hidden)
    near, unit_grads = lax.optimization_barrier((near, unit_grads))
    parts = (grad_two, local_keep, sibling, near)
    return (*norm_back(parts, residual_one, norm_pair), unit_grads)


def heads_backward(kept, low, attn_block, layout, maps, tables):
    tokens, heads_kept, context = kept[:3]
    grad_attn = gather_rows(low)
    grad_projected, *partial = attend_back(
        grad_attn, attn_block, maps[1], *tables[1:], *layout, heads_kept
    )
    return (partial, attend_weights(tokens, grad_attn, grad_projected, context))


def per_device(
    tokens,
    segment_ids,
    pair_doc,
    slot_of,
    master,
    first_moment,
    second_moment,
    norm_params,
    norm_first,
    norm_second,
):
    columns = lax.axis_size("g")
    owners = 2 * columns
    column = lax.axis_index("g")
    core = lax.axis_index("c")
    z_pair = lax.axis_index("zp")
    near_bit = lax.axis_index("a")
    width = master.shape[1]
    shard_rows = tokens.shape[0]
    in_place = core == z_pair
    seg_row = jnp.where(in_place, segment_ids, swap_core(segment_ids))[0]
    targets = jnp.where(in_place, pair_doc, swap_core(pair_doc))[0]
    member, positions, counts = segment_layout(seg_row, SEGS)
    chunk = near_bit + 2 * core
    chunk_order = [chunk, chunk ^ 2, chunk ^ 1, chunk ^ 3]

    def in_order(values):
        return jnp.concatenate(
            [
                lax.dynamic_slice_in_dim(values, index * shard_rows, shard_rows, 0)
                for index in chunk_order
            ],
            axis=0,
        )

    cosine, sine_table = rope_tables(in_order(positions), HEAD_DIM)
    heads = width // lax.axis_size(("zp", "a")) // HEAD_DIM
    maps = (spread_map(heads), unspread_map(heads))
    tables = (
        jnp.concatenate([cosine, sine_table], axis=1),
        jnp.concatenate([cosine, cosine], axis=1),
        jnp.concatenate([sine_table, sine_table], axis=1),
    )
    seg_local = in_order(seg_row)
    layout = (seg_local[:, None], seg_local[None, :])
    my_member = lax.dynamic_slice_in_dim(member, chunk * shard_rows, shard_rows, 0)[
        :, : SEGS - 1
    ].astype(jnp.float32)
    piece_rows = width // owners

    def to_owners(blocks):
        return lax.all_to_all(blocks, ("g", "c"), split_axis=0, concat_axis=0, tiled=True)

    outgoing = master.astype(jnp.bfloat16).reshape(OWN_MAX, owners, piece_rows, width)
    incoming = to_owners(outgoing.transpose(1, 0, 2, 3)).reshape(-1, piece_rows, width)
    low = turn(tokens)
    first_tokens = gather_rows(low)
    lengths = counts[: SEGS - 1].astype(jnp.float32)[:, None]
    targets = jnp.pad(targets.astype(jnp.float32)[:, None], ((0, SEGS - 1 - QRY_DEV), (0, 127)))
    early = (maps, tables, layout, lengths, targets, my_member)
    incoming, first_tokens, early = lax.optimization_barrier((incoming, first_tokens, early))
    maps, tables, layout, lengths, targets, my_member = early
    hidden = first_tokens[0].astype(jnp.float32)

    def piece_of(*matrices):
        return jnp.concatenate(
            [
                lax.dynamic_index_in_dim(incoming, slot_of[matrix], 0, keepdims=False)
                for matrix in matrices
            ],
            axis=1,
        )

    attn_pieces = to_working_block(piece_of(0))
    unit_pieces = to_working_block(after(piece_of(1, 2, 3), attn_pieces))
    attn_block = gather_rest(*gather_half(*attn_pieces))
    unit_pieces, attn_block = lax.optimization_barrier((unit_pieces, attn_block))
    unit_block = gather_rows_of(*unit_pieces)
    tokens_all = first_tokens
    kept_list, weight_list = [], []
    for layer_index in range(LAYERS):
        if layer_index > 0:
            tokens_all = gather_rows(low)
        norm_set = norm_params[layer_index]
        later = layer_index + 1 < LAYERS
        if later:
            base = 4 * (layer_index + 1)
            pieces = piece_of(base, base + 1, base + 2, base + 3)
            pieces = to_working_block(after(pieces, unit_pieces))
        weight_list.append((attn_block, unit_block))
        normed, low, heads_kept = heads_forward(
            hidden, tokens_all, attn_block, norm_set[:2], layout, maps, tables
        )
        if later:
            pieces, low = lax.optimization_barrier((pieces, low))
            attn_block = gather_rows_of(*[part[:, :width] for part in pieces])
        hidden, low, units_kept = units_forward(normed, low, unit_block, norm_set[2:])
        if later:
            unit_pieces, low = lax.optimization_barrier(([part[:, width:] for part in pieces], low))
            unit_block = gather_rows_of(*unit_pieces)
        kept_list.append((*heads_kept, *units_kept))
    pool_part = contract_exact(my_member, hidden)
    pool_part = pool_part + swap_core(pool_part)
    pooled_sum, sent = embed(pool_part, swap_near(pool_part), lengths, targets)
    far = swap_far(sent)
    pair = jnp.stack([jnp.where(z_pair == 0, sent, far), jnp.where(z_pair == 0, far, sent)])
    every = lax.all_gather(pair, "g", axis=0, tiled=True).reshape(-1, sent.shape[1])
    loss_total, gradient, low, second_params = loss_and_back(
        every,
        pooled_sum,
        lengths,
        my_member,
        (2 * column + z_pair).reshape(1, 1),
        kept_list[-1][-1],
        norm_params[LAYERS - 1, 2:],
    )
    loss_total = loss_total[0, 0]
    norm_list = [None] * LAYERS
    pending = []
    for layer_index in reversed(range(LAYERS)):
        kept = kept_list[layer_index]
        attn_block, unit_block = weight_list[layer_index]
        grad_one, low, first_params, unit_grads = units_backward(
            kept, gradient, low, unit_block, norm_params[layer_index, :2]
        )
        norm_list[layer_index] = jnp.concatenate([first_params, second_params], axis=0)
        unit_pieces = scatter_rows_of(after(unit_grads, pending))
        pending, low = lax.optimization_barrier((pending, low))
        arriving = [from_working_block(*pieces) for pieces in pending]
        (local_keep, local_send, keep, send), attn_grads = heads_backward(
            kept, low, attn_block, layout, maps, tables
        )
        if layer_index > 0:
            sibling = swap_core(local_send)
            near = swap_near(fold_remote(keep, send))
            near, attn_grads = lax.optimization_barrier((near, attn_grads))
            gradient, low, second_params = norm_back(
                (grad_one, local_keep, sibling, near),
                kept_list[layer_index - 1][-1],
                norm_params[layer_index - 1, 2:],
            )
            pending = [scatter_rows_of(after(attn_grads, unit_pieces)), unit_pieces]
    attn_halves = scatter_half(attn_grads)
    local_send, send = after((local_send, send), attn_halves)
    unit_arrived = from_working_block(*unit_pieces)
    attn_arrived = from_working_block(*scatter_rest(*attn_halves))
    sibling = swap_core(local_send)
    near = swap_near(fold_remote(keep, send))
    arrived = [attn_arrived, unit_arrived] + arriving
    parts = (grad_one, local_keep, sibling, near)
    gradient = sum(part.astype(jnp.float32) for part in parts)
    norm_stack = jnp.stack(norm_list).reshape(-1, width)
    gradient, norm_stack = after((gradient, norm_stack), attn_arrived)
    token_grad = turn(gradient.astype(jnp.bfloat16)).astype(jnp.float32)
    outgoing = jnp.zeros((OWN_MAX * owners, piece_rows, width), jnp.bfloat16)
    pieces = jnp.concatenate(arrived, axis=1).astype(jnp.bfloat16)
    for matrix in range(MATS):
        outgoing = lax.dynamic_update_index_in_dim(
            outgoing, pieces[:, matrix * width : (matrix + 1) * width], slot_of[matrix], 0
        )
    incoming = to_owners(outgoing.reshape(owners, OWN_MAX, piece_rows, width))
    my_grads = (
        incoming.transpose(1, 0, 2, 3).reshape(OWN_MAX, width, width).astype(jnp.float32)
    )
    slot_ids = (2 * column + core) * OWN_MAX + jnp.arange(OWN_MAX, dtype=jnp.int32)
    in_use = jnp.any(slot_of[None, :] == slot_ids[:, None], axis=1)[:, None, None]
    norm_total = norm_stack + swap_core(norm_stack)
    norm_total = norm_total + swap_near(norm_total)
    norm_total = norm_total + swap_far(norm_total)
    norm_total = jnp.sum(lax.all_gather(norm_total, "g", axis=0), axis=0)
    norm_total = norm_total.reshape(norm_params.shape)
    new_master, new_first, new_second = adam_update(
        master, first_moment, second_moment, my_grads, LEARN_RATE
    )
    new_master = jnp.where(in_use, new_master, master)
    new_first = jnp.where(in_use, new_first, first_moment)
    new_second = jnp.where(in_use, new_second, second_moment)
    new_norm, new_norm_first, new_norm_second = adam_update(
        norm_params, norm_first, norm_second, norm_total, NORM_RATE
    )
    return (
        loss_total,
        token_grad,
        new_master,
        new_first,
        new_second,
        new_master.astype(jnp.bfloat16),
        new_norm,
        new_norm_first,
        new_norm_second,
    )


def solution(mesh):
    owners, model_parts = mesh.devices.shape
    work_mesh = Mesh(mesh.devices.reshape(owners // 2, 2, model_parts // 2, 2), AXES)
    dp, mp = ("g", "c"), ("zp", "a")
    in_specs = (
        P(AXES, None),
        P(dp, None),
        P(dp, None),
        P(),
        P(dp, None, mp),
        P(dp, None, mp),
        P(dp, None, mp),
        P(),
        P(),
        P(),
    )
    out_specs = (
        P(),
        P(AXES, None),
        P(dp, None, mp),
        P(dp, None, mp),
        P(dp, None, mp),
        P(dp, None, mp),
        P(),
        P(),
        P(),
    )
    return jax.shard_map(
        per_device, mesh=work_mesh, in_specs=in_specs, out_specs=out_specs, check_vma=False
    )
```

```python
import functools

import jax
import jax.numpy as jnp
from jax import lax
from jax.experimental import pallas as pl
from jax.experimental.pallas import tpu as pltpu
from jax.sharding import Mesh
from jax.sharding import PartitionSpec as P

HEAD_DIM = 64
LAYERS = 2
QRY_DEV = 4
OWN_MAX = 2
STEP = 7
SEGS = 9
MATS = 8


BETA_ONE = 0.9
BETA_TWO = 0.999
LEARN_RATE = 0.02
NORM_RATE = 0.4
WEIGHT_DECAY = 0.5
ADAM_EPSILON = 1e-08
NORM_EPSILON = 1e-05
SOFTMAX_DIVISOR = 0.01
EXACT_ARITHMETIC = lax.Precision.HIGHEST


def segment_layout(seg_row, seg_count):
    length = seg_row.shape[0]
    place_ids = jnp.arange(length, dtype=jnp.int32)
    member = seg_row[:, None] == jnp.arange(seg_count, dtype=jnp.int32)[None, :]
    starts = jnp.min(jnp.where(member, place_ids[:, None], length), axis=0)
    counts = jnp.sum(member.astype(jnp.int32), axis=0)
    positions = place_ids - jnp.sum(jnp.where(member, starts[None, :], 0), axis=1)
    return (member, positions, counts)


def rope_tables(positions, head_dim):
    half_dim = head_dim // 2
    inverse = 1000.0 ** (-(jnp.arange(half_dim, dtype=jnp.float32) * 2.0 / head_dim))
    angles = positions.astype(jnp.float32)[:, None] * inverse[None, :]
    cosine = jnp.concatenate([jnp.cos(angles), jnp.cos(angles)], axis=1)
    sine_table = jnp.concatenate([jnp.sin(angles), jnp.sin(angles)], axis=1)
    return (cosine, sine_table)


def adam_update(weight, first_state, second_state, gradient, step_rate):
    first_new = BETA_ONE * first_state + (1.0 - BETA_ONE) * gradient
    second_new = BETA_TWO * second_state + (1.0 - BETA_TWO) * gradient * gradient
    first_hat = first_new / (1.0 - BETA_ONE**STEP)
    second_hat = second_new / (1.0 - BETA_TWO**STEP)
    weight_new = weight - step_rate * (
        first_hat / (jnp.sqrt(second_hat) + ADAM_EPSILON) + WEIGHT_DECAY * weight
    )
    return (weight_new, first_new, second_new)


def spread_map(heads):
    width = heads * HEAD_DIM
    half = HEAD_DIM // 2
    row = jnp.arange(3 * width, dtype=jnp.int32)[:, None]
    column = jnp.arange(6 * width, dtype=jnp.int32)[None, :]
    kind = column // (2 * width)
    head = column % (2 * width) // (2 * HEAD_DIM)
    lane = column % (2 * HEAD_DIM)
    base = kind * width + head * HEAD_DIM
    within = lane % HEAD_DIM
    plain = (row == base + within) & (lane < HEAD_DIM)
    turned = (lane >= HEAD_DIM) & (kind < 2)
    minus = turned & (within < half) & (row == base + within + half)
    plus = turned & (within >= half) & (row == base + within - half)
    return (plain.astype(jnp.float32) + plus - minus.astype(jnp.float32)).astype(jnp.bfloat16)


def unspread_map(heads):
    width = heads * HEAD_DIM
    half = HEAD_DIM // 2
    row = jnp.arange(4 * width, dtype=jnp.int32)[:, None]
    column = jnp.arange(2 * width, dtype=jnp.int32)[None, :]
    base = (column // HEAD_DIM) * 2 * HEAD_DIM
    within = column % HEAD_DIM
    plain = (row == base + within).astype(jnp.float32)
    plus = ((within < half) & (row == base + within + half)).astype(jnp.float32)
    minus = ((within >= half) & (row == base + within - half)).astype(jnp.float32)
    return jnp.stack([plain, plus - minus]).astype(jnp.bfloat16)


def flipped(left_side, right_side):
    return lax.dot_general(
        left_side, right_side, (((1,), (1,)), ((), ())), preferred_element_type=jnp.float32
    )


def straight(left_side, right_side):
    return jnp.dot(left_side, right_side, preferred_element_type=jnp.float32)


def over_rows(left_side, right_side):
    return lax.dot_general(
        left_side, right_side, (((0,), (0,)), ((), ())), preferred_element_type=jnp.float32
    )


def call(
    body, outputs, operands, scratch=(), mebibytes=16, blocked=False, near=(), far_out=(), name=None
):
    out_shape = tuple(
        pltpu.HBM(shape, dtype) if place in far_out else jax.ShapeDtypeStruct(shape, dtype)
        for place, (shape, dtype) in enumerate(outputs)
    )
    specs = {}
    if blocked:

        def whole(shape):
            zeros = (0,) * len(shape)
            return pl.BlockSpec(shape, lambda step: zeros, pipeline_mode=pl.Buffered(1))

        specs = {
            "grid": (1,),
            "in_specs": [whole(value.shape) for value in operands],
            "out_specs": tuple(whole(shape) for shape, _ in outputs),
        }
        operands = [
            value if place in near else pltpu.with_memory_space_constraint(value, pltpu.HBM)
            for place, value in enumerate(operands)
        ]
    return pl.pallas_call(
        body,
        out_shape=out_shape,
        scratch_shapes=list(scratch),
        compiler_params=pltpu.CompilerParams(vmem_limit_bytes=mebibytes * 2**20),
        cost_estimate=pl.CostEstimate(flops=10**6, bytes_accessed=10**5, transcendentals=0),
        name=name,
        **specs,
    )(*operands)


def attend_block(
    heads, chunk, rows, query_ref, key_ref, value_ref, seg_col_ref, seg_row_ref
):
    pad = 2 * HEAD_DIM
    span = slice(chunk * rows, (chunk + 1) * rows)
    bias = jnp.where(seg_col_ref[span, :] == seg_row_ref[...], 0.0, -1e30)
    lanes = lax.broadcasted_iota(jnp.int32, (rows, pad), 1)
    totals_all = jnp.zeros((rows, pad), jnp.float32)
    pieces = []
    for head in range(heads):
        cols = slice(head * pad, (head + 1) * pad)
        scores = flipped(query_ref[span, cols], key_ref[:, cols]) + bias
        row_top = jnp.max(scores, axis=-1, keepdims=True)
        weights = jnp.exp(scores - row_top)
        totals = jnp.sum(weights, axis=-1, keepdims=True)
        probs = (weights * (1.0 / totals)).astype(jnp.bfloat16)
        context = straight(probs, value_ref[:, cols])
        pieces.append(context[:, :HEAD_DIM].astype(jnp.bfloat16))
        totals_all = jnp.where(lanes == head, row_top + jnp.log(totals), totals_all)
    return (jnp.concatenate(pieces, axis=1), totals_all)


def attend_first_kernel(heads, *refs):
    chunk_refs, refs = refs[:4], refs[4:]
    weight_ref, map_ref, table_ref, seg_col_ref, seg_row_ref = refs[:5]
    query_ref, key_ref, value_ref, context_ref, total_ref, keep_ref, send_ref = refs[5:]
    width = heads * HEAD_DIM
    pad = 2 * HEAD_DIM
    rows = chunk_refs[0].shape[0]
    weights = straight(weight_ref[:, : 3 * width], map_ref[...]).astype(jnp.bfloat16)
    for chunk in range(4):
        span = slice(chunk * rows, (chunk + 1) * rows)
        projected = straight(chunk_refs[chunk][...], weights)
        table = table_ref[span, :]
        for head in range(heads):
            for base, ref, scale in ((0, query_ref, 0.0625), (heads * pad, key_ref, 1.0)):
                lanes = slice(base + head * pad, base + (head + 1) * pad)
                turned = projected[:, lanes] * table
                turned = turned + pltpu.roll(turned, HEAD_DIM, 1)
                ref[span, head * pad : (head + 1) * pad] = (turned * scale).astype(jnp.bfloat16)
        value_ref[span, :] = projected[:, 2 * heads * pad :].astype(jnp.bfloat16)
    out_weights = weight_ref[:, 3 * width :]
    for place, out_ref in enumerate((keep_ref, send_ref)):
        span = slice(place * rows, (place + 1) * rows)
        context, totals = attend_block(
            heads, place, rows, query_ref, key_ref, value_ref, seg_col_ref, seg_row_ref
        )
        context_ref[span, :] = context
        total_ref[span, :] = totals
        out_ref[...] = flipped(context, out_weights).astype(out_ref.dtype)


def attend_second_kernel(heads, *refs):
    weight_ref, seg_col_ref, seg_row_ref, query_ref, key_ref, value_ref = refs[:6]
    context_ref, total_ref, keep_ref, send_ref = refs[6:]
    rows = keep_ref.shape[0]
    out_weights = weight_ref[:, 3 * heads * HEAD_DIM :]
    for place, out_ref in enumerate((keep_ref, send_ref)):
        span = slice(place * rows, (place + 1) * rows)
        context, totals = attend_block(
            heads, 2 + place, rows, query_ref, key_ref, value_ref, seg_col_ref, seg_row_ref
        )
        context_ref[span, :] = context
        total_ref[span, :] = totals
        out_ref[...] = flipped(context, out_weights).astype(out_ref.dtype)


def attend_first(chunks, attn_block, mapping, table, seg_col, seg_row):
    width = attn_block.shape[0]
    part = attn_block.shape[1] // 4
    rows = chunks[0].shape[0]
    length = 4 * rows
    return call(
        functools.partial(attend_first_kernel, part // HEAD_DIM),
        [((length, 2 * part), jnp.bfloat16)] * 3
        + [
            ((2 * rows, part), jnp.bfloat16),
            ((2 * rows, 2 * HEAD_DIM), jnp.float32),
            ((rows, width), jnp.float32),
            ((rows, width), jnp.bfloat16),
        ],
        (*chunks, attn_block, mapping, table, seg_col, seg_row),
        mebibytes=28,
        blocked=True,
        near=(0, 1, 2, 3),
        name="attend_first",
    )


def attend_second(attn_block, seg_col, seg_row, query, key, value):
    width = attn_block.shape[0]
    part = attn_block.shape[1] // 4
    rows = query.shape[0] // 4
    return call(
        functools.partial(attend_second_kernel, part // HEAD_DIM),
        [
            ((2 * rows, part), jnp.bfloat16),
            ((2 * rows, 2 * HEAD_DIM), jnp.float32),
            ((rows, width), jnp.float32),
            ((rows, width), jnp.bfloat16),
        ],
        (attn_block, seg_col, seg_row, query, key, value),
        mebibytes=28,
        name="attend_second",
    )


def attend_back_kernel(heads, *refs):
    chunk_refs, refs = refs[:4], refs[4:]
    weight_ref, map_ref, cos_ref, sin_ref, seg_col_ref, seg_row_ref = refs[:6]
    query_ref, key_ref, value_ref, even_total_ref, odd_total_ref = refs[6:11]
    projected_ref, *out_refs = refs[11:16]
    grad_query, grad_key, grad_value = refs[16:]
    width = heads * HEAD_DIM
    pad = 2 * HEAD_DIM
    rows = chunk_refs[0].shape[0]
    out_weights = weight_ref[:, 3 * width :]
    empty = jnp.zeros((out_weights.shape[0], HEAD_DIM), jnp.bfloat16)
    wide = []
    for head in range(heads):
        wide += [out_weights[:, head * HEAD_DIM : (head + 1) * HEAD_DIM], empty]
    wide = jnp.concatenate(wide, axis=1)
    for chunk in range(4):
        span = slice(chunk * rows, (chunk + 1) * rows)
        grads_all = straight(chunk_refs[chunk][...], wide).astype(jnp.bfloat16)
        total_ref = even_total_ref if chunk < 2 else odd_total_ref
        total_span = slice(chunk % 2 * rows, (chunk % 2 + 1) * rows)
        bias = jnp.where(seg_col_ref[span, :] == seg_row_ref[...], 0.0, -1e30)
        for head in range(heads):
            cols = slice(head * pad, (head + 1) * pad)
            query = query_ref[span, cols]
            key = key_ref[:, cols]
            grads = grads_all[:, cols]
            scores = flipped(query, key) + bias
            probs = jnp.exp(scores - total_ref[total_span, head : head + 1])
            grad_probs = flipped(grads, value_ref[:, cols])
            inner = jnp.sum(probs * grad_probs, axis=-1, keepdims=True)
            grad_scores = (probs * (grad_probs - inner)).astype(jnp.bfloat16)
            grad_query[span, cols] = (straight(grad_scores, key) * 0.125).astype(jnp.bfloat16)
            key_part = straight(query.T, grad_scores)
            value_part = straight(grads.T, probs.astype(jnp.bfloat16))
            if chunk == 0:
                grad_key[cols, :] = key_part
                grad_value[cols, :] = value_part
            else:
                grad_key[cols, :] += key_part
                grad_value[cols, :] += value_part
    for chunk, out_ref in enumerate(out_refs):
        span = slice(chunk * rows, (chunk + 1) * rows)
        grad_k = (grad_key[:, span] * 2.0).astype(jnp.bfloat16).T
        grad_v = grad_value[:, span].astype(jnp.bfloat16).T
        both = jnp.concatenate([grad_query[span, :], grad_k], axis=1)
        plain = straight(both, map_ref[0])
        turned = straight(both, map_ref[1])
        cosine = jnp.concatenate([cos_ref[span, :]] * heads, axis=1)
        sine = jnp.concatenate([sin_ref[span, :]] * heads, axis=1)
        turned = (plain * cosine + turned * sine).astype(jnp.bfloat16)
        grad_v = [grad_v[:, head * pad : head * pad + HEAD_DIM] for head in range(heads)]
        projected = jnp.concatenate([turned, *grad_v], axis=1)
        projected_ref[span, :] = projected
        out_ref[...] = flipped(projected, weight_ref[:, : 3 * width]).astype(out_ref.dtype)


def attend_back(chunks, attn_block, mapping, cosine, sine, seg_col, seg_row, kept):
    width = attn_block.shape[0]
    part = attn_block.shape[1] // 4
    rows = chunks[0].shape[0]
    length = 4 * rows
    return call(
        functools.partial(attend_back_kernel, part // HEAD_DIM),
        [((length, 3 * part), jnp.bfloat16)]
        + [((rows, width), jnp.float32), ((rows, width), jnp.bfloat16)] * 2,
        (*chunks, attn_block, mapping, cosine, sine, seg_col, seg_row, *kept),
        mebibytes=28,
        scratch=[
            pltpu.VMEM((length, 2 * part), jnp.bfloat16),
            pltpu.VMEM((2 * part, length), jnp.float32),
            pltpu.VMEM((2 * part, length), jnp.float32),
        ],
        name="attend_back",
    )


def units_kernel(*refs):
    chunk_refs, (weight_ref, keep_ref, send_ref) = refs[:2], refs[2:]
    units = weight_ref.shape[1] // 3
    for chunk_ref, out_ref in zip(chunk_refs, (keep_ref, send_ref)):
        tokens = chunk_ref[...]
        gate = straight(tokens, weight_ref[:, :units])
        up = straight(tokens, weight_ref[:, units : 2 * units])
        hidden = (gate / (1.0 + jnp.exp(-gate)) * up).astype(jnp.bfloat16)
        out_ref[...] = flipped(hidden, weight_ref[:, 2 * units :]).astype(out_ref.dtype)


def hidden_units(chunks, weights):
    rows, width = chunks[0].shape
    return call(
        units_kernel,
        [((rows, width), jnp.float32), ((rows, width), jnp.bfloat16)],
        (*chunks, weights),
        name="hidden_units",
    )


def units_back_kernel(*refs):
    token_refs, chunk_refs, weight_ref = refs[:2], refs[2:4], refs[4]
    grad_ref, hidden_ref, keep_ref, send_ref = refs[5:]
    rows, width = chunk_refs[0].shape
    units = weight_ref.shape[1] // 3
    for place, out_ref in enumerate((keep_ref, send_ref)):
        span = slice(place * rows, (place + 1) * rows)
        tokens = token_refs[place][...]
        gate = straight(tokens, weight_ref[:, :units])
        up = straight(tokens, weight_ref[:, units : 2 * units])
        grad_hidden = straight(chunk_refs[place][...], weight_ref[:, 2 * units :])
        share = 1.0 / (1.0 + jnp.exp(-gate))
        silu = gate * share
        hidden_ref[span, :] = (silu * up).astype(jnp.bfloat16)
        grad_up = (grad_hidden * silu).astype(jnp.bfloat16)
        slope = share + silu * (1.0 - share)
        grad_gate = (grad_hidden * up * slope).astype(jnp.bfloat16)
        grad_ref[span, :units] = grad_gate
        grad_ref[span, units:] = grad_up
        result = flipped(grad_gate, weight_ref[:, :units])
        result = result + flipped(grad_up, weight_ref[:, units : 2 * units])
        out_ref[...] = result.astype(out_ref.dtype)


def units_back(tokens, chunks, weights):
    rows, width = chunks[0].shape
    units = weights.shape[1] // 3
    return call(
        units_back_kernel,
        [
            ((2 * rows, 2 * units), jnp.bfloat16),
            ((2 * rows, units), jnp.bfloat16),
            ((rows, width), jnp.float32),
            ((rows, width), jnp.bfloat16),
        ],
        (*tokens, *chunks, weights),
        mebibytes=24,
        name="units_back",
    )


def units_weights_kernel(*refs):
    token_refs, grad_refs, refs = refs[:4], refs[4:8], refs[8:]
    even_pair_ref, odd_pair_ref, even_hidden_ref, odd_hidden_ref, out_ref = refs
    rows, width = token_refs[0].shape
    units = even_hidden_ref.shape[1]
    for tile in range(0, width, 256):
        cols = slice(tile, tile + 256)
        pair, down = 0.0, 0.0
        for chunk in range(4):
            span = slice(chunk % 2 * rows, (chunk % 2 + 1) * rows)
            pair_ref = even_pair_ref if chunk < 2 else odd_pair_ref
            hidden_ref = even_hidden_ref if chunk < 2 else odd_hidden_ref
            pair = pair + over_rows(token_refs[chunk][:, cols], pair_ref[span, :])
            down = down + over_rows(grad_refs[chunk][:, cols], hidden_ref[span, :])
        out_ref[cols, : 2 * units] = pair.astype(jnp.bfloat16)
        out_ref[cols, 2 * units :] = down.astype(jnp.bfloat16)


def units_weights(tokens, grads, pairs, hidden):
    rows, width = tokens[0].shape
    units = hidden[0].shape[1]
    return call(
        units_weights_kernel,
        [((width, 3 * units), jnp.bfloat16)],
        (*tokens, *grads, *pairs, *hidden),
        blocked=True,
        near=tuple(range(12)),
        far_out=(0,),
        name="units_weights",
    )[0]


def attend_weights_kernel(*refs):
    token_refs, grad_refs, refs = refs[:4], refs[4:8], refs[8:]
    projected_ref, even_context_ref, odd_context_ref, out_ref = refs
    rows, width = token_refs[0].shape
    for tile in range(0, width, 256):
        cols = slice(tile, tile + 256)
        left, right = 0.0, 0.0
        for chunk in range(4):
            span = slice(chunk % 2 * rows, (chunk % 2 + 1) * rows)
            context_ref = even_context_ref if chunk < 2 else odd_context_ref
            projected = projected_ref[chunk * rows : (chunk + 1) * rows, :]
            left = left + over_rows(token_refs[chunk][:, cols], projected)
            right = right + over_rows(grad_refs[chunk][:, cols], context_ref[span, :])
        both = jnp.concatenate([left, right], axis=1)
        out_ref[cols, :] = both.astype(jnp.bfloat16)


def attend_weights(tokens, grads, projected, context):
    rows, width = tokens[0].shape
    part = context[0].shape[1]
    return call(
        attend_weights_kernel,
        [((width, 4 * part), jnp.bfloat16)],
        (*tokens, *grads, projected, *context),
        blocked=True,
        near=tuple(range(11)),
        far_out=(0,),
        name="attend_weights",
    )[0]


def norm_kernel(*refs):
    base_ref, own_ref, near_ref, norm_ref, residual_ref, normed_ref, low_ref = refs
    residual = base_ref[...] + own_ref[...] + near_ref[...].astype(jnp.float32)
    residual_ref[...] = residual
    centered = residual - jnp.mean(residual, axis=-1, keepdims=True)
    variance = jnp.mean(centered * centered, axis=-1, keepdims=True)
    normed = centered * lax.rsqrt(variance + NORM_EPSILON) * norm_ref[0:1, :] + norm_ref[1:2, :]
    normed_ref[...] = normed
    low_ref[...] = normed.astype(jnp.bfloat16)


def add_and_norm(base, own, near, norm_pair):
    shape = base.shape
    return call(
        norm_kernel,
        [(shape, jnp.float32), (shape, jnp.float32), (shape, jnp.bfloat16)],
        (base, own, near, norm_pair),
        blocked=True,
        near=(1, 2),
        far_out=(0, 1),
        name="add_and_norm",
    )


def norm_back_rows(grad, residual, gain):
    centered = residual - jnp.mean(residual, axis=-1, keepdims=True)
    variance = jnp.mean(centered * centered, axis=-1, keepdims=True)
    inverse = lax.rsqrt(variance + NORM_EPSILON)
    scaled = centered * inverse
    wide = grad * gain
    inner = jnp.mean(wide * scaled, axis=-1, keepdims=True)
    result = inverse * (wide - jnp.mean(wide, axis=-1, keepdims=True) - scaled * inner)
    gain_grad = jnp.sum(grad * scaled, axis=0, keepdims=True)
    return (result, jnp.concatenate([gain_grad, jnp.sum(grad, axis=0, keepdims=True)], axis=0))


def norm_back_kernel(*refs):
    part_refs, (residual_ref, norm_ref, out_ref, low_ref, params_ref) = refs[:-5], refs[-5:]
    grad = part_refs[0][...]
    for part_ref in part_refs[1:]:
        grad = grad + part_ref[...].astype(jnp.float32)
    result, params = norm_back_rows(grad, residual_ref[...], norm_ref[0:1, :])
    out_ref[...] = result
    low_ref[...] = result.astype(jnp.bfloat16)
    params_ref[...] = params


def norm_back(parts, residual, norm_pair):
    shape = residual.shape
    return call(
        norm_back_kernel,
        [(shape, jnp.float32), (shape, jnp.bfloat16), ((2, shape[1]), jnp.float32)],
        (*parts, residual, norm_pair),
        blocked=True,
        near=tuple(range(1, len(parts))),
        far_out=(0, 2),
        name="norm_back",
    )


def embed_kernel(sum_ref, near_ref, length_ref, target_ref, total_ref, out_ref):
    total = sum_ref[...] + near_ref[...]
    total_ref[...] = total
    pooled = total / length_ref[...]
    embeds = pooled * lax.rsqrt(jnp.sum(pooled * pooled, axis=1, keepdims=True) + 1e-06)
    out_ref[...] = jnp.concatenate([embeds, target_ref[...]], axis=1).astype(jnp.bfloat16)


def embed(pool_part, near_part, lengths, targets):
    rows, width = pool_part.shape
    return call(
        embed_kernel,
        [
            ((rows, width), jnp.float32),
            ((rows, width + targets.shape[1]), jnp.bfloat16),
        ],
        (pool_part, near_part, lengths, targets),
        blocked=True,
        far_out=(),
        name="embed",
    )


def pool_kernel(even_ref, odd_ref, member_ref, out_ref):
    rows = even_ref.shape[0]
    total = 0.0
    for chunk, hidden_ref in enumerate((even_ref, odd_ref)):
        member = member_ref[chunk * rows : (chunk + 1) * rows, :]
        total = total + exact(member.T, hidden_ref[...])
    out_ref[...] = total


def pool(hidden, member):
    return call(
        pool_kernel,
        [((member.shape[1], hidden[0].shape[1]), jnp.float32)],
        (*hidden, member),
        blocked=True,
        near=(0, 1),
        name="pool",
    )[0]


def loss_kernel(*refs):
    every_ref, sum_ref, length_ref, member_ref, group_ref, *residual_refs, norm_ref = refs[:8]
    loss_ref, *out_refs = refs[8:]
    width = sum_ref.shape[1]
    rows = SEGS - 1
    docs = rows - QRY_DEV
    total = every_ref.shape[0]
    vectors = every_ref[:, :width]
    targets = every_ref[:, width : width + 1].astype(jnp.float32)
    scores = flipped(vectors, vectors) / SOFTMAX_DIVISOR
    row = lax.broadcasted_iota(jnp.int32, (total, total), 0)
    column = lax.broadcasted_iota(jnp.int32, (total, total), 1)
    place = column % rows
    is_doc = place >= QRY_DEV
    doc = column // rows * docs + place - QRY_DEV
    is_query = row % rows < QRY_DEV
    hit = is_doc & (doc.astype(jnp.float32) == targets)
    masked = jnp.where(is_doc, scores, -1e30)
    row_top = jnp.max(masked, axis=1, keepdims=True)
    log_totals = row_top + jnp.log(jnp.sum(jnp.exp(masked - row_top), axis=1, keepdims=True))
    chosen = jnp.sum(jnp.where(hit, scores, 0.0), axis=1, keepdims=True)
    losses = jnp.where(is_query[:, :1], log_totals - chosen, 0.0)
    loss_ref[...] = jnp.sum(losses, axis=0, keepdims=True)
    logits = (jnp.exp(masked - log_totals) - hit.astype(jnp.float32)) / SOFTMAX_DIVISOR
    logits = jnp.where(is_query & is_doc, logits, 0.0)
    wide = vectors.astype(jnp.float32)
    embed_grads = exact(logits, wide) + exact(logits.T, wide)
    mine = lax.broadcasted_iota(jnp.int32, (rows, total), 1) - group_ref[...] * rows
    mine = (mine == lax.broadcasted_iota(jnp.int32, (rows, total), 0)).astype(jnp.float32)
    embed_grads = exact(mine, embed_grads)
    pooled = sum_ref[...] / length_ref[...]
    inverse = lax.rsqrt(jnp.sum(pooled * pooled, axis=1, keepdims=True) + 1e-06)
    inner = jnp.sum(embed_grads * pooled, axis=1, keepdims=True)
    pooled_grads = embed_grads * inverse - pooled * (inverse * inverse * inverse * inner)
    pooled_grads = pooled_grads / length_ref[...]
    chunk_rows = residual_refs[0].shape[0]
    for chunk, residual_ref in enumerate(residual_refs):
        member = member_ref[chunk * chunk_rows : (chunk + 1) * chunk_rows, :]
        grad = exact(member, pooled_grads)
        result, params = norm_back_rows(grad, residual_ref[...], norm_ref[0:1, :])
        out_ref, low_ref, params_ref = out_refs[3 * chunk : 3 * chunk + 3]
        out_ref[...] = result
        low_ref[...] = result.astype(jnp.bfloat16)
        params_ref[...] = params


def exact(left_side, right_side):
    return lax.dot_general(
        left_side,
        right_side,
        (((1,), (0,)), ((), ())),
        precision=EXACT_ARITHMETIC,
        preferred_element_type=jnp.float32,
    )


def loss_and_back(every, pooled_sum, lengths, member, group, residual, norm_pair):
    shape = residual[0].shape
    chunk_out = [
        (shape, jnp.float32),
        (shape, jnp.bfloat16),
        ((2, shape[1]), jnp.float32),
    ]
    loss, *outputs = call(
        loss_kernel,
        [((1, 1), jnp.float32), *chunk_out, *chunk_out],
        (every, pooled_sum, lengths, member, group, *residual, norm_pair),
        blocked=True,
        far_out=(0, 1, 3, 4, 6),
        name="loss_and_back",
    )
    return (loss[0, 0], *zip(outputs[:3], outputs[3:]))


AXES = ("g", "c", "zp", "a")


def hop(value, move):
    columns = lax.axis_size("g")
    pairs = []
    for column in range(columns):
        for core in range(2):
            for z in range(4):
                to_column, to_core, to_z = move(column, core, z)
                pairs.append(((column * 2 + core) * 4 + z, (to_column * 2 + to_core) * 4 + to_z))
    return lax.ppermute(value, AXES, pairs)


def swap_core(value):
    return hop(value, lambda g, c, z: (g, 1 - c, z))


def swap_near(value):
    return hop(value, lambda g, c, z: (g, c, z ^ 1))


def swap_far(value):
    return hop(value, lambda g, c, z: (g, c, z ^ 2))


def turn(value):
    return hop(value, lambda g, c, z: (g, z // 2, 2 * c + z % 2))


def first_rows(tokens):
    own = turn(tokens)
    sibling = hop(tokens, lambda g, c, z: (g, 1 - z // 2, 2 * c + z % 2))
    near = hop(tokens, lambda g, c, z: (g, z // 2, 2 * c + (z % 2 ^ 1)))
    across = hop(tokens, lambda g, c, z: (g, 1 - z // 2, 2 * c + (z % 2 ^ 1)))
    even = lax.axis_index("a") == 0
    return (
        jnp.where(even, own, near),
        jnp.where(even, sibling, across),
        jnp.where(even, near, own),
        jnp.where(even, across, sibling),
    )


def share(low):
    return (low[0], swap_core(low[0]), low[1], swap_core(low[1]))


def core_sum(keep, send):
    total = keep + swap_core(send).astype(jnp.float32)
    return (total, total.astype(jnp.bfloat16))


def core_sum_at_once(keep, send):
    both = lax.all_gather(send, "c", axis=0)
    other = jnp.where(lax.axis_index("c") == 0, both[1], both[0])
    total = keep + other.astype(jnp.float32)
    return (total, total.astype(jnp.bfloat16))


def after(value, *others):
    return lax.optimization_barrier((value, *others))[0]


def swap_x(value):
    return hop(value, lambda g, c, z: (g ^ 1, c, z))


def swap_y(value):
    return hop(value, lambda g, c, z: (g ^ 2, c, z))


def ordered(bit, mine, other, axis):
    low = jnp.where(bit == 0, mine, other)
    return jnp.stack([low, jnp.where(bit == 0, other, mine)], axis=axis)


def to_working_block(piece):
    core = lax.axis_index("c")
    first = hop(piece, lambda g, c, z: (g, 0, z) if c == 1 else (g, 1, z ^ 2))
    second = hop(piece, lambda g, c, z: (g, 1, z ^ 2) if c == 1 else (g, 0, z))
    return (jnp.where(core == 0, piece, first), jnp.where(core == 0, first, second))


def from_working_block(upper, lower):
    core = lax.axis_index("c")
    first = hop(
        jnp.where(core == 0, lower, upper),
        lambda g, c, z: (g, 1, z) if c == 0 else (g, 0, z ^ 2),
    )
    second = hop(lower, lambda g, c, z: (g, 1, z ^ 2) if c == 1 else (g, 0, z))
    mine = jnp.where(core == 0, upper, second).astype(jnp.float32)
    return mine + first.astype(jnp.float32)


def gather_rows_of(upper, lower):
    return lax.all_gather(jnp.concatenate([upper, lower], axis=0), "g", axis=0, tiled=True)


def gather_half(upper, lower):
    if lax.axis_size("g") != 4:
        return (upper, lower)
    column = lax.axis_index("g")
    return (
        ordered(column % 2, upper, swap_x(upper), 0),
        ordered(column // 2, lower, swap_y(lower), 0),
    )


def gather_rest(upper, lower):
    if lax.axis_size("g") != 4:
        return gather_rows_of(upper, lower)
    column = lax.axis_index("g")
    upper_all = ordered(column // 2, upper, swap_y(upper), 0)
    lower_all = ordered(column % 2, lower, swap_x(lower), 1)
    return jnp.stack([upper_all, lower_all], axis=2).reshape(-1, upper.shape[2])


def scatter_rows_of(partial):
    rows = lax.psum_scatter(partial, "g", scatter_dimension=0, tiled=True)
    half = rows.shape[0] // 2
    return (rows[:half], rows[half:])


def split_halves(values, bit, axis):
    low = lax.index_in_dim(values, 0, axis, keepdims=False)
    high = lax.index_in_dim(values, 1, axis, keepdims=False)
    mine = jnp.where(bit == 0, low, high).astype(jnp.float32)
    return (mine, jnp.where(bit == 0, high, low).astype(jnp.bfloat16))


def scatter_half(partial):
    if lax.axis_size("g") != 4:
        return scatter_rows_of(partial)
    column = lax.axis_index("g")
    blocks = partial.reshape(2, 2, 2, partial.shape[0] // 8, partial.shape[1])
    upper, upper_sent = split_halves(blocks[:, :, 0], column % 2, 1)
    lower, lower_sent = split_halves(blocks[:, :, 1], column // 2, 0)
    return (
        upper + swap_x(upper_sent).astype(jnp.float32),
        lower + swap_y(lower_sent).astype(jnp.float32),
    )


def scatter_rest(upper, lower):
    if lax.axis_size("g") != 4:
        return (upper, lower)
    column = lax.axis_index("g")
    upper, upper_sent = split_halves(upper, column // 2, 0)
    lower, lower_sent = split_halves(lower, column % 2, 0)
    upper = upper + swap_y(upper_sent).astype(jnp.float32)
    lower = lower + swap_x(lower_sent).astype(jnp.float32)
    return (upper.astype(jnp.bfloat16), lower.astype(jnp.bfloat16))


def heads_forward(hidden, tokens, attn_block, norm_pair, layout, maps, tables):
    query, key, value, even_context, even_totals, keep, send = attend_first(
        tokens, attn_block, maps[0], tables[0], *layout
    )
    even, leaving = core_sum(keep, send)
    leaving, query = lax.optimization_barrier((leaving, query))
    even_near = swap_near(leaving)
    odd_context, odd_totals, keep, send = attend_second(attn_block, *layout, query, key, value)
    odd, leaving = core_sum_at_once(keep, send)
    odd_near = swap_near(leaving)
    even_results = add_and_norm(hidden[0], even, even_near, norm_pair)

    def finish(other):
        return add_and_norm(hidden[1], odd, after(odd_near, other), norm_pair)

    kept = (
        tokens,
        (query, key, value, even_totals, odd_totals),
        (even_context, odd_context),
    )
    return (even_results, finish, kept)


def units_forward(even_results, finish, unit_block, norm_pair):
    residual_one, normed, low = even_results
    even_all = (low, swap_core(low))
    keep, send = hidden_units(even_all, unit_block)
    even, leaving = core_sum_at_once(keep, send)
    residual_odd, normed_odd, low = finish(leaving)
    even_near = swap_near(leaving)
    odd_all = (low, swap_core(low))
    keep, send = hidden_units(odd_all, unit_block)
    odd, leaving = core_sum_at_once(keep, send)
    results = (
        add_and_norm(normed, even, even_near, norm_pair),
        add_and_norm(normed_odd, odd, swap_near(leaving), norm_pair),
    )
    residual, output, low = zip(*results)
    kept = ((residual_one, residual_odd), (*even_all, *odd_all), residual)
    return (output, low, kept)


def units_backward(kept, grad_two, low, unit_block, norm_pair):
    residual_one, normed_all = kept[3:5]
    grad_mlp = share(low)
    pairs, hidden, sums, nears = [], [], [], []
    for chunk in range(2):
        span = slice(2 * chunk, 2 * chunk + 2)
        pair, units, keep, send = units_back(normed_all[span], grad_mlp[span], unit_block)
        own, leaving = core_sum_at_once(keep, send)
        pairs.append(pair)
        hidden.append(units)
        sums.append(own)
        nears.append(swap_near(leaving))
    unit_grads = units_weights(normed_all, grad_mlp, pairs, hidden)
    nears, unit_grads = lax.optimization_barrier((nears, unit_grads))
    results = [
        norm_back((grad_two[chunk], sums[chunk], nears[chunk]), residual_one[chunk], norm_pair)
        for chunk in range(2)
    ]
    return (*zip(*results), unit_grads)


def heads_backward(kept, low, attn_block, layout, maps, tables):
    tokens, heads_kept, context = kept[:3]
    grad_attn = share(low)
    grad_projected, *partial = attend_back(
        grad_attn, attn_block, maps[1], *tables[1:], *layout, heads_kept
    )
    return (partial, attend_weights(tokens, grad_attn, grad_projected, context))


def per_device(
    tokens,
    segment_ids,
    pair_doc,
    slot_of,
    master,
    first_moment,
    second_moment,
    norm_params,
    norm_first,
    norm_second,
):
    columns = lax.axis_size("g")
    owners = 2 * columns
    column = lax.axis_index("g")
    core = lax.axis_index("c")
    z_pair = lax.axis_index("zp")
    near_bit = lax.axis_index("a")
    width = master.shape[1]
    shard_rows = tokens.shape[0]
    in_place = core == z_pair
    seg_row = jnp.where(in_place, segment_ids, swap_core(segment_ids))[0]
    targets = jnp.where(in_place, pair_doc, swap_core(pair_doc))[0]
    member, positions, counts = segment_layout(seg_row, SEGS)
    even = near_bit == 0
    chunk_order = [2 * core, 2 * core ^ 2, 2 * core + 1, 2 * core + 1 ^ 2]

    def in_order(values):
        return jnp.concatenate(
            [
                lax.dynamic_slice_in_dim(values, index * shard_rows, shard_rows, 0)
                for index in chunk_order
            ],
            axis=0,
        )

    cosine, sine_table = rope_tables(in_order(positions), HEAD_DIM)
    heads = width // lax.axis_size(("zp", "a")) // HEAD_DIM
    maps = (spread_map(heads), unspread_map(heads))
    tables = (
        jnp.concatenate([cosine, sine_table], axis=1),
        jnp.concatenate([cosine, cosine], axis=1),
        jnp.concatenate([sine_table, sine_table], axis=1),
    )
    seg_local = in_order(seg_row)
    layout = (seg_local[:, None], seg_local[None, :])
    member = lax.dynamic_slice_in_dim(member, 2 * core * shard_rows, 2 * shard_rows, 0)
    member = member[:, : SEGS - 1].astype(jnp.float32)
    counted = jnp.arange(2 * shard_rows)[:, None] // shard_rows == near_bit
    own_member = jnp.where(counted, member, 0.0)
    piece_rows = width // owners

    def to_owners(blocks):
        return lax.all_to_all(blocks, ("g", "c"), split_axis=0, concat_axis=0, tiled=True)

    tokens_all = first_rows(tokens)
    outgoing = master.astype(jnp.bfloat16).reshape(OWN_MAX, owners, piece_rows, width)
    incoming = to_owners(outgoing.transpose(1, 0, 2, 3)).reshape(-1, piece_rows, width)
    lengths = counts[: SEGS - 1].astype(jnp.float32)[:, None]
    targets = jnp.pad(targets.astype(jnp.float32)[:, None], ((0, SEGS - 1 - QRY_DEV), (0, 127)))
    hidden = (tokens_all[0].astype(jnp.float32), tokens_all[2].astype(jnp.float32))
    early = (tokens_all, hidden, maps, tables, layout, lengths, targets, member, own_member)
    incoming, early = lax.optimization_barrier((incoming, early))
    tokens_all, hidden, maps, tables, layout, lengths, targets, member, own_member = early

    def piece_of(*matrices):
        return jnp.concatenate(
            [
                lax.dynamic_index_in_dim(incoming, slot_of[matrix], 0, keepdims=False)
                for matrix in matrices
            ],
            axis=1,
        )

    attn_pieces = to_working_block(piece_of(0))
    unit_pieces = to_working_block(piece_of(1, 2, 3))
    attn_block = gather_rest(*gather_half(*attn_pieces))
    unit_pieces, attn_block = lax.optimization_barrier((unit_pieces, attn_block))
    unit_block = gather_rows_of(*unit_pieces)
    kept_list, weight_list = [], []
    for layer_index in range(LAYERS):
        if layer_index > 0:
            tokens_all = share(low)
        norm_set = norm_params[layer_index]
        later = layer_index + 1 < LAYERS
        if later:
            base = 4 * (layer_index + 1)
            pieces = piece_of(base, base + 1, base + 2, base + 3)
            pieces = to_working_block(after(pieces, unit_pieces))
        weight_list.append((attn_block, unit_block))
        even_results, finish, heads_kept = heads_forward(
            hidden, tokens_all, attn_block, norm_set[:2], layout, maps, tables
        )
        if later:
            pieces, even_results = lax.optimization_barrier((pieces, even_results))
            attn_block = gather_rows_of(*[part[:, :width] for part in pieces])
        hidden, low, units_kept = units_forward(
            even_results, finish, unit_block, norm_set[2:]
        )
        if later:
            unit_pieces, low = lax.optimization_barrier(([part[:, width:] for part in pieces], low))
            unit_block = gather_rows_of(*unit_pieces)
        kept_list.append((*heads_kept, *units_kept))
    pool_part = pool(hidden, own_member)
    pool_part = pool_part + swap_core(pool_part)
    pooled_sum, sent = embed(pool_part, swap_near(pool_part), lengths, targets)
    far = swap_far(sent)
    pair = jnp.stack([jnp.where(z_pair == 0, sent, far), jnp.where(z_pair == 0, far, sent)])
    every = lax.all_gather(pair, "g", axis=0, tiled=True).reshape(-1, sent.shape[1])
    loss_total, gradient, low, second_params = loss_and_back(
        every,
        pooled_sum,
        lengths,
        member,
        (2 * column + z_pair).reshape(1, 1),
        kept_list[-1][-1],
        norm_params[LAYERS - 1, 2:],
    )
    norm_list = [None] * LAYERS
    pending = []
    for layer_index in reversed(range(LAYERS)):
        kept = kept_list[layer_index]
        attn_block, unit_block = weight_list[layer_index]
        grad_one, low, first_params, unit_grads = units_backward(
            kept, gradient, low, unit_block, norm_params[layer_index, :2]
        )
        norm_list[layer_index] = jnp.concatenate(
            [jnp.where(even, *first_params), jnp.where(even, *second_params)], axis=0
        )
        unit_pieces = scatter_rows_of(after(unit_grads, pending))
        pending, low = lax.optimization_barrier((pending, low))
        arriving = [from_working_block(*pieces) for pieces in pending]
        partial, attn_grads = heads_backward(kept, low, attn_block, layout, maps, tables)
        if layer_index > 0:
            sums, nears = [], []
            for chunk in range(2):
                own, leaving = core_sum_at_once(*partial[2 * chunk : 2 * chunk + 2])
                sums.append(own)
                nears.append(swap_near(leaving))
            nears, attn_grads = lax.optimization_barrier((nears, attn_grads))
            results = [
                norm_back(
                    (grad_one[chunk], sums[chunk], nears[chunk]),
                    kept_list[layer_index - 1][-1][chunk],
                    norm_params[layer_index - 1, 2:],
                )
                for chunk in range(2)
            ]
            gradient, low, second_params = zip(*results)
            pending = [scatter_rows_of(after(attn_grads, unit_pieces)), unit_pieces]
    partial, attn_grads = lax.optimization_barrier((partial, attn_grads))
    attn_halves = scatter_half(attn_grads)
    even_sum, even_low = core_sum(*partial[:2])
    odd_sum, odd_low = core_sum(*partial[2:])
    near = swap_near(jnp.where(even, odd_low, even_low))
    attn_halves, unit_pieces = lax.optimization_barrier((attn_halves, unit_pieces))
    unit_arrived = from_working_block(*unit_pieces)
    attn_arrived = from_working_block(*scatter_rest(*attn_halves))
    arrived = [attn_arrived, unit_arrived] + arriving
    gradient = jnp.where(even, grad_one[0], grad_one[1])
    gradient = gradient + jnp.where(even, even_sum, odd_sum) + near.astype(jnp.float32)
    norm_stack = jnp.stack(norm_list).reshape(-1, width)
    gradient, norm_stack = after((gradient, norm_stack), attn_arrived)
    token_grad = turn(gradient.astype(jnp.bfloat16)).astype(jnp.float32)
    outgoing = jnp.zeros((OWN_MAX * owners, piece_rows, width), jnp.bfloat16)
    pieces = jnp.concatenate(arrived, axis=1).astype(jnp.bfloat16)
    for matrix in range(MATS):
        outgoing = lax.dynamic_update_index_in_dim(
            outgoing, pieces[:, matrix * width : (matrix + 1) * width], slot_of[matrix], 0
        )
    incoming = to_owners(outgoing.reshape(owners, OWN_MAX, piece_rows, width))
    my_grads = (
        incoming.transpose(1, 0, 2, 3).reshape(OWN_MAX, width, width).astype(jnp.float32)
    )
    slot_ids = (2 * column + core) * OWN_MAX + jnp.arange(OWN_MAX, dtype=jnp.int32)
    in_use = jnp.any(slot_of[None, :] == slot_ids[:, None], axis=1)[:, None, None]
    norm_total = norm_stack + swap_core(norm_stack)
    norm_total = norm_total + swap_near(norm_total)
    norm_total = norm_total + swap_far(norm_total)
    if columns == 4:
        norm_total = norm_total + swap_x(norm_total)
        norm_total = norm_total + swap_y(norm_total)
    else:
        norm_total = jnp.sum(lax.all_gather(norm_total, "g", axis=0), axis=0)
    norm_total = norm_total.reshape(norm_params.shape)
    new_master, new_first, new_second = adam_update(
        master, first_moment, second_moment, my_grads, LEARN_RATE
    )
    new_master = jnp.where(in_use, new_master, master)
    new_first = jnp.where(in_use, new_first, first_moment)
    new_second = jnp.where(in_use, new_second, second_moment)
    new_norm, new_norm_first, new_norm_second = adam_update(
        norm_params, norm_first, norm_second, norm_total, NORM_RATE
    )
    return (
        loss_total,
        token_grad,
        new_master,
        new_first,
        new_second,
        new_master.astype(jnp.bfloat16),
        new_norm,
        new_norm_first,
        new_norm_second,
    )


def solution(mesh):
    owners, model_parts = mesh.devices.shape
    work_mesh = Mesh(mesh.devices.reshape(owners // 2, 2, model_parts // 2, 2), AXES)
    dp, mp = ("g", "c"), ("zp", "a")
    in_specs = (
        P(AXES, None),
        P(dp, None),
        P(dp, None),
        P(),
        P(dp, None, mp),
        P(dp, None, mp),
        P(dp, None, mp),
        P(),
        P(),
        P(),
    )
    out_specs = (
        P(),
        P(AXES, None),
        P(dp, None, mp),
        P(dp, None, mp),
        P(dp, None, mp),
        P(dp, None, mp),
        P(),
        P(),
        P(),
    )
    return jax.shard_map(
        per_device, mesh=work_mesh, in_specs=in_specs, out_specs=out_specs, check_vma=False
    )
```

```python
import functools

import jax
import jax.numpy as jnp
from jax import lax
from jax.experimental import pallas as pl
from jax.experimental.pallas import tpu as pltpu
from jax.sharding import Mesh
from jax.sharding import PartitionSpec as P

HEAD_DIM = 64
LAYERS = 2
QRY_DEV = 4
OWN_MAX = 2
STEP = 7
SEGS = 9
MATS = 8


BETA_ONE = 0.9
BETA_TWO = 0.999
LEARN_RATE = 0.02
NORM_RATE = 0.4
WEIGHT_DECAY = 0.5
ADAM_EPSILON = 1e-08
NORM_EPSILON = 1e-05
SOFTMAX_DIVISOR = 0.01
EXACT_ARITHMETIC = lax.Precision.HIGHEST


def segment_layout(seg_row, seg_count):
    length = seg_row.shape[0]
    place_ids = jnp.arange(length, dtype=jnp.int32)
    member = seg_row[:, None] == jnp.arange(seg_count, dtype=jnp.int32)[None, :]
    starts = jnp.min(jnp.where(member, place_ids[:, None], length), axis=0)
    counts = jnp.sum(member.astype(jnp.int32), axis=0)
    positions = place_ids - jnp.sum(jnp.where(member, starts[None, :], 0), axis=1)
    return (member, positions, counts)


def rope_tables(positions, head_dim):
    half_dim = head_dim // 2
    inverse = 1000.0 ** (-(jnp.arange(half_dim, dtype=jnp.float32) * 2.0 / head_dim))
    angles = positions.astype(jnp.float32)[:, None] * inverse[None, :]
    cosine = jnp.concatenate([jnp.cos(angles), jnp.cos(angles)], axis=1)
    sine_table = jnp.concatenate([jnp.sin(angles), jnp.sin(angles)], axis=1)
    return (cosine, sine_table)


def adam_update(weight, first_state, second_state, gradient, step_rate):
    first_new = BETA_ONE * first_state + (1.0 - BETA_ONE) * gradient
    second_new = BETA_TWO * second_state + (1.0 - BETA_TWO) * gradient * gradient
    first_hat = first_new / (1.0 - BETA_ONE**STEP)
    second_hat = second_new / (1.0 - BETA_TWO**STEP)
    weight_new = weight - step_rate * (
        first_hat / (jnp.sqrt(second_hat) + ADAM_EPSILON) + WEIGHT_DECAY * weight
    )
    return (weight_new, first_new, second_new)


def spread_map(heads):
    width = heads * HEAD_DIM
    half = HEAD_DIM // 2
    row = jnp.arange(3 * width, dtype=jnp.int32)[:, None]
    column = jnp.arange(6 * width, dtype=jnp.int32)[None, :]
    kind = column // (2 * width)
    head = column % (2 * width) // (2 * HEAD_DIM)
    lane = column % (2 * HEAD_DIM)
    base = kind * width + head * HEAD_DIM
    within = lane % HEAD_DIM
    plain = (row == base + within) & (lane < HEAD_DIM)
    turned = (lane >= HEAD_DIM) & (kind < 2)
    minus = turned & (within < half) & (row == base + within + half)
    plus = turned & (within >= half) & (row == base + within - half)
    return (plain.astype(jnp.float32) + plus - minus.astype(jnp.float32)).astype(jnp.bfloat16)


def unspread_map(heads):
    width = heads * HEAD_DIM
    half = HEAD_DIM // 2
    row = jnp.arange(4 * width, dtype=jnp.int32)[:, None]
    column = jnp.arange(2 * width, dtype=jnp.int32)[None, :]
    base = (column // HEAD_DIM) * 2 * HEAD_DIM
    within = column % HEAD_DIM
    plain = (row == base + within).astype(jnp.float32)
    plus = ((within < half) & (row == base + within + half)).astype(jnp.float32)
    minus = ((within >= half) & (row == base + within - half)).astype(jnp.float32)
    return jnp.stack([plain, plus - minus]).astype(jnp.bfloat16)


def flipped(left_side, right_side):
    return lax.dot_general(
        left_side, right_side, (((1,), (1,)), ((), ())), preferred_element_type=jnp.float32
    )


def straight(left_side, right_side):
    return jnp.dot(left_side, right_side, preferred_element_type=jnp.float32)


def over_rows(left_side, right_side):
    return lax.dot_general(
        left_side, right_side, (((0,), (0,)), ((), ())), preferred_element_type=jnp.float32
    )


def call(
    body, outputs, operands, scratch=(), mebibytes=16, blocked=False, near=(), far_out=(), name=None
):
    out_shape = tuple(
        pltpu.HBM(shape, dtype) if place in far_out else jax.ShapeDtypeStruct(shape, dtype)
        for place, (shape, dtype) in enumerate(outputs)
    )
    specs = {}
    if blocked:

        def whole(shape):
            zeros = (0,) * len(shape)
            return pl.BlockSpec(shape, lambda step: zeros, pipeline_mode=pl.Buffered(1))

        specs = {
            "grid": (1,),
            "in_specs": [whole(value.shape) for value in operands],
            "out_specs": tuple(whole(shape) for shape, _ in outputs),
        }
        operands = [
            value if place in near else pltpu.with_memory_space_constraint(value, pltpu.HBM)
            for place, value in enumerate(operands)
        ]
    return pl.pallas_call(
        body,
        out_shape=out_shape,
        scratch_shapes=list(scratch),
        compiler_params=pltpu.CompilerParams(vmem_limit_bytes=mebibytes * 2**20),
        cost_estimate=pl.CostEstimate(flops=10**6, bytes_accessed=10**5, transcendentals=0),
        name=name,
        **specs,
    )(*operands)


def attend_block(
    heads, chunk, rows, query_ref, key_ref, value_ref, seg_col_ref, seg_row_ref
):
    pad = 2 * HEAD_DIM
    span = slice(chunk * rows, (chunk + 1) * rows)
    bias = jnp.where(seg_col_ref[span, :] == seg_row_ref[...], 0.0, -1e30)
    lanes = lax.broadcasted_iota(jnp.int32, (rows, pad), 1)
    totals_all = jnp.zeros((rows, pad), jnp.float32)
    pieces = []
    for head in range(heads):
        cols = slice(head * pad, (head + 1) * pad)
        scores = flipped(query_ref[span, cols], key_ref[:, cols]) + bias
        row_top = jnp.max(scores, axis=-1, keepdims=True)
        weights = jnp.exp(scores - row_top)
        totals = jnp.sum(weights, axis=-1, keepdims=True)
        probs = (weights * (1.0 / totals)).astype(jnp.bfloat16)
        context = straight(probs, value_ref[:, cols])
        pieces.append(context[:, :HEAD_DIM].astype(jnp.bfloat16))
        totals_all = jnp.where(lanes == head, row_top + jnp.log(totals), totals_all)
    return (jnp.concatenate(pieces, axis=1), totals_all)


def attend_first_kernel(heads, *refs):
    chunk_refs, refs = refs[:4], refs[4:]
    weight_ref, map_ref, table_ref, seg_col_ref, seg_row_ref = refs[:5]
    query_ref, key_ref, value_ref, context_ref, total_ref, keep_ref, send_ref = refs[5:]
    width = heads * HEAD_DIM
    pad = 2 * HEAD_DIM
    rows = chunk_refs[0].shape[0]
    weights = straight(weight_ref[:, : 3 * width], map_ref[...]).astype(jnp.bfloat16)
    for chunk in range(4):
        span = slice(chunk * rows, (chunk + 1) * rows)
        projected = straight(chunk_refs[chunk][...], weights)
        table = table_ref[span, :]
        for head in range(heads):
            for base, ref, scale in ((0, query_ref, 0.0625), (heads * pad, key_ref, 1.0)):
                lanes = slice(base + head * pad, base + (head + 1) * pad)
                turned = projected[:, lanes] * table
                turned = turned + pltpu.roll(turned, HEAD_DIM, 1)
                ref[span, head * pad : (head + 1) * pad] = (turned * scale).astype(jnp.bfloat16)
        value_ref[span, :] = projected[:, 2 * heads * pad :].astype(jnp.bfloat16)
    out_weights = weight_ref[:, 3 * width :]
    for place, out_ref in enumerate((keep_ref, send_ref)):
        span = slice(place * rows, (place + 1) * rows)
        context, totals = attend_block(
            heads, place, rows, query_ref, key_ref, value_ref, seg_col_ref, seg_row_ref
        )
        context_ref[span, :] = context
        total_ref[span, :] = totals
        out_ref[...] = flipped(context, out_weights).astype(out_ref.dtype)


def attend_second_kernel(heads, *refs):
    weight_ref, seg_col_ref, seg_row_ref, query_ref, key_ref, value_ref = refs[:6]
    context_ref, total_ref, keep_ref, send_ref = refs[6:]
    rows = keep_ref.shape[0]
    out_weights = weight_ref[:, 3 * heads * HEAD_DIM :]
    for place, out_ref in enumerate((keep_ref, send_ref)):
        span = slice(place * rows, (place + 1) * rows)
        context, totals = attend_block(
            heads, 2 + place, rows, query_ref, key_ref, value_ref, seg_col_ref, seg_row_ref
        )
        context_ref[span, :] = context
        total_ref[span, :] = totals
        out_ref[...] = flipped(context, out_weights).astype(out_ref.dtype)


def attend_first(chunks, attn_block, mapping, table, seg_col, seg_row):
    width = attn_block.shape[0]
    part = attn_block.shape[1] // 4
    rows = chunks[0].shape[0]
    length = 4 * rows
    return call(
        functools.partial(attend_first_kernel, part // HEAD_DIM),
        [((length, 2 * part), jnp.bfloat16)] * 3
        + [
            ((2 * rows, part), jnp.bfloat16),
            ((2 * rows, 2 * HEAD_DIM), jnp.float32),
            ((rows, width), jnp.float32),
            ((rows, width), jnp.bfloat16),
        ],
        (*chunks, attn_block, mapping, table, seg_col, seg_row),
        mebibytes=28,
        blocked=True,
        near=(0, 1, 2, 3),
        name="attend_first",
    )


def attend_second(attn_block, seg_col, seg_row, query, key, value):
    width = attn_block.shape[0]
    part = attn_block.shape[1] // 4
    rows = query.shape[0] // 4
    return call(
        functools.partial(attend_second_kernel, part // HEAD_DIM),
        [
            ((2 * rows, part), jnp.bfloat16),
            ((2 * rows, 2 * HEAD_DIM), jnp.float32),
            ((rows, width), jnp.float32),
            ((rows, width), jnp.bfloat16),
        ],
        (attn_block, seg_col, seg_row, query, key, value),
        mebibytes=28,
        name="attend_second",
    )


def attend_back_kernel(heads, *refs):
    chunk_refs, refs = refs[:4], refs[4:]
    weight_ref, map_ref, cos_ref, sin_ref, seg_col_ref, seg_row_ref = refs[:6]
    query_ref, key_ref, value_ref, even_total_ref, odd_total_ref = refs[6:11]
    projected_ref, *out_refs = refs[11:16]
    grad_query, grad_key, grad_value = refs[16:]
    width = heads * HEAD_DIM
    pad = 2 * HEAD_DIM
    rows = chunk_refs[0].shape[0]
    out_weights = weight_ref[:, 3 * width :]
    empty = jnp.zeros((out_weights.shape[0], HEAD_DIM), jnp.bfloat16)
    wide = []
    for head in range(heads):
        wide += [out_weights[:, head * HEAD_DIM : (head + 1) * HEAD_DIM], empty]
    wide = jnp.concatenate(wide, axis=1)
    for chunk in range(4):
        span = slice(chunk * rows, (chunk + 1) * rows)
        grads_all = straight(chunk_refs[chunk][...], wide).astype(jnp.bfloat16)
        total_ref = even_total_ref if chunk < 2 else odd_total_ref
        total_span = slice(chunk % 2 * rows, (chunk % 2 + 1) * rows)
        bias = jnp.where(seg_col_ref[span, :] == seg_row_ref[...], 0.0, -1e30)
        for head in range(heads):
            cols = slice(head * pad, (head + 1) * pad)
            query = query_ref[span, cols]
            key = key_ref[:, cols]
            grads = grads_all[:, cols]
            scores = flipped(query, key) + bias
            probs = jnp.exp(scores - total_ref[total_span, head : head + 1])
            grad_probs = flipped(grads, value_ref[:, cols])
            inner = jnp.sum(probs * grad_probs, axis=-1, keepdims=True)
            grad_scores = (probs * (grad_probs - inner)).astype(jnp.bfloat16)
            grad_query[span, cols] = (straight(grad_scores, key) * 0.125).astype(jnp.bfloat16)
            key_part = straight(query.T, grad_scores)
            value_part = straight(grads.T, probs.astype(jnp.bfloat16))
            if chunk == 0:
                grad_key[cols, :] = key_part
                grad_value[cols, :] = value_part
            else:
                grad_key[cols, :] += key_part
                grad_value[cols, :] += value_part
    for chunk, out_ref in enumerate(out_refs):
        span = slice(chunk * rows, (chunk + 1) * rows)
        grad_k = (grad_key[:, span] * 2.0).astype(jnp.bfloat16).T
        grad_v = grad_value[:, span].astype(jnp.bfloat16).T
        both = jnp.concatenate([grad_query[span, :], grad_k], axis=1)
        plain = straight(both, map_ref[0])
        turned = straight(both, map_ref[1])
        cosine = jnp.concatenate([cos_ref[span, :]] * heads, axis=1)
        sine = jnp.concatenate([sin_ref[span, :]] * heads, axis=1)
        turned = (plain * cosine + turned * sine).astype(jnp.bfloat16)
        grad_v = [grad_v[:, head * pad : head * pad + HEAD_DIM] for head in range(heads)]
        projected = jnp.concatenate([turned, *grad_v], axis=1)
        projected_ref[span, :] = projected
        out_ref[...] = flipped(projected, weight_ref[:, : 3 * width]).astype(out_ref.dtype)


def attend_back(chunks, attn_block, mapping, cosine, sine, seg_col, seg_row, kept):
    width = attn_block.shape[0]
    part = attn_block.shape[1] // 4
    rows = chunks[0].shape[0]
    length = 4 * rows
    return call(
        functools.partial(attend_back_kernel, part // HEAD_DIM),
        [((length, 3 * part), jnp.bfloat16)]
        + [((rows, width), jnp.float32), ((rows, width), jnp.bfloat16)] * 2,
        (*chunks, attn_block, mapping, cosine, sine, seg_col, seg_row, *kept),
        mebibytes=28,
        scratch=[
            pltpu.VMEM((length, 2 * part), jnp.bfloat16),
            pltpu.VMEM((2 * part, length), jnp.float32),
            pltpu.VMEM((2 * part, length), jnp.float32),
        ],
        name="attend_back",
    )


def units_kernel(*refs):
    chunk_refs, (weight_ref, keep_ref, send_ref) = refs[:2], refs[2:]
    units = weight_ref.shape[1] // 3
    for chunk_ref, out_ref in zip(chunk_refs, (keep_ref, send_ref)):
        tokens = chunk_ref[...]
        gate = straight(tokens, weight_ref[:, :units])
        up = straight(tokens, weight_ref[:, units : 2 * units])
        hidden = (gate / (1.0 + jnp.exp(-gate)) * up).astype(jnp.bfloat16)
        out_ref[...] = flipped(hidden, weight_ref[:, 2 * units :]).astype(out_ref.dtype)


def hidden_units(chunks, weights):
    rows, width = chunks[0].shape
    return call(
        units_kernel,
        [((rows, width), jnp.float32), ((rows, width), jnp.bfloat16)],
        (*chunks, weights),
        name="hidden_units",
    )


def units_back_kernel(*refs):
    token_refs, chunk_refs, weight_ref = refs[:2], refs[2:4], refs[4]
    grad_ref, hidden_ref, keep_ref, send_ref = refs[5:]
    rows, width = chunk_refs[0].shape
    units = weight_ref.shape[1] // 3
    for place, out_ref in enumerate((keep_ref, send_ref)):
        span = slice(place * rows, (place + 1) * rows)
        tokens = token_refs[place][...]
        gate = straight(tokens, weight_ref[:, :units])
        up = straight(tokens, weight_ref[:, units : 2 * units])
        grad_hidden = straight(chunk_refs[place][...], weight_ref[:, 2 * units :])
        share = 1.0 / (1.0 + jnp.exp(-gate))
        silu = gate * share
        hidden_ref[span, :] = (silu * up).astype(jnp.bfloat16)
        grad_up = (grad_hidden * silu).astype(jnp.bfloat16)
        slope = share + silu * (1.0 - share)
        grad_gate = (grad_hidden * up * slope).astype(jnp.bfloat16)
        grad_ref[span, :units] = grad_gate
        grad_ref[span, units:] = grad_up
        result = flipped(grad_gate, weight_ref[:, :units])
        result = result + flipped(grad_up, weight_ref[:, units : 2 * units])
        out_ref[...] = result.astype(out_ref.dtype)


def units_back(tokens, chunks, weights):
    rows, width = chunks[0].shape
    units = weights.shape[1] // 3
    return call(
        units_back_kernel,
        [
            ((2 * rows, 2 * units), jnp.bfloat16),
            ((2 * rows, units), jnp.bfloat16),
            ((rows, width), jnp.float32),
            ((rows, width), jnp.bfloat16),
        ],
        (*tokens, *chunks, weights),
        mebibytes=24,
        name="units_back",
    )


def units_weights_kernel(*refs):
    token_refs, grad_refs, refs = refs[:4], refs[4:8], refs[8:]
    even_pair_ref, odd_pair_ref, even_hidden_ref, odd_hidden_ref, out_ref = refs
    rows, width = token_refs[0].shape
    units = even_hidden_ref.shape[1]
    for tile in range(0, width, 256):
        cols = slice(tile, tile + 256)
        pair, down = 0.0, 0.0
        for chunk in range(4):
            span = slice(chunk % 2 * rows, (chunk % 2 + 1) * rows)
            pair_ref = even_pair_ref if chunk < 2 else odd_pair_ref
            hidden_ref = even_hidden_ref if chunk < 2 else odd_hidden_ref
            pair = pair + over_rows(token_refs[chunk][:, cols], pair_ref[span, :])
            down = down + over_rows(grad_refs[chunk][:, cols], hidden_ref[span, :])
        out_ref[cols, : 2 * units] = pair.astype(jnp.bfloat16)
        out_ref[cols, 2 * units :] = down.astype(jnp.bfloat16)


def units_weights(tokens, grads, pairs, hidden):
    rows, width = tokens[0].shape
    units = hidden[0].shape[1]
    return call(
        units_weights_kernel,
        [((width, 3 * units), jnp.bfloat16)],
        (*tokens, *grads, *pairs, *hidden),
        blocked=True,
        near=tuple(range(12)),
        far_out=(0,),
        name="units_weights",
    )[0]


def attend_weights_kernel(*refs):
    token_refs, grad_refs, refs = refs[:4], refs[4:8], refs[8:]
    projected_ref, even_context_ref, odd_context_ref, out_ref = refs
    rows, width = token_refs[0].shape
    for tile in range(0, width, 256):
        cols = slice(tile, tile + 256)
        left, right = 0.0, 0.0
        for chunk in range(4):
            span = slice(chunk % 2 * rows, (chunk % 2 + 1) * rows)
            context_ref = even_context_ref if chunk < 2 else odd_context_ref
            projected = projected_ref[chunk * rows : (chunk + 1) * rows, :]
            left = left + over_rows(token_refs[chunk][:, cols], projected)
            right = right + over_rows(grad_refs[chunk][:, cols], context_ref[span, :])
        both = jnp.concatenate([left, right], axis=1)
        out_ref[cols, :] = both.astype(jnp.bfloat16)


def attend_weights(tokens, grads, projected, context):
    rows, width = tokens[0].shape
    part = context[0].shape[1]
    return call(
        attend_weights_kernel,
        [((width, 4 * part), jnp.bfloat16)],
        (*tokens, *grads, projected, *context),
        blocked=True,
        near=tuple(range(11)),
        far_out=(0,),
        name="attend_weights",
    )[0]


def norm_kernel(*refs):
    base_ref, own_ref, near_ref, norm_ref, residual_ref, normed_ref, low_ref = refs
    residual = base_ref[...] + own_ref[...] + near_ref[...].astype(jnp.float32)
    residual_ref[...] = residual
    centered = residual - jnp.mean(residual, axis=-1, keepdims=True)
    variance = jnp.mean(centered * centered, axis=-1, keepdims=True)
    normed = centered * lax.rsqrt(variance + NORM_EPSILON) * norm_ref[0:1, :] + norm_ref[1:2, :]
    normed_ref[...] = normed
    low_ref[...] = normed.astype(jnp.bfloat16)


def add_and_norm(base, own, near, norm_pair):
    shape = base.shape
    return call(
        norm_kernel,
        [(shape, jnp.float32), (shape, jnp.float32), (shape, jnp.bfloat16)],
        (base, own, near, norm_pair),
        blocked=True,
        near=(1, 2),
        far_out=(0, 1),
        name="add_and_norm",
    )


def norm_back_rows(grad, residual, gain):
    centered = residual - jnp.mean(residual, axis=-1, keepdims=True)
    variance = jnp.mean(centered * centered, axis=-1, keepdims=True)
    inverse = lax.rsqrt(variance + NORM_EPSILON)
    scaled = centered * inverse
    wide = grad * gain
    inner = jnp.mean(wide * scaled, axis=-1, keepdims=True)
    result = inverse * (wide - jnp.mean(wide, axis=-1, keepdims=True) - scaled * inner)
    gain_grad = jnp.sum(grad * scaled, axis=0, keepdims=True)
    return (result, jnp.concatenate([gain_grad, jnp.sum(grad, axis=0, keepdims=True)], axis=0))


def norm_back_kernel(*refs):
    norm_ref = refs[8]
    for chunk in range(2):
        base_ref, own_ref, near_ref, residual_ref = refs[4 * chunk : 4 * chunk + 4]
        out_ref, low_ref, params_ref = refs[9 + 3 * chunk : 12 + 3 * chunk]
        grad = base_ref[...] + own_ref[...] + near_ref[...].astype(jnp.float32)
        result, params = norm_back_rows(grad, residual_ref[...], norm_ref[0:1, :])
        out_ref[...] = result
        low_ref[...] = result.astype(jnp.bfloat16)
        params_ref[...] = params


def norm_back(bases, sums, nears, residuals, norm_pair):
    shape = residuals[0].shape
    chunk_out = [(shape, jnp.float32), (shape, jnp.bfloat16), ((2, shape[1]), jnp.float32)]
    operands = [part for parts in zip(bases, sums, nears, residuals) for part in parts]
    outputs = call(
        norm_back_kernel,
        chunk_out * 2,
        (*operands, norm_pair),
        blocked=True,
        near=(1, 2, 5, 6),
        far_out=(0, 2, 3, 5),
        name="norm_back",
    )
    return tuple(zip(outputs[:3], outputs[3:]))


def embed_kernel(sum_ref, near_ref, length_ref, target_ref, total_ref, out_ref):
    total = sum_ref[...] + near_ref[...]
    total_ref[...] = total
    pooled = total / length_ref[...]
    embeds = pooled * lax.rsqrt(jnp.sum(pooled * pooled, axis=1, keepdims=True) + 1e-06)
    out_ref[...] = jnp.concatenate([embeds, target_ref[...]], axis=1).astype(jnp.bfloat16)


def embed(pool_part, near_part, lengths, targets):
    rows, width = pool_part.shape
    return call(
        embed_kernel,
        [
            ((rows, width), jnp.float32),
            ((rows, width + targets.shape[1]), jnp.bfloat16),
        ],
        (pool_part, near_part, lengths, targets),
        blocked=True,
        far_out=(),
        name="embed",
    )


def pool_kernel(even_ref, odd_ref, member_ref, out_ref):
    rows = even_ref.shape[0]
    total = 0.0
    for chunk, hidden_ref in enumerate((even_ref, odd_ref)):
        member = member_ref[chunk * rows : (chunk + 1) * rows, :]
        total = total + exact(member.T, hidden_ref[...])
    out_ref[...] = total


def pool(hidden, member):
    return call(
        pool_kernel,
        [((member.shape[1], hidden[0].shape[1]), jnp.float32)],
        (*hidden, member),
        blocked=True,
        near=(0, 1),
        name="pool",
    )[0]


def loss_kernel(*refs):
    every_ref, sum_ref, length_ref, member_ref, group_ref, *residual_refs, norm_ref = refs[:8]
    loss_ref, *out_refs = refs[8:]
    width = sum_ref.shape[1]
    rows = SEGS - 1
    docs = rows - QRY_DEV
    total = every_ref.shape[0]
    vectors = every_ref[:, :width]
    targets = every_ref[:, width : width + 1].astype(jnp.float32)
    scores = flipped(vectors, vectors) / SOFTMAX_DIVISOR
    row = lax.broadcasted_iota(jnp.int32, (total, total), 0)
    column = lax.broadcasted_iota(jnp.int32, (total, total), 1)
    place = column % rows
    is_doc = place >= QRY_DEV
    doc = column // rows * docs + place - QRY_DEV
    is_query = row % rows < QRY_DEV
    hit = is_doc & (doc.astype(jnp.float32) == targets)
    masked = jnp.where(is_doc, scores, -1e30)
    row_top = jnp.max(masked, axis=1, keepdims=True)
    log_totals = row_top + jnp.log(jnp.sum(jnp.exp(masked - row_top), axis=1, keepdims=True))
    chosen = jnp.sum(jnp.where(hit, scores, 0.0), axis=1, keepdims=True)
    losses = jnp.where(is_query[:, :1], log_totals - chosen, 0.0)
    loss_ref[...] = jnp.sum(losses, axis=0, keepdims=True)
    logits = (jnp.exp(masked - log_totals) - hit.astype(jnp.float32)) / SOFTMAX_DIVISOR
    logits = jnp.where(is_query & is_doc, logits, 0.0)
    wide = vectors.astype(jnp.float32)
    embed_grads = exact(logits, wide) + exact(logits.T, wide)
    mine = lax.broadcasted_iota(jnp.int32, (rows, total), 1) - group_ref[...] * rows
    mine = (mine == lax.broadcasted_iota(jnp.int32, (rows, total), 0)).astype(jnp.float32)
    embed_grads = exact(mine, embed_grads)
    pooled = sum_ref[...] / length_ref[...]
    inverse = lax.rsqrt(jnp.sum(pooled * pooled, axis=1, keepdims=True) + 1e-06)
    inner = jnp.sum(embed_grads * pooled, axis=1, keepdims=True)
    pooled_grads = embed_grads * inverse - pooled * (inverse * inverse * inverse * inner)
    pooled_grads = pooled_grads / length_ref[...]
    chunk_rows = residual_refs[0].shape[0]
    for chunk, residual_ref in enumerate(residual_refs):
        member = member_ref[chunk * chunk_rows : (chunk + 1) * chunk_rows, :]
        grad = exact(member, pooled_grads)
        result, params = norm_back_rows(grad, residual_ref[...], norm_ref[0:1, :])
        out_ref, low_ref, params_ref = out_refs[3 * chunk : 3 * chunk + 3]
        out_ref[...] = result
        low_ref[...] = result.astype(jnp.bfloat16)
        params_ref[...] = params


def exact(left_side, right_side):
    return lax.dot_general(
        left_side,
        right_side,
        (((1,), (0,)), ((), ())),
        precision=EXACT_ARITHMETIC,
        preferred_element_type=jnp.float32,
    )


def loss_and_back(every, pooled_sum, lengths, member, group, residual, norm_pair):
    shape = residual[0].shape
    chunk_out = [
        (shape, jnp.float32),
        (shape, jnp.bfloat16),
        ((2, shape[1]), jnp.float32),
    ]
    loss, *outputs = call(
        loss_kernel,
        [((1, 1), jnp.float32), *chunk_out, *chunk_out],
        (every, pooled_sum, lengths, member, group, *residual, norm_pair),
        blocked=True,
        far_out=(0, 1, 3, 4, 6),
        name="loss_and_back",
    )
    return (loss[0, 0], *zip(outputs[:3], outputs[3:]))


AXES = ("g", "c", "zp", "a")


def hop(value, move):
    columns = lax.axis_size("g")
    pairs = []
    for column in range(columns):
        for core in range(2):
            for z in range(4):
                to_column, to_core, to_z = move(column, core, z)
                pairs.append(((column * 2 + core) * 4 + z, (to_column * 2 + to_core) * 4 + to_z))
    return lax.ppermute(value, AXES, pairs)


def swap_core(value):
    return hop(value, lambda g, c, z: (g, 1 - c, z))


def swap_near(value):
    return hop(value, lambda g, c, z: (g, c, z ^ 1))


def swap_far(value):
    return hop(value, lambda g, c, z: (g, c, z ^ 2))


def turn(value):
    return hop(value, lambda g, c, z: (g, z // 2, 2 * c + z % 2))


def first_rows(tokens):
    own = turn(tokens)
    sibling = hop(tokens, lambda g, c, z: (g, 1 - z // 2, 2 * c + z % 2))
    near = hop(tokens, lambda g, c, z: (g, z // 2, 2 * c + (z % 2 ^ 1)))
    across = hop(tokens, lambda g, c, z: (g, 1 - z // 2, 2 * c + (z % 2 ^ 1)))
    even = lax.axis_index("a") == 0
    return (
        jnp.where(even, own, near),
        jnp.where(even, sibling, across),
        jnp.where(even, near, own),
        jnp.where(even, across, sibling),
    )


def share(low):
    return (low[0], swap_core(low[0]), low[1], swap_core(low[1]))


def core_sum(keep, send):
    total = keep + swap_core(send).astype(jnp.float32)
    return (total, total.astype(jnp.bfloat16))


def core_sum_at_once(keep, send):
    both = lax.all_gather(send, "c", axis=0)
    other = jnp.where(lax.axis_index("c") == 0, both[1], both[0])
    total = keep + other.astype(jnp.float32)
    return (total, total.astype(jnp.bfloat16))


def after(value, *others):
    return lax.optimization_barrier((value, *others))[0]


def swap_x(value):
    return hop(value, lambda g, c, z: (g ^ 1, c, z))


def swap_y(value):
    return hop(value, lambda g, c, z: (g ^ 2, c, z))


def ordered(bit, mine, other, axis):
    low = jnp.where(bit == 0, mine, other)
    return jnp.stack([low, jnp.where(bit == 0, other, mine)], axis=axis)


def to_working_block(piece):
    core = lax.axis_index("c")
    first = hop(piece, lambda g, c, z: (g, 0, z) if c == 1 else (g, 1, z ^ 2))
    second = hop(piece, lambda g, c, z: (g, 1, z ^ 2) if c == 1 else (g, 0, z))
    return (jnp.where(core == 0, piece, first), jnp.where(core == 0, first, second))


def from_working_block(upper, lower):
    core = lax.axis_index("c")
    first = hop(
        jnp.where(core == 0, lower, upper),
        lambda g, c, z: (g, 1, z) if c == 0 else (g, 0, z ^ 2),
    )
    second = hop(lower, lambda g, c, z: (g, 1, z ^ 2) if c == 1 else (g, 0, z))
    mine = jnp.where(core == 0, upper, second).astype(jnp.float32)
    return mine + first.astype(jnp.float32)


def gather_rows_of(upper, lower):
    return lax.all_gather(jnp.concatenate([upper, lower], axis=0), "g", axis=0, tiled=True)


def gather_half(upper, lower):
    if lax.axis_size("g") != 4:
        return (upper, lower)
    column = lax.axis_index("g")
    return (
        ordered(column % 2, upper, swap_x(upper), 0),
        ordered(column // 2, lower, swap_y(lower), 0),
    )


def gather_rest(upper, lower):
    if lax.axis_size("g") != 4:
        return gather_rows_of(upper, lower)
    column = lax.axis_index("g")
    upper_all = ordered(column // 2, upper, swap_y(upper), 0)
    lower_all = ordered(column % 2, lower, swap_x(lower), 1)
    return jnp.stack([upper_all, lower_all], axis=2).reshape(-1, upper.shape[2])


def scatter_rows_of(partial):
    rows = lax.psum_scatter(partial, "g", scatter_dimension=0, tiled=True)
    half = rows.shape[0] // 2
    return (rows[:half], rows[half:])


def split_halves(values, bit, axis):
    low = lax.index_in_dim(values, 0, axis, keepdims=False)
    high = lax.index_in_dim(values, 1, axis, keepdims=False)
    mine = jnp.where(bit == 0, low, high).astype(jnp.float32)
    return (mine, jnp.where(bit == 0, high, low).astype(jnp.bfloat16))


def scatter_half(partial):
    if lax.axis_size("g") != 4:
        return scatter_rows_of(partial)
    column = lax.axis_index("g")
    blocks = partial.reshape(2, 2, 2, partial.shape[0] // 8, partial.shape[1])
    upper, upper_sent = split_halves(blocks[:, :, 0], column % 2, 1)
    lower, lower_sent = split_halves(blocks[:, :, 1], column // 2, 0)
    return (
        upper + swap_x(upper_sent).astype(jnp.float32),
        lower + swap_y(lower_sent).astype(jnp.float32),
    )


def scatter_rest(upper, lower):
    if lax.axis_size("g") != 4:
        return (upper, lower)
    column = lax.axis_index("g")
    upper, upper_sent = split_halves(upper, column // 2, 0)
    lower, lower_sent = split_halves(lower, column % 2, 0)
    upper = upper + swap_y(upper_sent).astype(jnp.float32)
    lower = lower + swap_x(lower_sent).astype(jnp.float32)
    return (upper.astype(jnp.bfloat16), lower.astype(jnp.bfloat16))


def heads_forward(hidden, tokens, attn_block, norm_pair, layout, maps, tables):
    query, key, value, even_context, even_totals, keep, send = attend_first(
        tokens, attn_block, maps[0], tables[0], *layout
    )
    even, leaving = core_sum(keep, send)
    leaving, query = lax.optimization_barrier((leaving, query))
    even_near = swap_near(leaving)
    odd_context, odd_totals, keep, send = attend_second(attn_block, *layout, query, key, value)
    odd, leaving = core_sum_at_once(keep, send)
    odd_near = swap_near(leaving)
    even_results = add_and_norm(hidden[0], even, even_near, norm_pair)

    def finish(other):
        return add_and_norm(hidden[1], odd, after(odd_near, other), norm_pair)

    kept = (
        tokens,
        (query, key, value, even_totals, odd_totals),
        (even_context, odd_context),
    )
    return (even_results, finish, kept)


def units_forward(even_results, finish, unit_block, norm_pair):
    residual_one, normed, low = even_results
    even_all = (low, swap_core(low))
    keep, send = hidden_units(even_all, unit_block)
    even, leaving = core_sum_at_once(keep, send)
    residual_odd, normed_odd, low = finish(leaving)
    even_near = swap_near(leaving)
    odd_all = (low, swap_core(low))
    keep, send = hidden_units(odd_all, unit_block)
    odd, leaving = core_sum_at_once(keep, send)
    results = (
        add_and_norm(normed, even, even_near, norm_pair),
        add_and_norm(normed_odd, odd, swap_near(leaving), norm_pair),
    )
    residual, output, low = zip(*results)
    kept = ((residual_one, residual_odd), (*even_all, *odd_all), residual)
    return (output, low, kept)


def units_backward(kept, grad_two, low, unit_block, norm_pair):
    residual_one, normed_all = kept[3:5]
    grad_mlp = share(low)
    pairs, hidden, sums, nears = [], [], [], []
    for chunk in range(2):
        span = slice(2 * chunk, 2 * chunk + 2)
        pair, units, keep, send = units_back(normed_all[span], grad_mlp[span], unit_block)
        own, leaving = core_sum_at_once(keep, send)
        pairs.append(pair)
        hidden.append(units)
        sums.append(own)
        nears.append(swap_near(leaving))
    unit_grads = units_weights(normed_all, grad_mlp, pairs, hidden)
    nears, unit_grads = lax.optimization_barrier((nears, unit_grads))
    results = norm_back(grad_two, sums, nears, residual_one, norm_pair)
    return (*results, unit_grads)


def heads_backward(kept, low, attn_block, layout, maps, tables):
    tokens, heads_kept, context = kept[:3]
    grad_attn = share(low)
    grad_projected, *partial = attend_back(
        grad_attn, attn_block, maps[1], *tables[1:], *layout, heads_kept
    )
    return (partial, attend_weights(tokens, grad_attn, grad_projected, context))


def per_device(
    tokens,
    segment_ids,
    pair_doc,
    slot_of,
    master,
    first_moment,
    second_moment,
    norm_params,
    norm_first,
    norm_second,
):
    columns = lax.axis_size("g")
    owners = 2 * columns
    column = lax.axis_index("g")
    core = lax.axis_index("c")
    z_pair = lax.axis_index("zp")
    near_bit = lax.axis_index("a")
    width = master.shape[1]
    shard_rows = tokens.shape[0]
    in_place = core == z_pair
    seg_row = jnp.where(in_place, segment_ids, swap_core(segment_ids))[0]
    targets = jnp.where(in_place, pair_doc, swap_core(pair_doc))[0]
    member, positions, counts = segment_layout(seg_row, SEGS)
    even = near_bit == 0
    chunk_order = [2 * core, 2 * core ^ 2, 2 * core + 1, 2 * core + 1 ^ 2]

    def in_order(values):
        return jnp.concatenate(
            [
                lax.dynamic_slice_in_dim(values, index * shard_rows, shard_rows, 0)
                for index in chunk_order
            ],
            axis=0,
        )

    cosine, sine_table = rope_tables(in_order(positions), HEAD_DIM)
    heads = width // lax.axis_size(("zp", "a")) // HEAD_DIM
    maps = (spread_map(heads), unspread_map(heads))
    tables = (
        jnp.concatenate([cosine, sine_table], axis=1),
        jnp.concatenate([cosine, cosine], axis=1),
        jnp.concatenate([sine_table, sine_table], axis=1),
    )
    seg_local = in_order(seg_row)
    layout = (seg_local[:, None], seg_local[None, :])
    member = lax.dynamic_slice_in_dim(member, 2 * core * shard_rows, 2 * shard_rows, 0)
    member = member[:, : SEGS - 1].astype(jnp.float32)
    counted = jnp.arange(2 * shard_rows)[:, None] // shard_rows == near_bit
    own_member = jnp.where(counted, member, 0.0)
    piece_rows = width // owners

    def to_owners(blocks):
        return lax.all_to_all(blocks, ("g", "c"), split_axis=0, concat_axis=0, tiled=True)

    tokens_all = first_rows(tokens)
    outgoing = master.astype(jnp.bfloat16).reshape(OWN_MAX, owners, piece_rows, width)
    incoming = to_owners(outgoing.transpose(1, 0, 2, 3)).reshape(-1, piece_rows, width)
    lengths = counts[: SEGS - 1].astype(jnp.float32)[:, None]
    targets = jnp.pad(targets.astype(jnp.float32)[:, None], ((0, SEGS - 1 - QRY_DEV), (0, 127)))
    hidden = (tokens_all[0].astype(jnp.float32), tokens_all[2].astype(jnp.float32))
    early = (tokens_all, hidden, maps, tables, layout, lengths, targets, member, own_member)
    incoming, early = lax.optimization_barrier((incoming, early))
    tokens_all, hidden, maps, tables, layout, lengths, targets, member, own_member = early

    def piece_of(*matrices):
        return jnp.concatenate(
            [
                lax.dynamic_index_in_dim(incoming, slot_of[matrix], 0, keepdims=False)
                for matrix in matrices
            ],
            axis=1,
        )

    attn_pieces = to_working_block(piece_of(0))
    unit_pieces = to_working_block(piece_of(1, 2, 3))
    attn_block = gather_rest(*gather_half(*attn_pieces))
    unit_pieces, attn_block = lax.optimization_barrier((unit_pieces, attn_block))
    unit_block = gather_rows_of(*unit_pieces)
    kept_list, weight_list = [], []
    for layer_index in range(LAYERS):
        if layer_index > 0:
            tokens_all = share(low)
        norm_set = norm_params[layer_index]
        later = layer_index + 1 < LAYERS
        if later:
            base = 4 * (layer_index + 1)
            pieces = piece_of(base, base + 1, base + 2, base + 3)
            pieces = to_working_block(after(pieces, unit_pieces))
        weight_list.append((attn_block, unit_block))
        even_results, finish, heads_kept = heads_forward(
            hidden, tokens_all, attn_block, norm_set[:2], layout, maps, tables
        )
        if later:
            pieces, even_results = lax.optimization_barrier((pieces, even_results))
            attn_block = gather_rows_of(*[part[:, :width] for part in pieces])
        hidden, low, units_kept = units_forward(
            even_results, finish, unit_block, norm_set[2:]
        )
        if later:
            unit_pieces, low = lax.optimization_barrier(([part[:, width:] for part in pieces], low))
            unit_block = gather_rows_of(*unit_pieces)
        kept_list.append((*heads_kept, *units_kept))
    pool_part = pool(hidden, own_member)
    pool_part = pool_part + swap_core(pool_part)
    pooled_sum, sent = embed(pool_part, swap_near(pool_part), lengths, targets)
    far = swap_far(sent)
    pair = jnp.stack([jnp.where(z_pair == 0, sent, far), jnp.where(z_pair == 0, far, sent)])
    every = lax.all_gather(pair, "g", axis=0, tiled=True).reshape(-1, sent.shape[1])
    loss_total, gradient, low, second_params = loss_and_back(
        every,
        pooled_sum,
        lengths,
        member,
        (2 * column + z_pair).reshape(1, 1),
        kept_list[-1][-1],
        norm_params[LAYERS - 1, 2:],
    )
    norm_list = [None] * LAYERS
    pending = []
    for layer_index in reversed(range(LAYERS)):
        kept = kept_list[layer_index]
        attn_block, unit_block = weight_list[layer_index]
        grad_one, low, first_params, unit_grads = units_backward(
            kept, gradient, low, unit_block, norm_params[layer_index, :2]
        )
        norm_list[layer_index] = jnp.concatenate(
            [jnp.where(even, *first_params), jnp.where(even, *second_params)], axis=0
        )
        unit_pieces = scatter_rows_of(after(unit_grads, pending))
        pending, low = lax.optimization_barrier((pending, low))
        arriving = [from_working_block(*pieces) for pieces in pending]
        partial, attn_grads = heads_backward(kept, low, attn_block, layout, maps, tables)
        if layer_index > 0:
            sums, nears = [], []
            for chunk in range(2):
                own, leaving = core_sum_at_once(*partial[2 * chunk : 2 * chunk + 2])
                sums.append(own)
                nears.append(swap_near(leaving))
            nears, attn_grads = lax.optimization_barrier((nears, attn_grads))
            gradient, low, second_params = norm_back(
                grad_one,
                sums,
                nears,
                kept_list[layer_index - 1][-1],
                norm_params[layer_index - 1, 2:],
            )
            attn_pieces = scatter_rows_of(after(attn_grads, unit_pieces))
            pending = [
                tuple(
                    jnp.concatenate(halves, axis=1) for halves in zip(attn_pieces, unit_pieces)
                )
            ]
    partial, attn_grads = lax.optimization_barrier((partial, attn_grads))
    attn_halves = scatter_half(attn_grads)
    even_sum, even_low = core_sum(*partial[:2])
    odd_sum, odd_low = core_sum(*partial[2:])
    near = swap_near(jnp.where(even, odd_low, even_low))
    attn_halves, unit_pieces = lax.optimization_barrier((attn_halves, unit_pieces))
    unit_arrived = from_working_block(*unit_pieces)
    attn_arrived = from_working_block(*scatter_rest(*attn_halves))
    arrived = [attn_arrived, unit_arrived] + arriving
    arrived, near = lax.optimization_barrier((arrived, near))
    gradient = jnp.where(even, grad_one[0], grad_one[1])
    gradient = gradient + jnp.where(even, even_sum, odd_sum) + near.astype(jnp.float32)
    norm_stack = jnp.stack(norm_list).reshape(-1, width)
    gradient, norm_stack = after((gradient, norm_stack), attn_arrived)
    token_grad = turn(gradient.astype(jnp.bfloat16)).astype(jnp.float32)
    outgoing = jnp.zeros((OWN_MAX * owners, piece_rows, width), jnp.bfloat16)
    pieces = jnp.concatenate(arrived, axis=1).astype(jnp.bfloat16)
    for matrix in range(MATS):
        outgoing = lax.dynamic_update_index_in_dim(
            outgoing, pieces[:, matrix * width : (matrix + 1) * width], slot_of[matrix], 0
        )
    incoming = to_owners(outgoing.reshape(owners, OWN_MAX, piece_rows, width))
    my_grads = (
        incoming.transpose(1, 0, 2, 3).reshape(OWN_MAX, width, width).astype(jnp.float32)
    )
    slot_ids = (2 * column + core) * OWN_MAX + jnp.arange(OWN_MAX, dtype=jnp.int32)
    in_use = jnp.any(slot_of[None, :] == slot_ids[:, None], axis=1)[:, None, None]
    norm_total = norm_stack + swap_core(norm_stack)
    norm_total = norm_total + swap_near(norm_total)
    norm_total = norm_total + swap_far(norm_total)
    if columns == 4:
        norm_total = norm_total + swap_x(norm_total)
        norm_total = norm_total + swap_y(norm_total)
    else:
        norm_total = jnp.sum(lax.all_gather(norm_total, "g", axis=0), axis=0)
    norm_total = norm_total.reshape(norm_params.shape)
    new_master, new_first, new_second = adam_update(
        master, first_moment, second_moment, my_grads, LEARN_RATE
    )
    new_master = jnp.where(in_use, new_master, master)
    new_first = jnp.where(in_use, new_first, first_moment)
    new_second = jnp.where(in_use, new_second, second_moment)
    new_norm, new_norm_first, new_norm_second = adam_update(
        norm_params, norm_first, norm_second, norm_total, NORM_RATE
    )
    return (
        loss_total,
        token_grad,
        new_master,
        new_first,
        new_second,
        new_master.astype(jnp.bfloat16),
        new_norm,
        new_norm_first,
        new_norm_second,
    )


def solution(mesh):
    owners, model_parts = mesh.devices.shape
    work_mesh = Mesh(mesh.devices.reshape(owners // 2, 2, model_parts // 2, 2), AXES)
    dp, mp = ("g", "c"), ("zp", "a")
    in_specs = (
        P(AXES, None),
        P(dp, None),
        P(dp, None),
        P(),
        P(dp, None, mp),
        P(dp, None, mp),
        P(dp, None, mp),
        P(),
        P(),
        P(),
    )
    out_specs = (
        P(),
        P(AXES, None),
        P(dp, None, mp),
        P(dp, None, mp),
        P(dp, None, mp),
        P(dp, None, mp),
        P(),
        P(),
        P(),
    )
    return jax.shard_map(
        per_device, mesh=work_mesh, in_specs=in_specs, out_specs=out_specs, check_vma=False
    )
```

```python
import functools

import jax
import jax.numpy as jnp
from jax import lax
from jax.experimental import pallas as pl
from jax.experimental.pallas import tpu as pltpu
from jax.sharding import Mesh
from jax.sharding import PartitionSpec as P

HEAD_DIM = 64
LAYERS = 2
QRY_DEV = 4
OWN_MAX = 2
STEP = 7
SEGS = 9
MATS = 8


BETA_ONE = 0.9
BETA_TWO = 0.999
LEARN_RATE = 0.02
NORM_RATE = 0.4
WEIGHT_DECAY = 0.5
ADAM_EPSILON = 1e-08
NORM_EPSILON = 1e-05
SOFTMAX_DIVISOR = 0.01
EXACT_ARITHMETIC = lax.Precision.HIGHEST


def segment_layout(seg_row, seg_count):
    length = seg_row.shape[0]
    place_ids = jnp.arange(length, dtype=jnp.int32)
    member = seg_row[:, None] == jnp.arange(seg_count, dtype=jnp.int32)[None, :]
    starts = jnp.min(jnp.where(member, place_ids[:, None], length), axis=0)
    counts = jnp.sum(member.astype(jnp.int32), axis=0)
    positions = place_ids - jnp.sum(jnp.where(member, starts[None, :], 0), axis=1)
    return (member, positions, counts)


def rope_tables(positions, head_dim):
    half_dim = head_dim // 2
    inverse = 1000.0 ** (-(jnp.arange(half_dim, dtype=jnp.float32) * 2.0 / head_dim))
    angles = positions.astype(jnp.float32)[:, None] * inverse[None, :]
    cosine = jnp.concatenate([jnp.cos(angles), jnp.cos(angles)], axis=1)
    sine_table = jnp.concatenate([jnp.sin(angles), jnp.sin(angles)], axis=1)
    return (cosine, sine_table)


def adam_update(weight, first_state, second_state, gradient, step_rate):
    first_new = BETA_ONE * first_state + (1.0 - BETA_ONE) * gradient
    second_new = BETA_TWO * second_state + (1.0 - BETA_TWO) * gradient * gradient
    first_hat = first_new / (1.0 - BETA_ONE**STEP)
    second_hat = second_new / (1.0 - BETA_TWO**STEP)
    weight_new = weight - step_rate * (
        first_hat / (jnp.sqrt(second_hat) + ADAM_EPSILON) + WEIGHT_DECAY * weight
    )
    return (weight_new, first_new, second_new)


def spread_map(heads):
    width = heads * HEAD_DIM
    half = HEAD_DIM // 2
    row = jnp.arange(3 * width, dtype=jnp.int32)[:, None]
    column = jnp.arange(6 * width, dtype=jnp.int32)[None, :]
    kind = column // (2 * width)
    head = column % (2 * width) // (2 * HEAD_DIM)
    lane = column % (2 * HEAD_DIM)
    base = kind * width + head * HEAD_DIM
    within = lane % HEAD_DIM
    plain = (row == base + within) & (lane < HEAD_DIM)
    turned = (lane >= HEAD_DIM) & (kind < 2)
    minus = turned & (within < half) & (row == base + within + half)
    plus = turned & (within >= half) & (row == base + within - half)
    return (plain.astype(jnp.float32) + plus - minus.astype(jnp.float32)).astype(jnp.bfloat16)


def unspread_map(heads):
    width = heads * HEAD_DIM
    half = HEAD_DIM // 2
    row = jnp.arange(4 * width, dtype=jnp.int32)[:, None]
    column = jnp.arange(2 * width, dtype=jnp.int32)[None, :]
    base = (column // HEAD_DIM) * 2 * HEAD_DIM
    within = column % HEAD_DIM
    plain = (row == base + within).astype(jnp.float32)
    plus = ((within < half) & (row == base + within + half)).astype(jnp.float32)
    minus = ((within >= half) & (row == base + within - half)).astype(jnp.float32)
    return jnp.stack([plain, plus - minus]).astype(jnp.bfloat16)


def flipped(left_side, right_side):
    return lax.dot_general(
        left_side, right_side, (((1,), (1,)), ((), ())), preferred_element_type=jnp.float32
    )


def straight(left_side, right_side):
    return jnp.dot(left_side, right_side, preferred_element_type=jnp.float32)


def over_rows(left_side, right_side):
    return lax.dot_general(
        left_side, right_side, (((0,), (0,)), ((), ())), preferred_element_type=jnp.float32
    )


def call(
    body, outputs, operands, scratch=(), mebibytes=16, blocked=False, near=(), far_out=(), name=None,
    long=False,
):
    out_shape = tuple(
        pltpu.HBM(shape, dtype) if place in far_out else jax.ShapeDtypeStruct(shape, dtype)
        for place, (shape, dtype) in enumerate(outputs)
    )
    specs = {}
    if blocked:

        def whole(shape):
            zeros = (0,) * len(shape)
            return pl.BlockSpec(shape, lambda step: zeros, pipeline_mode=pl.Buffered(1))

        specs = {
            "grid": (1,),
            "in_specs": [whole(value.shape) for value in operands],
            "out_specs": tuple(whole(shape) for shape, _ in outputs),
        }
        operands = [
            value if place in near else pltpu.with_memory_space_constraint(value, pltpu.HBM)
            for place, value in enumerate(operands)
        ]
    return pl.pallas_call(
        body,
        out_shape=out_shape,
        scratch_shapes=list(scratch),
        compiler_params=pltpu.CompilerParams(vmem_limit_bytes=mebibytes * 2**20),
        cost_estimate=pl.CostEstimate(
            flops=4 * 10**9 if long else 10**6,
            bytes_accessed=10**7 if long else 10**5,
            transcendentals=0,
        ),
        name=name,
        **specs,
    )(*operands)


def attend_block(
    heads, chunk, rows, query_ref, key_ref, value_ref, seg_col_ref, seg_row_ref
):
    pad = 2 * HEAD_DIM
    span = slice(chunk * rows, (chunk + 1) * rows)
    bias = jnp.where(seg_col_ref[span, :] == seg_row_ref[...], 0.0, -1e30)
    lanes = lax.broadcasted_iota(jnp.int32, (rows, pad), 1)
    totals_all = jnp.zeros((rows, pad), jnp.float32)
    pieces = []
    for head in range(heads):
        cols = slice(head * pad, (head + 1) * pad)
        scores = flipped(query_ref[span, cols], key_ref[:, cols]) + bias
        row_top = jnp.max(scores, axis=-1, keepdims=True)
        weights = jnp.exp(scores - row_top)
        totals = jnp.sum(weights, axis=-1, keepdims=True)
        probs = (weights * (1.0 / totals)).astype(jnp.bfloat16)
        context = straight(probs, value_ref[:, cols])
        pieces.append(context[:, :HEAD_DIM].astype(jnp.bfloat16))
        totals_all = jnp.where(lanes == head, row_top + jnp.log(totals), totals_all)
    return (jnp.concatenate(pieces, axis=1), totals_all)


def attend_first_kernel(heads, *refs):
    chunk_refs, refs = refs[:4], refs[4:]
    weight_ref, map_ref, table_ref, seg_col_ref, seg_row_ref = refs[:5]
    query_ref, key_ref, value_ref, context_ref, total_ref, keep_ref, send_ref = refs[5:]
    width = heads * HEAD_DIM
    pad = 2 * HEAD_DIM
    rows = chunk_refs[0].shape[0]
    weights = straight(weight_ref[:, : 3 * width], map_ref[...]).astype(jnp.bfloat16)
    for chunk in range(4):
        span = slice(chunk * rows, (chunk + 1) * rows)
        projected = straight(chunk_refs[chunk][...], weights)
        table = table_ref[span, :]
        for head in range(heads):
            for base, ref, scale in ((0, query_ref, 0.0625), (heads * pad, key_ref, 1.0)):
                lanes = slice(base + head * pad, base + (head + 1) * pad)
                turned = projected[:, lanes] * table
                turned = turned + pltpu.roll(turned, HEAD_DIM, 1)
                ref[span, head * pad : (head + 1) * pad] = (turned * scale).astype(jnp.bfloat16)
        value_ref[span, :] = projected[:, 2 * heads * pad :].astype(jnp.bfloat16)
    out_weights = weight_ref[:, 3 * width :]
    for place, out_ref in enumerate((keep_ref, send_ref)):
        span = slice(place * rows, (place + 1) * rows)
        context, totals = attend_block(
            heads, place, rows, query_ref, key_ref, value_ref, seg_col_ref, seg_row_ref
        )
        context_ref[span, :] = context
        total_ref[span, :] = totals
        out_ref[...] = flipped(context, out_weights).astype(out_ref.dtype)


def attend_second_kernel(heads, *refs):
    weight_ref, seg_col_ref, seg_row_ref, query_ref, key_ref, value_ref = refs[:6]
    context_ref, total_ref, keep_ref, send_ref = refs[6:]
    rows = keep_ref.shape[0]
    out_weights = weight_ref[:, 3 * heads * HEAD_DIM :]
    for place, out_ref in enumerate((keep_ref, send_ref)):
        span = slice(place * rows, (place + 1) * rows)
        context, totals = attend_block(
            heads, 2 + place, rows, query_ref, key_ref, value_ref, seg_col_ref, seg_row_ref
        )
        context_ref[span, :] = context
        total_ref[span, :] = totals
        out_ref[...] = flipped(context, out_weights).astype(out_ref.dtype)


def attend_first(chunks, attn_block, mapping, table, seg_col, seg_row):
    width = attn_block.shape[0]
    part = attn_block.shape[1] // 4
    rows = chunks[0].shape[0]
    length = 4 * rows
    return call(
        functools.partial(attend_first_kernel, part // HEAD_DIM),
        [((length, 2 * part), jnp.bfloat16)] * 3
        + [
            ((2 * rows, part), jnp.bfloat16),
            ((2 * rows, 2 * HEAD_DIM), jnp.float32),
            ((rows, width), jnp.float32),
            ((rows, width), jnp.bfloat16),
        ],
        (*chunks, attn_block, mapping, table, seg_col, seg_row),
        mebibytes=28,
        blocked=True,
        near=(0, 1, 2, 3),
        name="attend_first",
    )


def attend_second(attn_block, seg_col, seg_row, query, key, value):
    width = attn_block.shape[0]
    part = attn_block.shape[1] // 4
    rows = query.shape[0] // 4
    return call(
        functools.partial(attend_second_kernel, part // HEAD_DIM),
        [
            ((2 * rows, part), jnp.bfloat16),
            ((2 * rows, 2 * HEAD_DIM), jnp.float32),
            ((rows, width), jnp.float32),
            ((rows, width), jnp.bfloat16),
        ],
        (attn_block, seg_col, seg_row, query, key, value),
        mebibytes=28,
        name="attend_second",
    )


def attend_back_kernel(heads, *refs):
    chunk_refs, refs = refs[:4], refs[4:]
    weight_ref, map_ref, cos_ref, sin_ref, seg_col_ref, seg_row_ref = refs[:6]
    query_ref, key_ref, value_ref, even_total_ref, odd_total_ref = refs[6:11]
    projected_ref, *out_refs = refs[11:16]
    grad_query, grad_key, grad_value = refs[16:]
    width = heads * HEAD_DIM
    pad = 2 * HEAD_DIM
    rows = chunk_refs[0].shape[0]
    out_weights = weight_ref[:, 3 * width :]
    empty = jnp.zeros((out_weights.shape[0], HEAD_DIM), jnp.bfloat16)
    wide = []
    for head in range(heads):
        wide += [out_weights[:, head * HEAD_DIM : (head + 1) * HEAD_DIM], empty]
    wide = jnp.concatenate(wide, axis=1)
    for chunk in range(4):
        span = slice(chunk * rows, (chunk + 1) * rows)
        grads_all = straight(chunk_refs[chunk][...], wide).astype(jnp.bfloat16)
        total_ref = even_total_ref if chunk < 2 else odd_total_ref
        total_span = slice(chunk % 2 * rows, (chunk % 2 + 1) * rows)
        bias = jnp.where(seg_col_ref[span, :] == seg_row_ref[...], 0.0, -1e30)
        for head in range(heads):
            cols = slice(head * pad, (head + 1) * pad)
            query = query_ref[span, cols]
            key = key_ref[:, cols]
            grads = grads_all[:, cols]
            scores = flipped(query, key) + bias
            probs = jnp.exp(scores - total_ref[total_span, head : head + 1])
            grad_probs = flipped(grads, value_ref[:, cols])
            inner = jnp.sum(probs * grad_probs, axis=-1, keepdims=True)
            grad_scores = (probs * (grad_probs - inner)).astype(jnp.bfloat16)
            grad_query[span, cols] = (straight(grad_scores, key) * 0.125).astype(jnp.bfloat16)
            key_part = straight(query.T, grad_scores)
            value_part = straight(grads.T, probs.astype(jnp.bfloat16))
            if chunk == 0:
                grad_key[cols, :] = key_part
                grad_value[cols, :] = value_part
            else:
                grad_key[cols, :] += key_part
                grad_value[cols, :] += value_part
    for chunk, out_ref in enumerate(out_refs):
        span = slice(chunk * rows, (chunk + 1) * rows)
        grad_k = (grad_key[:, span] * 2.0).astype(jnp.bfloat16).T
        grad_v = grad_value[:, span].astype(jnp.bfloat16).T
        both = jnp.concatenate([grad_query[span, :], grad_k], axis=1)
        plain = straight(both, map_ref[0])
        turned = straight(both, map_ref[1])
        cosine = jnp.concatenate([cos_ref[span, :]] * heads, axis=1)
        sine = jnp.concatenate([sin_ref[span, :]] * heads, axis=1)
        turned = (plain * cosine + turned * sine).astype(jnp.bfloat16)
        grad_v = [grad_v[:, head * pad : head * pad + HEAD_DIM] for head in range(heads)]
        projected = jnp.concatenate([turned, *grad_v], axis=1)
        projected_ref[span, :] = projected
        out_ref[...] = flipped(projected, weight_ref[:, : 3 * width]).astype(out_ref.dtype)


def attend_back(chunks, attn_block, mapping, cosine, sine, seg_col, seg_row, kept):
    width = attn_block.shape[0]
    part = attn_block.shape[1] // 4
    rows = chunks[0].shape[0]
    length = 4 * rows
    return call(
        functools.partial(attend_back_kernel, part // HEAD_DIM),
        [((length, 3 * part), jnp.bfloat16)]
        + [((rows, width), jnp.float32), ((rows, width), jnp.bfloat16)] * 2,
        (*chunks, attn_block, mapping, cosine, sine, seg_col, seg_row, *kept),
        mebibytes=28,
        scratch=[
            pltpu.VMEM((length, 2 * part), jnp.bfloat16),
            pltpu.VMEM((2 * part, length), jnp.float32),
            pltpu.VMEM((2 * part, length), jnp.float32),
        ],
        long=True,
        name="attend_back",
    )


def units_kernel(*refs):
    chunk_refs, (weight_ref, keep_ref, send_ref) = refs[:2], refs[2:]
    units = weight_ref.shape[1] // 3
    for chunk_ref, out_ref in zip(chunk_refs, (keep_ref, send_ref)):
        tokens = chunk_ref[...]
        gate = straight(tokens, weight_ref[:, :units])
        up = straight(tokens, weight_ref[:, units : 2 * units])
        hidden = (gate / (1.0 + jnp.exp(-gate)) * up).astype(jnp.bfloat16)
        out_ref[...] = flipped(hidden, weight_ref[:, 2 * units :]).astype(out_ref.dtype)


def hidden_units(chunks, weights):
    rows, width = chunks[0].shape
    return call(
        units_kernel,
        [((rows, width), jnp.float32), ((rows, width), jnp.bfloat16)],
        (*chunks, weights),
        name="hidden_units",
    )


def units_back_kernel(*refs):
    token_refs, chunk_refs, weight_ref = refs[:2], refs[2:4], refs[4]
    grad_ref, hidden_ref, keep_ref, send_ref = refs[5:]
    rows, width = chunk_refs[0].shape
    units = weight_ref.shape[1] // 3
    for place, out_ref in enumerate((keep_ref, send_ref)):
        span = slice(place * rows, (place + 1) * rows)
        tokens = token_refs[place][...]
        gate = straight(tokens, weight_ref[:, :units])
        up = straight(tokens, weight_ref[:, units : 2 * units])
        grad_hidden = straight(chunk_refs[place][...], weight_ref[:, 2 * units :])
        share = 1.0 / (1.0 + jnp.exp(-gate))
        silu = gate * share
        hidden_ref[span, :] = (silu * up).astype(jnp.bfloat16)
        grad_up = (grad_hidden * silu).astype(jnp.bfloat16)
        slope = share + silu * (1.0 - share)
        grad_gate = (grad_hidden * up * slope).astype(jnp.bfloat16)
        grad_ref[span, :units] = grad_gate
        grad_ref[span, units:] = grad_up
        result = flipped(grad_gate, weight_ref[:, :units])
        result = result + flipped(grad_up, weight_ref[:, units : 2 * units])
        out_ref[...] = result.astype(out_ref.dtype)


def units_back(tokens, chunks, weights):
    rows, width = chunks[0].shape
    units = weights.shape[1] // 3
    return call(
        units_back_kernel,
        [
            ((2 * rows, 2 * units), jnp.bfloat16),
            ((2 * rows, units), jnp.bfloat16),
            ((rows, width), jnp.float32),
            ((rows, width), jnp.bfloat16),
        ],
        (*tokens, *chunks, weights),
        mebibytes=24,
        long=True,
        name="units_back",
    )


def units_weights_kernel(*refs):
    token_refs, grad_refs, refs = refs[:4], refs[4:8], refs[8:]
    even_pair_ref, odd_pair_ref, even_hidden_ref, odd_hidden_ref, out_ref = refs
    rows, width = token_refs[0].shape
    units = even_hidden_ref.shape[1]
    for tile in range(0, width, 256):
        cols = slice(tile, tile + 256)
        pair, down = 0.0, 0.0
        for chunk in range(4):
            span = slice(chunk % 2 * rows, (chunk % 2 + 1) * rows)
            pair_ref = even_pair_ref if chunk < 2 else odd_pair_ref
            hidden_ref = even_hidden_ref if chunk < 2 else odd_hidden_ref
            pair = pair + over_rows(token_refs[chunk][:, cols], pair_ref[span, :])
            down = down + over_rows(grad_refs[chunk][:, cols], hidden_ref[span, :])
        out_ref[cols, : 2 * units] = pair.astype(jnp.bfloat16)
        out_ref[cols, 2 * units :] = down.astype(jnp.bfloat16)


def units_weights(tokens, grads, pairs, hidden):
    rows, width = tokens[0].shape
    units = hidden[0].shape[1]
    return call(
        units_weights_kernel,
        [((width, 3 * units), jnp.bfloat16)],
        (*tokens, *grads, *pairs, *hidden),
        blocked=True,
        near=tuple(range(12)),
        far_out=(0,),
        long=True,
        name="units_weights",
    )[0]


def attend_weights_kernel(*refs):
    token_refs, grad_refs, refs = refs[:4], refs[4:8], refs[8:]
    projected_ref, even_context_ref, odd_context_ref, out_ref = refs
    rows, width = token_refs[0].shape
    for tile in range(0, width, 256):
        cols = slice(tile, tile + 256)
        left, right = 0.0, 0.0
        for chunk in range(4):
            span = slice(chunk % 2 * rows, (chunk % 2 + 1) * rows)
            context_ref = even_context_ref if chunk < 2 else odd_context_ref
            projected = projected_ref[chunk * rows : (chunk + 1) * rows, :]
            left = left + over_rows(token_refs[chunk][:, cols], projected)
            right = right + over_rows(grad_refs[chunk][:, cols], context_ref[span, :])
        both = jnp.concatenate([left, right], axis=1)
        out_ref[cols, :] = both.astype(jnp.bfloat16)


def attend_weights(tokens, grads, projected, context):
    rows, width = tokens[0].shape
    part = context[0].shape[1]
    return call(
        attend_weights_kernel,
        [((width, 4 * part), jnp.bfloat16)],
        (*tokens, *grads, projected, *context),
        blocked=True,
        near=tuple(range(11)),
        far_out=(0,),
        long=True,
        name="attend_weights",
    )[0]


def norm_kernel(*refs):
    base_ref, own_ref, near_ref, norm_ref, residual_ref, normed_ref, low_ref = refs
    residual = base_ref[...] + own_ref[...] + near_ref[...].astype(jnp.float32)
    residual_ref[...] = residual
    centered = residual - jnp.mean(residual, axis=-1, keepdims=True)
    variance = jnp.mean(centered * centered, axis=-1, keepdims=True)
    normed = centered * lax.rsqrt(variance + NORM_EPSILON) * norm_ref[0:1, :] + norm_ref[1:2, :]
    normed_ref[...] = normed
    low_ref[...] = normed.astype(jnp.bfloat16)


def add_and_norm(base, own, near, norm_pair):
    shape = base.shape
    return call(
        norm_kernel,
        [(shape, jnp.float32), (shape, jnp.float32), (shape, jnp.bfloat16)],
        (base, own, near, norm_pair),
        blocked=True,
        near=(1, 2),
        far_out=(0, 1),
        name="add_and_norm",
    )


def norm_back_rows(grad, residual, gain):
    centered = residual - jnp.mean(residual, axis=-1, keepdims=True)
    variance = jnp.mean(centered * centered, axis=-1, keepdims=True)
    inverse = lax.rsqrt(variance + NORM_EPSILON)
    scaled = centered * inverse
    wide = grad * gain
    inner = jnp.mean(wide * scaled, axis=-1, keepdims=True)
    result = inverse * (wide - jnp.mean(wide, axis=-1, keepdims=True) - scaled * inner)
    gain_grad = jnp.sum(grad * scaled, axis=0, keepdims=True)
    return (result, jnp.concatenate([gain_grad, jnp.sum(grad, axis=0, keepdims=True)], axis=0))


def norm_back_kernel(*refs):
    norm_ref = refs[8]
    for chunk in range(2):
        base_ref, own_ref, near_ref, residual_ref = refs[4 * chunk : 4 * chunk + 4]
        out_ref, low_ref, params_ref = refs[9 + 3 * chunk : 12 + 3 * chunk]
        grad = base_ref[...] + own_ref[...] + near_ref[...].astype(jnp.float32)
        result, params = norm_back_rows(grad, residual_ref[...], norm_ref[0:1, :])
        out_ref[...] = result
        low_ref[...] = result.astype(jnp.bfloat16)
        params_ref[...] = params


def norm_back(bases, sums, nears, residuals, norm_pair):
    shape = residuals[0].shape
    chunk_out = [(shape, jnp.float32), (shape, jnp.bfloat16), ((2, shape[1]), jnp.float32)]
    operands = [part for parts in zip(bases, sums, nears, residuals) for part in parts]
    outputs = call(
        norm_back_kernel,
        chunk_out * 2,
        (*operands, norm_pair),
        blocked=True,
        near=(1, 2, 5, 6),
        far_out=(0, 2, 3, 5),
        long=True,
        name="norm_back",
    )
    return tuple(zip(outputs[:3], outputs[3:]))


def embed_kernel(sum_ref, near_ref, length_ref, target_ref, total_ref, out_ref):
    total = sum_ref[...] + near_ref[...]
    total_ref[...] = total
    pooled = total / length_ref[...]
    embeds = pooled * lax.rsqrt(jnp.sum(pooled * pooled, axis=1, keepdims=True) + 1e-06)
    out_ref[...] = jnp.concatenate([embeds, target_ref[...]], axis=1).astype(jnp.bfloat16)


def embed(pool_part, near_part, lengths, targets):
    rows, width = pool_part.shape
    return call(
        embed_kernel,
        [
            ((rows, width), jnp.float32),
            ((rows, width + targets.shape[1]), jnp.bfloat16),
        ],
        (pool_part, near_part, lengths, targets),
        blocked=True,
        far_out=(),
        name="embed",
    )


def pool_kernel(even_ref, odd_ref, member_ref, out_ref):
    rows = even_ref.shape[0]
    total = 0.0
    for chunk, hidden_ref in enumerate((even_ref, odd_ref)):
        member = member_ref[chunk * rows : (chunk + 1) * rows, :]
        total = total + exact(member.T, hidden_ref[...])
    out_ref[...] = total


def pool(hidden, member):
    return call(
        pool_kernel,
        [((member.shape[1], hidden[0].shape[1]), jnp.float32)],
        (*hidden, member),
        blocked=True,
        near=(0, 1),
        name="pool",
    )[0]


def loss_kernel(*refs):
    every_ref, sum_ref, length_ref, member_ref, group_ref, *residual_refs, norm_ref = refs[:8]
    loss_ref, *out_refs = refs[8:]
    width = sum_ref.shape[1]
    rows = SEGS - 1
    docs = rows - QRY_DEV
    total = every_ref.shape[0]
    vectors = every_ref[:, :width]
    targets = every_ref[:, width : width + 1].astype(jnp.float32)
    scores = flipped(vectors, vectors) / SOFTMAX_DIVISOR
    row = lax.broadcasted_iota(jnp.int32, (total, total), 0)
    column = lax.broadcasted_iota(jnp.int32, (total, total), 1)
    place = column % rows
    is_doc = place >= QRY_DEV
    doc = column // rows * docs + place - QRY_DEV
    is_query = row % rows < QRY_DEV
    hit = is_doc & (doc.astype(jnp.float32) == targets)
    masked = jnp.where(is_doc, scores, -1e30)
    row_top = jnp.max(masked, axis=1, keepdims=True)
    log_totals = row_top + jnp.log(jnp.sum(jnp.exp(masked - row_top), axis=1, keepdims=True))
    chosen = jnp.sum(jnp.where(hit, scores, 0.0), axis=1, keepdims=True)
    losses = jnp.where(is_query[:, :1], log_totals - chosen, 0.0)
    loss_ref[...] = jnp.sum(losses, axis=0, keepdims=True)
    logits = (jnp.exp(masked - log_totals) - hit.astype(jnp.float32)) / SOFTMAX_DIVISOR
    logits = jnp.where(is_query & is_doc, logits, 0.0)
    wide = vectors.astype(jnp.float32)
    embed_grads = exact(logits, wide) + exact(logits.T, wide)
    mine = lax.broadcasted_iota(jnp.int32, (rows, total), 1) - group_ref[...] * rows
    mine = (mine == lax.broadcasted_iota(jnp.int32, (rows, total), 0)).astype(jnp.float32)
    embed_grads = exact(mine, embed_grads)
    pooled = sum_ref[...] / length_ref[...]
    inverse = lax.rsqrt(jnp.sum(pooled * pooled, axis=1, keepdims=True) + 1e-06)
    inner = jnp.sum(embed_grads * pooled, axis=1, keepdims=True)
    pooled_grads = embed_grads * inverse - pooled * (inverse * inverse * inverse * inner)
    pooled_grads = pooled_grads / length_ref[...]
    chunk_rows = residual_refs[0].shape[0]
    for chunk, residual_ref in enumerate(residual_refs):
        member = member_ref[chunk * chunk_rows : (chunk + 1) * chunk_rows, :]
        grad = exact(member, pooled_grads)
        result, params = norm_back_rows(grad, residual_ref[...], norm_ref[0:1, :])
        out_ref, low_ref, params_ref = out_refs[3 * chunk : 3 * chunk + 3]
        out_ref[...] = result
        low_ref[...] = result.astype(jnp.bfloat16)
        params_ref[...] = params


def exact(left_side, right_side):
    return lax.dot_general(
        left_side,
        right_side,
        (((1,), (0,)), ((), ())),
        precision=EXACT_ARITHMETIC,
        preferred_element_type=jnp.float32,
    )


def loss_and_back(every, pooled_sum, lengths, member, group, residual, norm_pair):
    shape = residual[0].shape
    chunk_out = [
        (shape, jnp.float32),
        (shape, jnp.bfloat16),
        ((2, shape[1]), jnp.float32),
    ]
    loss, *outputs = call(
        loss_kernel,
        [((1, 1), jnp.float32), *chunk_out, *chunk_out],
        (every, pooled_sum, lengths, member, group, *residual, norm_pair),
        blocked=True,
        far_out=(0, 1, 3, 4, 6),
        long=True,
        name="loss_and_back",
    )
    return (loss[0, 0], *zip(outputs[:3], outputs[3:]))


AXES = ("g", "c", "zp", "a")


def hop(value, move):
    columns = lax.axis_size("g")
    pairs = []
    for column in range(columns):
        for core in range(2):
            for z in range(4):
                to_column, to_core, to_z = move(column, core, z)
                pairs.append(((column * 2 + core) * 4 + z, (to_column * 2 + to_core) * 4 + to_z))
    return lax.ppermute(value, AXES, pairs)


def swap_core(value):
    return hop(value, lambda g, c, z: (g, 1 - c, z))


def swap_near(value):
    return hop(value, lambda g, c, z: (g, c, z ^ 1))


def swap_far(value):
    return hop(value, lambda g, c, z: (g, c, z ^ 2))


def turn(value):
    return hop(value, lambda g, c, z: (g, z // 2, 2 * c + z % 2))


def first_rows(tokens):
    own = turn(tokens)
    sibling = hop(tokens, lambda g, c, z: (g, 1 - z // 2, 2 * c + z % 2))
    near = hop(tokens, lambda g, c, z: (g, z // 2, 2 * c + (z % 2 ^ 1)))
    across = hop(tokens, lambda g, c, z: (g, 1 - z // 2, 2 * c + (z % 2 ^ 1)))
    even = lax.axis_index("a") == 0
    return (
        jnp.where(even, own, near),
        jnp.where(even, sibling, across),
        jnp.where(even, near, own),
        jnp.where(even, across, sibling),
    )


def share(low):
    return (low[0], swap_core(low[0]), low[1], swap_core(low[1]))


def core_sum(keep, send):
    total = keep + swap_core(send).astype(jnp.float32)
    return (total, total.astype(jnp.bfloat16))


def core_sum_at_once(keep, send):
    both = lax.all_gather(send, "c", axis=0)
    other = jnp.where(lax.axis_index("c") == 0, both[1], both[0])
    total = keep + other.astype(jnp.float32)
    return (total, total.astype(jnp.bfloat16))


def after(value, *others):
    return lax.optimization_barrier((value, *others))[0]


def swap_x(value):
    return hop(value, lambda g, c, z: (g ^ 1, c, z))


def swap_y(value):
    return hop(value, lambda g, c, z: (g ^ 2, c, z))


def ordered(bit, mine, other, axis):
    low = jnp.where(bit == 0, mine, other)
    return jnp.stack([low, jnp.where(bit == 0, other, mine)], axis=axis)


def to_working_block(piece):
    core = lax.axis_index("c")
    first = hop(piece, lambda g, c, z: (g, 0, z) if c == 1 else (g, 1, z ^ 2))
    second = hop(piece, lambda g, c, z: (g, 1, z ^ 2) if c == 1 else (g, 0, z))
    return (jnp.where(core == 0, piece, first), jnp.where(core == 0, first, second))


def from_working_block(upper, lower):
    core = lax.axis_index("c")
    first = hop(
        jnp.where(core == 0, lower, upper),
        lambda g, c, z: (g, 1, z) if c == 0 else (g, 0, z ^ 2),
    )
    second = hop(lower, lambda g, c, z: (g, 1, z ^ 2) if c == 1 else (g, 0, z))
    mine = jnp.where(core == 0, upper, second).astype(jnp.float32)
    return mine + first.astype(jnp.float32)


def gather_rows_of(upper, lower):
    return lax.all_gather(jnp.concatenate([upper, lower], axis=0), "g", axis=0, tiled=True)


def gather_half(upper, lower):
    if lax.axis_size("g") != 4:
        return (upper, lower)
    column = lax.axis_index("g")
    return (
        ordered(column % 2, upper, swap_x(upper), 0),
        ordered(column // 2, lower, swap_y(lower), 0),
    )


def gather_rest(upper, lower):
    if lax.axis_size("g") != 4:
        return gather_rows_of(upper, lower)
    column = lax.axis_index("g")
    upper_all = ordered(column // 2, upper, swap_y(upper), 0)
    lower_all = ordered(column % 2, lower, swap_x(lower), 1)
    return jnp.stack([upper_all, lower_all], axis=2).reshape(-1, upper.shape[2])


def scatter_rows_of(partial):
    rows = lax.psum_scatter(partial, "g", scatter_dimension=0, tiled=True)
    half = rows.shape[0] // 2
    return (rows[:half], rows[half:])


def split_halves(values, bit, axis):
    low = lax.index_in_dim(values, 0, axis, keepdims=False)
    high = lax.index_in_dim(values, 1, axis, keepdims=False)
    mine = jnp.where(bit == 0, low, high).astype(jnp.float32)
    return (mine, jnp.where(bit == 0, high, low).astype(jnp.bfloat16))


def scatter_half(partial):
    if lax.axis_size("g") != 4:
        return scatter_rows_of(partial)
    column = lax.axis_index("g")
    blocks = partial.reshape(2, 2, 2, partial.shape[0] // 8, partial.shape[1])
    upper, upper_sent = split_halves(blocks[:, :, 0], column % 2, 1)
    lower, lower_sent = split_halves(blocks[:, :, 1], column // 2, 0)
    return (
        upper + swap_x(upper_sent).astype(jnp.float32),
        lower + swap_y(lower_sent).astype(jnp.float32),
    )


def scatter_rest(upper, lower):
    if lax.axis_size("g") != 4:
        return (upper, lower)
    column = lax.axis_index("g")
    upper, upper_sent = split_halves(upper, column // 2, 0)
    lower, lower_sent = split_halves(lower, column % 2, 0)
    upper = upper + swap_y(upper_sent).astype(jnp.float32)
    lower = lower + swap_x(lower_sent).astype(jnp.float32)
    return (upper.astype(jnp.bfloat16), lower.astype(jnp.bfloat16))


def heads_forward(hidden, tokens, attn_block, norm_pair, layout, maps, tables):
    query, key, value, even_context, even_totals, keep, send = attend_first(
        tokens, attn_block, maps[0], tables[0], *layout
    )
    even, leaving = core_sum(keep, send)
    leaving, query = lax.optimization_barrier((leaving, query))
    even_near = swap_near(leaving)
    odd_context, odd_totals, keep, send = attend_second(attn_block, *layout, query, key, value)
    odd, leaving = core_sum_at_once(keep, send)
    odd_near = swap_near(leaving)
    even_results = add_and_norm(hidden[0], even, even_near, norm_pair)

    def finish(other):
        return add_and_norm(hidden[1], odd, after(odd_near, other), norm_pair)

    kept = (
        tokens,
        (query, key, value, even_totals, odd_totals),
        (even_context, odd_context),
    )
    return (even_results, finish, kept)


def units_forward(even_results, finish, unit_block, norm_pair):
    residual_one, normed, low = even_results
    even_all = (low, swap_core(low))
    keep, send = hidden_units(even_all, unit_block)
    even, leaving = core_sum_at_once(keep, send)
    residual_odd, normed_odd, low = finish(leaving)
    even_near = swap_near(leaving)
    odd_all = (low, swap_core(low))
    keep, send = hidden_units(odd_all, unit_block)
    odd, leaving = core_sum_at_once(keep, send)
    results = (
        add_and_norm(normed, even, even_near, norm_pair),
        add_and_norm(normed_odd, odd, swap_near(leaving), norm_pair),
    )
    residual, output, low = zip(*results)
    kept = ((residual_one, residual_odd), (*even_all, *odd_all), residual)
    return (output, low, kept)


def units_backward(kept, grad_two, low, unit_block, norm_pair):
    residual_one, normed_all = kept[3:5]
    grad_mlp = share(low)
    pairs, hidden, sums, nears = [], [], [], []
    for chunk in range(2):
        span = slice(2 * chunk, 2 * chunk + 2)
        pair, units, keep, send = units_back(normed_all[span], grad_mlp[span], unit_block)
        own, leaving = core_sum_at_once(keep, send)
        pairs.append(pair)
        hidden.append(units)
        sums.append(own)
        nears.append(swap_near(leaving))
    unit_grads = units_weights(normed_all, grad_mlp, pairs, hidden)
    nears, unit_grads = lax.optimization_barrier((nears, unit_grads))
    results = norm_back(grad_two, sums, nears, residual_one, norm_pair)
    return (*results, unit_grads)


def heads_backward(kept, low, attn_block, layout, maps, tables):
    tokens, heads_kept, context = kept[:3]
    grad_attn = share(low)
    grad_projected, *partial = attend_back(
        grad_attn, attn_block, maps[1], *tables[1:], *layout, heads_kept
    )
    return (partial, attend_weights(tokens, grad_attn, grad_projected, context))


def per_device(
    tokens,
    segment_ids,
    pair_doc,
    slot_of,
    master,
    first_moment,
    second_moment,
    norm_params,
    norm_first,
    norm_second,
):
    columns = lax.axis_size("g")
    owners = 2 * columns
    column = lax.axis_index("g")
    core = lax.axis_index("c")
    z_pair = lax.axis_index("zp")
    near_bit = lax.axis_index("a")
    width = master.shape[1]
    shard_rows = tokens.shape[0]
    in_place = core == z_pair
    seg_row = jnp.where(in_place, segment_ids, swap_core(segment_ids))[0]
    targets = jnp.where(in_place, pair_doc, swap_core(pair_doc))[0]
    member, positions, counts = segment_layout(seg_row, SEGS)
    even = near_bit == 0
    chunk_order = [2 * core, 2 * core ^ 2, 2 * core + 1, 2 * core + 1 ^ 2]

    def in_order(values):
        return jnp.concatenate(
            [
                lax.dynamic_slice_in_dim(values, index * shard_rows, shard_rows, 0)
                for index in chunk_order
            ],
            axis=0,
        )

    cosine, sine_table = rope_tables(in_order(positions), HEAD_DIM)
    heads = width // lax.axis_size(("zp", "a")) // HEAD_DIM
    maps = (spread_map(heads), unspread_map(heads))
    tables = (
        jnp.concatenate([cosine, sine_table], axis=1),
        jnp.concatenate([cosine, cosine], axis=1),
        jnp.concatenate([sine_table, sine_table], axis=1),
    )
    seg_local = in_order(seg_row)
    layout = (seg_local[:, None], seg_local[None, :])
    member = lax.dynamic_slice_in_dim(member, 2 * core * shard_rows, 2 * shard_rows, 0)
    member = member[:, : SEGS - 1].astype(jnp.float32)
    counted = jnp.arange(2 * shard_rows)[:, None] // shard_rows == near_bit
    own_member = jnp.where(counted, member, 0.0)
    piece_rows = width // owners

    def to_owners(blocks):
        return lax.all_to_all(blocks, ("g", "c"), split_axis=0, concat_axis=0, tiled=True)

    tokens_all = first_rows(tokens)
    outgoing = master.astype(jnp.bfloat16).reshape(OWN_MAX, owners, piece_rows, width)
    incoming = to_owners(outgoing.transpose(1, 0, 2, 3)).reshape(-1, piece_rows, width)
    lengths = counts[: SEGS - 1].astype(jnp.float32)[:, None]
    targets = jnp.pad(targets.astype(jnp.float32)[:, None], ((0, SEGS - 1 - QRY_DEV), (0, 127)))
    hidden = (tokens_all[0].astype(jnp.float32), tokens_all[2].astype(jnp.float32))
    early = (tokens_all, hidden, maps, tables, layout, lengths, targets, member, own_member)
    incoming, early = lax.optimization_barrier((incoming, early))
    tokens_all, hidden, maps, tables, layout, lengths, targets, member, own_member = early

    def piece_of(*matrices):
        return jnp.concatenate(
            [
                lax.dynamic_index_in_dim(incoming, slot_of[matrix], 0, keepdims=False)
                for matrix in matrices
            ],
            axis=1,
        )

    attn_pieces = to_working_block(piece_of(0))
    unit_pieces = to_working_block(piece_of(1, 2, 3))
    attn_block = gather_rest(*gather_half(*attn_pieces))
    unit_pieces, attn_block = lax.optimization_barrier((unit_pieces, attn_block))
    unit_block = gather_rows_of(*unit_pieces)
    kept_list, weight_list = [], []
    for layer_index in range(LAYERS):
        if layer_index > 0:
            tokens_all = share(low)
        norm_set = norm_params[layer_index]
        later = layer_index + 1 < LAYERS
        if later:
            base = 4 * (layer_index + 1)
            pieces = piece_of(base, base + 1, base + 2, base + 3)
            pieces = to_working_block(after(pieces, unit_pieces))
        weight_list.append((attn_block, unit_block))
        even_results, finish, heads_kept = heads_forward(
            hidden, tokens_all, attn_block, norm_set[:2], layout, maps, tables
        )
        if later:
            pieces, even_results = lax.optimization_barrier((pieces, even_results))
            attn_block = gather_rows_of(*[part[:, :width] for part in pieces])
        hidden, low, units_kept = units_forward(
            even_results, finish, unit_block, norm_set[2:]
        )
        if later:
            unit_pieces, low = lax.optimization_barrier(([part[:, width:] for part in pieces], low))
            unit_block = gather_rows_of(*unit_pieces)
        kept_list.append((*heads_kept, *units_kept))
    pool_part = pool(hidden, own_member)
    pool_part = pool_part + swap_core(pool_part)
    pooled_sum, sent = embed(pool_part, swap_near(pool_part), lengths, targets)
    far = swap_far(sent)
    pair = jnp.stack([jnp.where(z_pair == 0, sent, far), jnp.where(z_pair == 0, far, sent)])
    every = lax.all_gather(pair, "g", axis=0, tiled=True).reshape(-1, sent.shape[1])
    loss_total, gradient, low, second_params = loss_and_back(
        every,
        pooled_sum,
        lengths,
        member,
        (2 * column + z_pair).reshape(1, 1),
        kept_list[-1][-1],
        norm_params[LAYERS - 1, 2:],
    )
    norm_list = [None] * LAYERS
    pending = []
    for layer_index in reversed(range(LAYERS)):
        kept = kept_list[layer_index]
        attn_block, unit_block = weight_list[layer_index]
        grad_one, low, first_params, unit_grads = units_backward(
            kept, gradient, low, unit_block, norm_params[layer_index, :2]
        )
        norm_list[layer_index] = jnp.concatenate(
            [jnp.where(even, *first_params), jnp.where(even, *second_params)], axis=0
        )
        unit_pieces = scatter_rows_of(after(unit_grads, pending))
        pending, low = lax.optimization_barrier((pending, low))
        arriving = [from_working_block(*pieces) for pieces in pending]
        partial, attn_grads = heads_backward(kept, low, attn_block, layout, maps, tables)
        if layer_index > 0:
            sums, nears = [], []
            for chunk in range(2):
                own, leaving = core_sum_at_once(*partial[2 * chunk : 2 * chunk + 2])
                sums.append(own)
                nears.append(swap_near(leaving))
            nears, attn_grads = lax.optimization_barrier((nears, attn_grads))
            gradient, low, second_params = norm_back(
                grad_one,
                sums,
                nears,
                kept_list[layer_index - 1][-1],
                norm_params[layer_index - 1, 2:],
            )
            attn_pieces = scatter_rows_of(after(attn_grads, unit_pieces))
            pending = [
                tuple(
                    jnp.concatenate(halves, axis=1) for halves in zip(attn_pieces, unit_pieces)
                )
            ]
    partial, attn_grads = lax.optimization_barrier((partial, attn_grads))
    attn_halves = scatter_half(attn_grads)
    even_sum, even_low = core_sum(*partial[:2])
    odd_sum, odd_low = core_sum(*partial[2:])
    near = swap_near(jnp.where(even, odd_low, even_low))
    attn_halves, unit_pieces = lax.optimization_barrier((attn_halves, unit_pieces))
    unit_arrived = from_working_block(*unit_pieces)
    attn_arrived = from_working_block(*scatter_rest(*attn_halves))
    arrived = [attn_arrived, unit_arrived] + arriving
    arrived, near = lax.optimization_barrier((arrived, near))
    gradient = jnp.where(even, grad_one[0], grad_one[1])
    gradient = gradient + jnp.where(even, even_sum, odd_sum) + near.astype(jnp.float32)
    norm_stack = jnp.stack(norm_list).reshape(-1, width)
    gradient, norm_stack = after((gradient, norm_stack), attn_arrived)
    token_grad = turn(gradient.astype(jnp.bfloat16)).astype(jnp.float32)
    outgoing = jnp.zeros((OWN_MAX * owners, piece_rows, width), jnp.bfloat16)
    pieces = jnp.concatenate(arrived, axis=1).astype(jnp.bfloat16)
    for matrix in range(MATS):
        outgoing = lax.dynamic_update_index_in_dim(
            outgoing, pieces[:, matrix * width : (matrix + 1) * width], slot_of[matrix], 0
        )
    incoming = to_owners(outgoing.reshape(owners, OWN_MAX, piece_rows, width))
    my_grads = (
        incoming.transpose(1, 0, 2, 3).reshape(OWN_MAX, width, width).astype(jnp.float32)
    )
    slot_ids = (2 * column + core) * OWN_MAX + jnp.arange(OWN_MAX, dtype=jnp.int32)
    in_use = jnp.any(slot_of[None, :] == slot_ids[:, None], axis=1)[:, None, None]
    norm_total = norm_stack + swap_core(norm_stack)
    norm_total = norm_total + swap_near(norm_total)
    norm_total = norm_total + swap_far(norm_total)
    if columns == 4:
        norm_total = norm_total + swap_x(norm_total)
        norm_total = norm_total + swap_y(norm_total)
    else:
        norm_total = jnp.sum(lax.all_gather(norm_total, "g", axis=0), axis=0)
    norm_total = norm_total.reshape(norm_params.shape)
    new_master, new_first, new_second = adam_update(
        master, first_moment, second_moment, my_grads, LEARN_RATE
    )
    new_master = jnp.where(in_use, new_master, master)
    new_first = jnp.where(in_use, new_first, first_moment)
    new_second = jnp.where(in_use, new_second, second_moment)
    new_norm, new_norm_first, new_norm_second = adam_update(
        norm_params, norm_first, norm_second, norm_total, NORM_RATE
    )
    return (
        loss_total,
        token_grad,
        new_master,
        new_first,
        new_second,
        new_master.astype(jnp.bfloat16),
        new_norm,
        new_norm_first,
        new_norm_second,
    )


def solution(mesh):
    owners, model_parts = mesh.devices.shape
    work_mesh = Mesh(mesh.devices.reshape(owners // 2, 2, model_parts // 2, 2), AXES)
    dp, mp = ("g", "c"), ("zp", "a")
    in_specs = (
        P(AXES, None),
        P(dp, None),
        P(dp, None),
        P(),
        P(dp, None, mp),
        P(dp, None, mp),
        P(dp, None, mp),
        P(),
        P(),
        P(),
    )
    out_specs = (
        P(),
        P(AXES, None),
        P(dp, None, mp),
        P(dp, None, mp),
        P(dp, None, mp),
        P(dp, None, mp),
        P(),
        P(),
        P(),
    )
    return jax.shard_map(
        per_device, mesh=work_mesh, in_specs=in_specs, out_specs=out_specs, check_vma=False
    )
```

```python
import functools

import jax
import jax.numpy as jnp
from jax import lax
from jax.experimental import pallas as pl
from jax.experimental.pallas import tpu as pltpu
from jax.sharding import Mesh
from jax.sharding import PartitionSpec as P

HEAD_DIM = 64
LAYERS = 2
QRY_DEV = 4
OWN_MAX = 2
STEP = 7
SEGS = 9
MATS = 8


BETA_ONE = 0.9
BETA_TWO = 0.999
LEARN_RATE = 0.02
NORM_RATE = 0.4
WEIGHT_DECAY = 0.5
ADAM_EPSILON = 1e-08
NORM_EPSILON = 1e-05
SOFTMAX_DIVISOR = 0.01
EXACT_ARITHMETIC = lax.Precision.HIGHEST


def segment_layout(seg_row, seg_count):
    length = seg_row.shape[0]
    place_ids = jnp.arange(length, dtype=jnp.int32)
    member = seg_row[:, None] == jnp.arange(seg_count, dtype=jnp.int32)[None, :]
    starts = jnp.min(jnp.where(member, place_ids[:, None], length), axis=0)
    counts = jnp.sum(member.astype(jnp.int32), axis=0)
    positions = place_ids - jnp.sum(jnp.where(member, starts[None, :], 0), axis=1)
    return (member, positions, counts)


def rope_tables(positions, head_dim):
    half_dim = head_dim // 2
    inverse = 1000.0 ** (-(jnp.arange(half_dim, dtype=jnp.float32) * 2.0 / head_dim))
    angles = positions.astype(jnp.float32)[:, None] * inverse[None, :]
    cosine = jnp.concatenate([jnp.cos(angles), jnp.cos(angles)], axis=1)
    sine_table = jnp.concatenate([jnp.sin(angles), jnp.sin(angles)], axis=1)
    return (cosine, sine_table)


def adam_update(weight, first_state, second_state, gradient, step_rate):
    first_new = BETA_ONE * first_state + (1.0 - BETA_ONE) * gradient
    second_new = BETA_TWO * second_state + (1.0 - BETA_TWO) * gradient * gradient
    first_hat = first_new / (1.0 - BETA_ONE**STEP)
    second_hat = second_new / (1.0 - BETA_TWO**STEP)
    weight_new = weight - step_rate * (
        first_hat / (jnp.sqrt(second_hat) + ADAM_EPSILON) + WEIGHT_DECAY * weight
    )
    return (weight_new, first_new, second_new)


def spread_map(heads):
    width = heads * HEAD_DIM
    half = HEAD_DIM // 2
    row = jnp.arange(3 * width, dtype=jnp.int32)[:, None]
    column = jnp.arange(6 * width, dtype=jnp.int32)[None, :]
    kind = column // (2 * width)
    head = column % (2 * width) // (2 * HEAD_DIM)
    lane = column % (2 * HEAD_DIM)
    base = kind * width + head * HEAD_DIM
    within = lane % HEAD_DIM
    plain = (row == base + within) & (lane < HEAD_DIM)
    turned = (lane >= HEAD_DIM) & (kind < 2)
    minus = turned & (within < half) & (row == base + within + half)
    plus = turned & (within >= half) & (row == base + within - half)
    return (plain.astype(jnp.float32) + plus - minus.astype(jnp.float32)).astype(jnp.bfloat16)


def unspread_map(heads):
    width = heads * HEAD_DIM
    half = HEAD_DIM // 2
    row = jnp.arange(4 * width, dtype=jnp.int32)[:, None]
    column = jnp.arange(2 * width, dtype=jnp.int32)[None, :]
    base = (column // HEAD_DIM) * 2 * HEAD_DIM
    within = column % HEAD_DIM
    plain = (row == base + within).astype(jnp.float32)
    plus = ((within < half) & (row == base + within + half)).astype(jnp.float32)
    minus = ((within >= half) & (row == base + within - half)).astype(jnp.float32)
    return jnp.stack([plain, plus - minus]).astype(jnp.bfloat16)


def flipped(left_side, right_side):
    return lax.dot_general(
        left_side, right_side, (((1,), (1,)), ((), ())), preferred_element_type=jnp.float32
    )


def straight(left_side, right_side):
    return jnp.dot(left_side, right_side, preferred_element_type=jnp.float32)


def over_rows(left_side, right_side):
    return lax.dot_general(
        left_side, right_side, (((0,), (0,)), ((), ())), preferred_element_type=jnp.float32
    )


def call(
    body, outputs, operands, scratch=(), mebibytes=16, blocked=False, near=(), far_out=(), name=None,
    long=False,
):
    out_shape = tuple(
        pltpu.HBM(shape, dtype) if place in far_out else jax.ShapeDtypeStruct(shape, dtype)
        for place, (shape, dtype) in enumerate(outputs)
    )
    specs = {}
    if blocked:

        def whole(shape):
            zeros = (0,) * len(shape)
            return pl.BlockSpec(shape, lambda step: zeros, pipeline_mode=pl.Buffered(1))

        specs = {
            "grid": (1,),
            "in_specs": [whole(value.shape) for value in operands],
            "out_specs": tuple(whole(shape) for shape, _ in outputs),
        }
        operands = [
            value if place in near else pltpu.with_memory_space_constraint(value, pltpu.HBM)
            for place, value in enumerate(operands)
        ]
    return pl.pallas_call(
        body,
        out_shape=out_shape,
        scratch_shapes=list(scratch),
        compiler_params=pltpu.CompilerParams(vmem_limit_bytes=mebibytes * 2**20),
        cost_estimate=pl.CostEstimate(
            flops=4 * 10**9 if long else 10**6,
            bytes_accessed=10**7 if long else 10**5,
            transcendentals=0,
        ),
        name=name,
        **specs,
    )(*operands)


def attend_block(
    heads, chunk, rows, query_ref, key_ref, value_ref, seg_col_ref, seg_row_ref
):
    pad = 2 * HEAD_DIM
    span = slice(chunk * rows, (chunk + 1) * rows)
    bias = jnp.where(seg_col_ref[span, :] == seg_row_ref[...], 0.0, -1e30)
    lanes = lax.broadcasted_iota(jnp.int32, (rows, pad), 1)
    totals_all = jnp.zeros((rows, pad), jnp.float32)
    pieces = []
    for head in range(heads):
        cols = slice(head * pad, (head + 1) * pad)
        scores = flipped(query_ref[span, cols], key_ref[:, cols]) + bias
        row_top = jnp.max(scores, axis=-1, keepdims=True)
        weights = jnp.exp(scores - row_top)
        totals = jnp.sum(weights, axis=-1, keepdims=True)
        probs = (weights * (1.0 / totals)).astype(jnp.bfloat16)
        context = straight(probs, value_ref[:, cols])
        pieces.append(context[:, :HEAD_DIM].astype(jnp.bfloat16))
        totals_all = jnp.where(lanes == head, row_top + jnp.log(totals), totals_all)
    return (jnp.concatenate(pieces, axis=1), totals_all)


def attend_first_kernel(heads, *refs):
    chunk_refs, refs = refs[:4], refs[4:]
    weight_ref, map_ref, table_ref, seg_col_ref, seg_row_ref = refs[:5]
    query_ref, key_ref, value_ref, context_ref, total_ref, keep_ref, send_ref = refs[5:]
    width = heads * HEAD_DIM
    pad = 2 * HEAD_DIM
    rows = chunk_refs[0].shape[0]
    weights = straight(weight_ref[:, : 3 * width], map_ref[...]).astype(jnp.bfloat16)
    for chunk in range(4):
        span = slice(chunk * rows, (chunk + 1) * rows)
        projected = straight(chunk_refs[chunk][...], weights)
        table = table_ref[span, :]
        for head in range(heads):
            for base, ref, scale in ((0, query_ref, 0.0625), (heads * pad, key_ref, 1.0)):
                lanes = slice(base + head * pad, base + (head + 1) * pad)
                turned = projected[:, lanes] * table
                turned = turned + pltpu.roll(turned, HEAD_DIM, 1)
                ref[span, head * pad : (head + 1) * pad] = (turned * scale).astype(jnp.bfloat16)
        value_ref[span, :] = projected[:, 2 * heads * pad :].astype(jnp.bfloat16)
    out_weights = weight_ref[:, 3 * width :]
    for place, out_ref in enumerate((keep_ref, send_ref)):
        span = slice(place * rows, (place + 1) * rows)
        context, totals = attend_block(
            heads, place, rows, query_ref, key_ref, value_ref, seg_col_ref, seg_row_ref
        )
        context_ref[span, :] = context
        total_ref[span, :] = totals
        out_ref[...] = flipped(context, out_weights).astype(out_ref.dtype)


def attend_second_kernel(heads, *refs):
    weight_ref, seg_col_ref, seg_row_ref, query_ref, key_ref, value_ref = refs[:6]
    context_ref, total_ref, keep_ref, send_ref = refs[6:]
    rows = keep_ref.shape[0]
    out_weights = weight_ref[:, 3 * heads * HEAD_DIM :]
    for place, out_ref in enumerate((keep_ref, send_ref)):
        span = slice(place * rows, (place + 1) * rows)
        context, totals = attend_block(
            heads, 2 + place, rows, query_ref, key_ref, value_ref, seg_col_ref, seg_row_ref
        )
        context_ref[span, :] = context
        total_ref[span, :] = totals
        out_ref[...] = flipped(context, out_weights).astype(out_ref.dtype)


def attend_first(chunks, attn_block, mapping, table, seg_col, seg_row):
    width = attn_block.shape[0]
    part = attn_block.shape[1] // 4
    rows = chunks[0].shape[0]
    length = 4 * rows
    return call(
        functools.partial(attend_first_kernel, part // HEAD_DIM),
        [((length, 2 * part), jnp.bfloat16)] * 3
        + [
            ((2 * rows, part), jnp.bfloat16),
            ((2 * rows, 2 * HEAD_DIM), jnp.float32),
            ((rows, width), jnp.float32),
            ((rows, width), jnp.bfloat16),
        ],
        (*chunks, attn_block, mapping, table, seg_col, seg_row),
        mebibytes=28,
        blocked=True,
        near=(0, 1, 2, 3),
        name="attend_first",
    )


def attend_second(attn_block, seg_col, seg_row, query, key, value):
    width = attn_block.shape[0]
    part = attn_block.shape[1] // 4
    rows = query.shape[0] // 4
    return call(
        functools.partial(attend_second_kernel, part // HEAD_DIM),
        [
            ((2 * rows, part), jnp.bfloat16),
            ((2 * rows, 2 * HEAD_DIM), jnp.float32),
            ((rows, width), jnp.float32),
            ((rows, width), jnp.bfloat16),
        ],
        (attn_block, seg_col, seg_row, query, key, value),
        mebibytes=28,
        name="attend_second",
    )


def attend_back_kernel(heads, *refs):
    chunk_refs, refs = refs[:4], refs[4:]
    weight_ref, map_ref, cos_ref, sin_ref, seg_col_ref, seg_row_ref = refs[:6]
    query_ref, key_ref, value_ref, even_total_ref, odd_total_ref = refs[6:11]
    projected_ref, *out_refs = refs[11:16]
    grad_query, grad_key, grad_value = refs[16:]
    width = heads * HEAD_DIM
    pad = 2 * HEAD_DIM
    rows = chunk_refs[0].shape[0]
    out_weights = weight_ref[:, 3 * width :]
    empty = jnp.zeros((out_weights.shape[0], HEAD_DIM), jnp.bfloat16)
    wide = []
    for head in range(heads):
        wide += [out_weights[:, head * HEAD_DIM : (head + 1) * HEAD_DIM], empty]
    wide = jnp.concatenate(wide, axis=1)
    for chunk in range(4):
        span = slice(chunk * rows, (chunk + 1) * rows)
        grads_all = straight(chunk_refs[chunk][...], wide).astype(jnp.bfloat16)
        total_ref = even_total_ref if chunk < 2 else odd_total_ref
        total_span = slice(chunk % 2 * rows, (chunk % 2 + 1) * rows)
        bias = jnp.where(seg_col_ref[span, :] == seg_row_ref[...], 0.0, -1e30)
        for head in range(heads):
            cols = slice(head * pad, (head + 1) * pad)
            query = query_ref[span, cols]
            key = key_ref[:, cols]
            grads = grads_all[:, cols]
            scores = flipped(query, key) + bias
            probs = jnp.exp(scores - total_ref[total_span, head : head + 1])
            grad_probs = flipped(grads, value_ref[:, cols])
            inner = jnp.sum(probs * grad_probs, axis=-1, keepdims=True)
            grad_scores = (probs * (grad_probs - inner)).astype(jnp.bfloat16)
            grad_query[span, cols] = (straight(grad_scores, key) * 0.125).astype(jnp.bfloat16)
            key_part = straight(query.T, grad_scores)
            value_part = straight(grads.T, probs.astype(jnp.bfloat16))
            if chunk == 0:
                grad_key[cols, :] = key_part
                grad_value[cols, :] = value_part
            else:
                grad_key[cols, :] += key_part
                grad_value[cols, :] += value_part
    for chunk, out_ref in enumerate(out_refs):
        span = slice(chunk * rows, (chunk + 1) * rows)
        grad_k = (grad_key[:, span] * 2.0).astype(jnp.bfloat16).T
        grad_v = grad_value[:, span].astype(jnp.bfloat16).T
        both = jnp.concatenate([grad_query[span, :], grad_k], axis=1)
        plain = straight(both, map_ref[0])
        turned = straight(both, map_ref[1])
        cosine = jnp.concatenate([cos_ref[span, :]] * heads, axis=1)
        sine = jnp.concatenate([sin_ref[span, :]] * heads, axis=1)
        turned = (plain * cosine + turned * sine).astype(jnp.bfloat16)
        grad_v = [grad_v[:, head * pad : head * pad + HEAD_DIM] for head in range(heads)]
        projected = jnp.concatenate([turned, *grad_v], axis=1)
        projected_ref[span, :] = projected
        out_ref[...] = flipped(projected, weight_ref[:, : 3 * width]).astype(out_ref.dtype)


def attend_back(chunks, attn_block, mapping, cosine, sine, seg_col, seg_row, kept):
    width = attn_block.shape[0]
    part = attn_block.shape[1] // 4
    rows = chunks[0].shape[0]
    length = 4 * rows
    return call(
        functools.partial(attend_back_kernel, part // HEAD_DIM),
        [((length, 3 * part), jnp.bfloat16)]
        + [((rows, width), jnp.float32), ((rows, width), jnp.bfloat16)] * 2,
        (*chunks, attn_block, mapping, cosine, sine, seg_col, seg_row, *kept),
        mebibytes=28,
        scratch=[
            pltpu.VMEM((length, 2 * part), jnp.bfloat16),
            pltpu.VMEM((2 * part, length), jnp.float32),
            pltpu.VMEM((2 * part, length), jnp.float32),
        ],
        long=True,
        name="attend_back",
    )


def units_kernel(*refs):
    chunk_refs, (weight_ref, keep_ref, send_ref) = refs[:2], refs[2:]
    units = weight_ref.shape[1] // 3
    for chunk_ref, out_ref in zip(chunk_refs, (keep_ref, send_ref)):
        tokens = chunk_ref[...]
        gate = straight(tokens, weight_ref[:, :units])
        up = straight(tokens, weight_ref[:, units : 2 * units])
        hidden = (gate / (1.0 + jnp.exp(-gate)) * up).astype(jnp.bfloat16)
        out_ref[...] = flipped(hidden, weight_ref[:, 2 * units :]).astype(out_ref.dtype)


def hidden_units(chunks, weights):
    rows, width = chunks[0].shape
    return call(
        units_kernel,
        [((rows, width), jnp.float32), ((rows, width), jnp.bfloat16)],
        (*chunks, weights),
        name="hidden_units",
    )


def units_back_kernel(*refs):
    token_refs, chunk_refs, weight_ref = refs[:2], refs[2:4], refs[4]
    grad_ref, hidden_ref, keep_ref, send_ref = refs[5:]
    rows, width = chunk_refs[0].shape
    units = weight_ref.shape[1] // 3
    for place, out_ref in enumerate((keep_ref, send_ref)):
        span = slice(place * rows, (place + 1) * rows)
        tokens = token_refs[place][...]
        gate = straight(tokens, weight_ref[:, :units])
        up = straight(tokens, weight_ref[:, units : 2 * units])
        grad_hidden = straight(chunk_refs[place][...], weight_ref[:, 2 * units :])
        share = 1.0 / (1.0 + jnp.exp(-gate))
        silu = gate * share
        hidden_ref[span, :] = (silu * up).astype(jnp.bfloat16)
        grad_up = (grad_hidden * silu).astype(jnp.bfloat16)
        slope = share + silu * (1.0 - share)
        grad_gate = (grad_hidden * up * slope).astype(jnp.bfloat16)
        grad_ref[span, :units] = grad_gate
        grad_ref[span, units:] = grad_up
        result = flipped(grad_gate, weight_ref[:, :units])
        result = result + flipped(grad_up, weight_ref[:, units : 2 * units])
        out_ref[...] = result.astype(out_ref.dtype)


def units_back(tokens, chunks, weights):
    rows, width = chunks[0].shape
    units = weights.shape[1] // 3
    return call(
        units_back_kernel,
        [
            ((2 * rows, 2 * units), jnp.bfloat16),
            ((2 * rows, units), jnp.bfloat16),
            ((rows, width), jnp.float32),
            ((rows, width), jnp.bfloat16),
        ],
        (*tokens, *chunks, weights),
        mebibytes=24,
        long=True,
        name="units_back",
    )


def units_weights_kernel(*refs):
    token_refs, grad_refs, refs = refs[:4], refs[4:8], refs[8:]
    even_pair_ref, odd_pair_ref, even_hidden_ref, odd_hidden_ref, out_ref = refs
    rows, width = token_refs[0].shape
    units = even_hidden_ref.shape[1]
    for tile in range(0, width, 256):
        cols = slice(tile, tile + 256)
        pair, down = 0.0, 0.0
        for chunk in range(4):
            span = slice(chunk % 2 * rows, (chunk % 2 + 1) * rows)
            pair_ref = even_pair_ref if chunk < 2 else odd_pair_ref
            hidden_ref = even_hidden_ref if chunk < 2 else odd_hidden_ref
            pair = pair + over_rows(token_refs[chunk][:, cols], pair_ref[span, :])
            down = down + over_rows(grad_refs[chunk][:, cols], hidden_ref[span, :])
        out_ref[cols, : 2 * units] = pair.astype(jnp.bfloat16)
        out_ref[cols, 2 * units :] = down.astype(jnp.bfloat16)


def units_weights(tokens, grads, pairs, hidden):
    rows, width = tokens[0].shape
    units = hidden[0].shape[1]
    return call(
        units_weights_kernel,
        [((width, 3 * units), jnp.bfloat16)],
        (*tokens, *grads, *pairs, *hidden),
        blocked=True,
        near=tuple(range(12)),
        far_out=(0,),
        long=True,
        name="units_weights",
    )[0]


def attend_weights_kernel(*refs):
    token_refs, grad_refs, refs = refs[:4], refs[4:8], refs[8:]
    projected_ref, even_context_ref, odd_context_ref, out_ref = refs
    rows, width = token_refs[0].shape
    for tile in range(0, width, 256):
        cols = slice(tile, tile + 256)
        left, right = 0.0, 0.0
        for chunk in range(4):
            span = slice(chunk % 2 * rows, (chunk % 2 + 1) * rows)
            context_ref = even_context_ref if chunk < 2 else odd_context_ref
            projected = projected_ref[chunk * rows : (chunk + 1) * rows, :]
            left = left + over_rows(token_refs[chunk][:, cols], projected)
            right = right + over_rows(grad_refs[chunk][:, cols], context_ref[span, :])
        both = jnp.concatenate([left, right], axis=1)
        out_ref[cols, :] = both.astype(jnp.bfloat16)


def attend_weights(tokens, grads, projected, context):
    rows, width = tokens[0].shape
    part = context[0].shape[1]
    return call(
        attend_weights_kernel,
        [((width, 4 * part), jnp.bfloat16)],
        (*tokens, *grads, projected, *context),
        blocked=True,
        near=tuple(range(11)),
        far_out=(0,),
        long=True,
        name="attend_weights",
    )[0]


def norm_kernel(*refs):
    base_ref, own_ref, near_ref, norm_ref, residual_ref, normed_ref, low_ref = refs
    residual = base_ref[...] + own_ref[...] + near_ref[...].astype(jnp.float32)
    residual_ref[...] = residual
    centered = residual - jnp.mean(residual, axis=-1, keepdims=True)
    variance = jnp.mean(centered * centered, axis=-1, keepdims=True)
    normed = centered * lax.rsqrt(variance + NORM_EPSILON) * norm_ref[0:1, :] + norm_ref[1:2, :]
    normed_ref[...] = normed
    low_ref[...] = normed.astype(jnp.bfloat16)


def add_and_norm(base, own, near, norm_pair):
    shape = base.shape
    return call(
        norm_kernel,
        [(shape, jnp.float32), (shape, jnp.float32), (shape, jnp.bfloat16)],
        (base, own, near, norm_pair),
        blocked=True,
        near=(1, 2),
        far_out=(0, 1),
        name="add_and_norm",
    )


def norm_back_rows(grad, residual, gain):
    centered = residual - jnp.mean(residual, axis=-1, keepdims=True)
    variance = jnp.mean(centered * centered, axis=-1, keepdims=True)
    inverse = lax.rsqrt(variance + NORM_EPSILON)
    scaled = centered * inverse
    wide = grad * gain
    inner = jnp.mean(wide * scaled, axis=-1, keepdims=True)
    result = inverse * (wide - jnp.mean(wide, axis=-1, keepdims=True) - scaled * inner)
    gain_grad = jnp.sum(grad * scaled, axis=0, keepdims=True)
    return (result, jnp.concatenate([gain_grad, jnp.sum(grad, axis=0, keepdims=True)], axis=0))


def norm_back_kernel(*refs):
    norm_ref = refs[8]
    for chunk in range(2):
        base_ref, own_ref, near_ref, residual_ref = refs[4 * chunk : 4 * chunk + 4]
        out_ref, low_ref, params_ref = refs[9 + 3 * chunk : 12 + 3 * chunk]
        grad = base_ref[...] + own_ref[...] + near_ref[...].astype(jnp.float32)
        result, params = norm_back_rows(grad, residual_ref[...], norm_ref[0:1, :])
        out_ref[...] = result
        low_ref[...] = result.astype(jnp.bfloat16)
        params_ref[...] = params


def norm_back(bases, sums, nears, residuals, norm_pair):
    shape = residuals[0].shape
    chunk_out = [(shape, jnp.float32), (shape, jnp.bfloat16), ((2, shape[1]), jnp.float32)]
    operands = [part for parts in zip(bases, sums, nears, residuals) for part in parts]
    outputs = call(
        norm_back_kernel,
        chunk_out * 2,
        (*operands, norm_pair),
        blocked=True,
        near=(1, 2, 5, 6),
        far_out=(0, 2, 3, 5),
        long=True,
        name="norm_back",
    )
    return tuple(zip(outputs[:3], outputs[3:]))


def embed_kernel(sum_ref, near_ref, length_ref, target_ref, total_ref, out_ref):
    total = sum_ref[...] + near_ref[...]
    total_ref[...] = total
    pooled = total / length_ref[...]
    embeds = pooled * lax.rsqrt(jnp.sum(pooled * pooled, axis=1, keepdims=True) + 1e-06)
    out_ref[...] = jnp.concatenate([embeds, target_ref[...]], axis=1).astype(jnp.bfloat16)


def embed(pool_part, near_part, lengths, targets):
    rows, width = pool_part.shape
    return call(
        embed_kernel,
        [
            ((rows, width), jnp.float32),
            ((rows, width + targets.shape[1]), jnp.bfloat16),
        ],
        (pool_part, near_part, lengths, targets),
        blocked=True,
        far_out=(),
        name="embed",
    )


def adam_kernel(use_ref, grad_ref, master_ref, first_ref, second_ref, *out_refs):
    new_master_ref, new_first_ref, new_second_ref, copy_ref = out_refs
    used = use_ref[pl.program_id(0)] > 0
    rows = grad_ref.shape[2]
    for part in range(grad_ref.shape[0]):
        span = slice(part * rows, (part + 1) * rows)
        master, first, second = master_ref[0, span], first_ref[0, span], second_ref[0, span]
        grad = grad_ref[part, 0].astype(jnp.float32)
        new_master, new_first, new_second = adam_update(master, first, second, grad, LEARN_RATE)
        new_master = jnp.where(used, new_master, master)
        new_master_ref[0, span] = new_master
        new_first_ref[0, span] = jnp.where(used, new_first, first)
        new_second_ref[0, span] = jnp.where(used, new_second, second)
        copy_ref[0, span] = new_master.astype(jnp.bfloat16)


def adam_slots(in_use, grads, master, first_moment, second_moment):
    owners, slots, rows, width = grads.shape
    if rows % 16 != 0 or owners % 4 != 0:
        grads = grads.transpose(1, 0, 2, 3).reshape(master.shape).astype(jnp.float32)
        new_master, new_first, new_second = adam_update(
            master, first_moment, second_moment, grads, LEARN_RATE
        )
        used = in_use[:, None, None]
        new_master = jnp.where(used, new_master, master)
        new_first = jnp.where(used, new_first, first_moment)
        new_second = jnp.where(used, new_second, second_moment)
        return (new_master, new_first, new_second, new_master.astype(jnp.bfloat16))
    block = pl.BlockSpec((1, 4 * rows, width), lambda slot, part: (slot, part, 0))
    shape = pltpu.HBM(master.shape, jnp.float32)
    far = [
        pltpu.with_memory_space_constraint(value, pltpu.HBM)
        for value in (grads, master, first_moment, second_moment)
    ]
    return pl.pallas_call(
        adam_kernel,
        grid=(slots, owners // 4),
        in_specs=[
            pl.BlockSpec(memory_space=pltpu.SMEM),
            pl.BlockSpec((4, 1, rows, width), lambda slot, part: (part, slot, 0, 0)),
            block,
            block,
            block,
        ],
        out_specs=(block, block, block, block),
        out_shape=(shape, shape, shape, pltpu.HBM(master.shape, jnp.bfloat16)),
        compiler_params=pltpu.CompilerParams(vmem_limit_bytes=32 * 2**20),
        name="adam_slots",
    )(in_use.astype(jnp.int32), *far)


def pool_kernel(even_ref, odd_ref, member_ref, out_ref):
    rows = even_ref.shape[0]
    total = 0.0
    for chunk, hidden_ref in enumerate((even_ref, odd_ref)):
        member = member_ref[chunk * rows : (chunk + 1) * rows, :]
        total = total + exact(member.T, hidden_ref[...])
    out_ref[...] = total


def pool(hidden, member):
    return call(
        pool_kernel,
        [((member.shape[1], hidden[0].shape[1]), jnp.float32)],
        (*hidden, member),
        blocked=True,
        near=(0, 1),
        name="pool",
    )[0]


def loss_kernel(*refs):
    every_ref, sum_ref, length_ref, member_ref, group_ref, *residual_refs, norm_ref = refs[:8]
    loss_ref, *out_refs = refs[8:]
    width = sum_ref.shape[1]
    rows = SEGS - 1
    docs = rows - QRY_DEV
    total = every_ref.shape[0]
    vectors = every_ref[:, :width]
    targets = every_ref[:, width : width + 1].astype(jnp.float32)
    scores = flipped(vectors, vectors) / SOFTMAX_DIVISOR
    row = lax.broadcasted_iota(jnp.int32, (total, total), 0)
    column = lax.broadcasted_iota(jnp.int32, (total, total), 1)
    place = column % rows
    is_doc = place >= QRY_DEV
    doc = column // rows * docs + place - QRY_DEV
    is_query = row % rows < QRY_DEV
    hit = is_doc & (doc.astype(jnp.float32) == targets)
    masked = jnp.where(is_doc, scores, -1e30)
    row_top = jnp.max(masked, axis=1, keepdims=True)
    log_totals = row_top + jnp.log(jnp.sum(jnp.exp(masked - row_top), axis=1, keepdims=True))
    chosen = jnp.sum(jnp.where(hit, scores, 0.0), axis=1, keepdims=True)
    losses = jnp.where(is_query[:, :1], log_totals - chosen, 0.0)
    loss_ref[...] = jnp.sum(losses, axis=0, keepdims=True)
    logits = (jnp.exp(masked - log_totals) - hit.astype(jnp.float32)) / SOFTMAX_DIVISOR
    logits = jnp.where(is_query & is_doc, logits, 0.0)
    wide = vectors.astype(jnp.float32)
    embed_grads = exact(logits, wide) + exact(logits.T, wide)
    mine = lax.broadcasted_iota(jnp.int32, (rows, total), 1) - group_ref[...] * rows
    mine = (mine == lax.broadcasted_iota(jnp.int32, (rows, total), 0)).astype(jnp.float32)
    embed_grads = exact(mine, embed_grads)
    pooled = sum_ref[...] / length_ref[...]
    inverse = lax.rsqrt(jnp.sum(pooled * pooled, axis=1, keepdims=True) + 1e-06)
    inner = jnp.sum(embed_grads * pooled, axis=1, keepdims=True)
    pooled_grads = embed_grads * inverse - pooled * (inverse * inverse * inverse * inner)
    pooled_grads = pooled_grads / length_ref[...]
    chunk_rows = residual_refs[0].shape[0]
    for chunk, residual_ref in enumerate(residual_refs):
        member = member_ref[chunk * chunk_rows : (chunk + 1) * chunk_rows, :]
        grad = exact(member, pooled_grads)
        result, params = norm_back_rows(grad, residual_ref[...], norm_ref[0:1, :])
        out_ref, low_ref, params_ref = out_refs[3 * chunk : 3 * chunk + 3]
        out_ref[...] = result
        low_ref[...] = result.astype(jnp.bfloat16)
        params_ref[...] = params


def exact(left_side, right_side):
    return lax.dot_general(
        left_side,
        right_side,
        (((1,), (0,)), ((), ())),
        precision=EXACT_ARITHMETIC,
        preferred_element_type=jnp.float32,
    )


def loss_and_back(every, pooled_sum, lengths, member, group, residual, norm_pair):
    shape = residual[0].shape
    chunk_out = [
        (shape, jnp.float32),
        (shape, jnp.bfloat16),
        ((2, shape[1]), jnp.float32),
    ]
    loss, *outputs = call(
        loss_kernel,
        [((1, 1), jnp.float32), *chunk_out, *chunk_out],
        (every, pooled_sum, lengths, member, group, *residual, norm_pair),
        blocked=True,
        far_out=(0, 1, 3, 4, 6),
        long=True,
        name="loss_and_back",
    )
    return (loss[0, 0], *zip(outputs[:3], outputs[3:]))


AXES = ("g", "c", "zp", "a")


def hop(value, move):
    columns = lax.axis_size("g")
    pairs = []
    for column in range(columns):
        for core in range(2):
            for z in range(4):
                to_column, to_core, to_z = move(column, core, z)
                pairs.append(((column * 2 + core) * 4 + z, (to_column * 2 + to_core) * 4 + to_z))
    return lax.ppermute(value, AXES, pairs)


def swap_core(value):
    return hop(value, lambda g, c, z: (g, 1 - c, z))


def swap_near(value):
    return hop(value, lambda g, c, z: (g, c, z ^ 1))


def swap_far(value):
    return hop(value, lambda g, c, z: (g, c, z ^ 2))


def turn(value):
    return hop(value, lambda g, c, z: (g, z // 2, 2 * c + z % 2))


def first_rows(tokens):
    own = turn(tokens)
    sibling = hop(tokens, lambda g, c, z: (g, 1 - z // 2, 2 * c + z % 2))
    near = hop(tokens, lambda g, c, z: (g, z // 2, 2 * c + (z % 2 ^ 1)))
    across = hop(tokens, lambda g, c, z: (g, 1 - z // 2, 2 * c + (z % 2 ^ 1)))
    even = lax.axis_index("a") == 0
    return (
        jnp.where(even, own, near),
        jnp.where(even, sibling, across),
        jnp.where(even, near, own),
        jnp.where(even, across, sibling),
    )


def share(low):
    return (low[0], swap_core(low[0]), low[1], swap_core(low[1]))


def core_sum(keep, send):
    total = keep + swap_core(send).astype(jnp.float32)
    return (total, total.astype(jnp.bfloat16))


def core_sum_at_once(keep, send):
    both = lax.all_gather(send, "c", axis=0)
    other = jnp.where(lax.axis_index("c") == 0, both[1], both[0])
    total = keep + other.astype(jnp.float32)
    return (total, total.astype(jnp.bfloat16))


def after(value, *others):
    return lax.optimization_barrier((value, *others))[0]


def swap_x(value):
    return hop(value, lambda g, c, z: (g ^ 1, c, z))


def swap_y(value):
    return hop(value, lambda g, c, z: (g ^ 2, c, z))


def ordered(bit, mine, other, axis):
    low = jnp.where(bit == 0, mine, other)
    return jnp.stack([low, jnp.where(bit == 0, other, mine)], axis=axis)


def to_working_block(piece):
    core = lax.axis_index("c")
    first = hop(piece, lambda g, c, z: (g, 0, z) if c == 1 else (g, 1, z ^ 2))
    second = hop(piece, lambda g, c, z: (g, 1, z ^ 2) if c == 1 else (g, 0, z))
    return (jnp.where(core == 0, piece, first), jnp.where(core == 0, first, second))


def from_working_block(upper, lower):
    core = lax.axis_index("c")
    first = hop(
        jnp.where(core == 0, lower, upper),
        lambda g, c, z: (g, 1, z) if c == 0 else (g, 0, z ^ 2),
    )
    second = hop(lower, lambda g, c, z: (g, 1, z ^ 2) if c == 1 else (g, 0, z))
    mine = jnp.where(core == 0, upper, second).astype(jnp.float32)
    return mine + first.astype(jnp.float32)


def gather_rows_of(upper, lower):
    return lax.all_gather(jnp.concatenate([upper, lower], axis=0), "g", axis=0, tiled=True)


def gather_half(upper, lower):
    if lax.axis_size("g") != 4:
        return (upper, lower)
    column = lax.axis_index("g")
    return (
        ordered(column % 2, upper, swap_x(upper), 0),
        ordered(column // 2, lower, swap_y(lower), 0),
    )


def gather_rest(upper, lower):
    if lax.axis_size("g") != 4:
        return gather_rows_of(upper, lower)
    column = lax.axis_index("g")
    upper_all = ordered(column // 2, upper, swap_y(upper), 0)
    lower_all = ordered(column % 2, lower, swap_x(lower), 1)
    return jnp.stack([upper_all, lower_all], axis=2).reshape(-1, upper.shape[2])


def scatter_rows_of(partial):
    rows = lax.psum_scatter(partial, "g", scatter_dimension=0, tiled=True)
    half = rows.shape[0] // 2
    return (rows[:half], rows[half:])


def split_halves(values, bit, axis):
    low = lax.index_in_dim(values, 0, axis, keepdims=False)
    high = lax.index_in_dim(values, 1, axis, keepdims=False)
    mine = jnp.where(bit == 0, low, high).astype(jnp.float32)
    return (mine, jnp.where(bit == 0, high, low).astype(jnp.bfloat16))


def scatter_half(partial):
    if lax.axis_size("g") != 4:
        return scatter_rows_of(partial)
    column = lax.axis_index("g")
    blocks = partial.reshape(2, 2, 2, partial.shape[0] // 8, partial.shape[1])
    upper, upper_sent = split_halves(blocks[:, :, 0], column % 2, 1)
    lower, lower_sent = split_halves(blocks[:, :, 1], column // 2, 0)
    return (
        upper + swap_x(upper_sent).astype(jnp.float32),
        lower + swap_y(lower_sent).astype(jnp.float32),
    )


def scatter_rest(upper, lower):
    if lax.axis_size("g") != 4:
        return (upper, lower)
    column = lax.axis_index("g")
    upper, upper_sent = split_halves(upper, column // 2, 0)
    lower, lower_sent = split_halves(lower, column % 2, 0)
    upper = upper + swap_y(upper_sent).astype(jnp.float32)
    lower = lower + swap_x(lower_sent).astype(jnp.float32)
    return (upper.astype(jnp.bfloat16), lower.astype(jnp.bfloat16))


def heads_forward(hidden, tokens, attn_block, norm_pair, layout, maps, tables):
    query, key, value, even_context, even_totals, keep, send = attend_first(
        tokens, attn_block, maps[0], tables[0], *layout
    )
    even, leaving = core_sum(keep, send)
    leaving, query = lax.optimization_barrier((leaving, query))
    even_near = swap_near(leaving)
    odd_context, odd_totals, keep, send = attend_second(attn_block, *layout, query, key, value)
    odd, leaving = core_sum_at_once(keep, send)
    odd_near = swap_near(leaving)
    even_results = add_and_norm(hidden[0], even, even_near, norm_pair)

    def finish(other):
        return add_and_norm(hidden[1], odd, after(odd_near, other), norm_pair)

    kept = (
        tokens,
        (query, key, value, even_totals, odd_totals),
        (even_context, odd_context),
    )
    return (even_results, finish, kept)


def units_forward(even_results, finish, unit_block, norm_pair):
    residual_one, normed, low = even_results
    even_all = (low, swap_core(low))
    keep, send = hidden_units(even_all, unit_block)
    even, leaving = core_sum_at_once(keep, send)
    residual_odd, normed_odd, low = finish(leaving)
    even_near = swap_near(leaving)
    odd_all = (low, swap_core(low))
    keep, send = hidden_units(odd_all, unit_block)
    odd, leaving = core_sum_at_once(keep, send)
    results = (
        add_and_norm(normed, even, even_near, norm_pair),
        add_and_norm(normed_odd, odd, swap_near(leaving), norm_pair),
    )
    residual, output, low = zip(*results)
    kept = ((residual_one, residual_odd), (*even_all, *odd_all), residual)
    return (output, low, kept)


def units_backward(kept, grad_two, low, unit_block, norm_pair):
    residual_one, normed_all = kept[3:5]
    grad_mlp = share(low)
    pairs, hidden, sums, nears = [], [], [], []
    for chunk in range(2):
        span = slice(2 * chunk, 2 * chunk + 2)
        pair, units, keep, send = units_back(normed_all[span], grad_mlp[span], unit_block)
        own, leaving = core_sum_at_once(keep, send)
        pairs.append(pair)
        hidden.append(units)
        sums.append(own)
        nears.append(swap_near(leaving))
    unit_grads = units_weights(normed_all, grad_mlp, pairs, hidden)
    nears, unit_grads = lax.optimization_barrier((nears, unit_grads))
    results = norm_back(grad_two, sums, nears, residual_one, norm_pair)
    return (*results, unit_grads)


def heads_backward(kept, low, attn_block, layout, maps, tables):
    tokens, heads_kept, context = kept[:3]
    grad_attn = share(low)
    grad_projected, *partial = attend_back(
        grad_attn, attn_block, maps[1], *tables[1:], *layout, heads_kept
    )
    return (partial, attend_weights(tokens, grad_attn, grad_projected, context))


def per_device(
    tokens,
    segment_ids,
    pair_doc,
    slot_of,
    master,
    first_moment,
    second_moment,
    norm_params,
    norm_first,
    norm_second,
):
    columns = lax.axis_size("g")
    owners = 2 * columns
    column = lax.axis_index("g")
    core = lax.axis_index("c")
    z_pair = lax.axis_index("zp")
    near_bit = lax.axis_index("a")
    width = master.shape[1]
    shard_rows = tokens.shape[0]
    in_place = core == z_pair
    seg_row = jnp.where(in_place, segment_ids, swap_core(segment_ids))[0]
    targets = jnp.where(in_place, pair_doc, swap_core(pair_doc))[0]
    member, positions, counts = segment_layout(seg_row, SEGS)
    even = near_bit == 0
    chunk_order = [2 * core, 2 * core ^ 2, 2 * core + 1, 2 * core + 1 ^ 2]

    def in_order(values):
        return jnp.concatenate(
            [
                lax.dynamic_slice_in_dim(values, index * shard_rows, shard_rows, 0)
                for index in chunk_order
            ],
            axis=0,
        )

    cosine, sine_table = rope_tables(in_order(positions), HEAD_DIM)
    heads = width // lax.axis_size(("zp", "a")) // HEAD_DIM
    maps = (spread_map(heads), unspread_map(heads))
    tables = (
        jnp.concatenate([cosine, sine_table], axis=1),
        jnp.concatenate([cosine, cosine], axis=1),
        jnp.concatenate([sine_table, sine_table], axis=1),
    )
    seg_local = in_order(seg_row)
    layout = (seg_local[:, None], seg_local[None, :])
    member = lax.dynamic_slice_in_dim(member, 2 * core * shard_rows, 2 * shard_rows, 0)
    member = member[:, : SEGS - 1].astype(jnp.float32)
    counted = jnp.arange(2 * shard_rows)[:, None] // shard_rows == near_bit
    own_member = jnp.where(counted, member, 0.0)
    piece_rows = width // owners

    def to_owners(blocks):
        return lax.all_to_all(blocks, ("g", "c"), split_axis=0, concat_axis=0, tiled=True)

    tokens_all = first_rows(tokens)
    outgoing = master.astype(jnp.bfloat16).reshape(OWN_MAX, owners, piece_rows, width)
    incoming = to_owners(outgoing.transpose(1, 0, 2, 3)).reshape(-1, piece_rows, width)
    lengths = counts[: SEGS - 1].astype(jnp.float32)[:, None]
    targets = jnp.pad(targets.astype(jnp.float32)[:, None], ((0, SEGS - 1 - QRY_DEV), (0, 127)))
    hidden = (tokens_all[0].astype(jnp.float32), tokens_all[2].astype(jnp.float32))
    early = (tokens_all, hidden, maps, tables, layout, lengths, targets, member, own_member)
    incoming, early = lax.optimization_barrier((incoming, early))
    tokens_all, hidden, maps, tables, layout, lengths, targets, member, own_member = early

    def piece_of(*matrices):
        return jnp.concatenate(
            [
                lax.dynamic_index_in_dim(incoming, slot_of[matrix], 0, keepdims=False)
                for matrix in matrices
            ],
            axis=1,
        )

    attn_pieces = to_working_block(piece_of(0))
    unit_pieces = to_working_block(piece_of(1, 2, 3))
    attn_block = gather_rest(*gather_half(*attn_pieces))
    unit_pieces, attn_block = lax.optimization_barrier((unit_pieces, attn_block))
    unit_block = gather_rows_of(*unit_pieces)
    kept_list, weight_list = [], []
    for layer_index in range(LAYERS):
        if layer_index > 0:
            tokens_all = share(low)
        norm_set = norm_params[layer_index]
        later = layer_index + 1 < LAYERS
        if later:
            base = 4 * (layer_index + 1)
            pieces = piece_of(base, base + 1, base + 2, base + 3)
            pieces = to_working_block(after(pieces, unit_pieces))
        weight_list.append((attn_block, unit_block))
        even_results, finish, heads_kept = heads_forward(
            hidden, tokens_all, attn_block, norm_set[:2], layout, maps, tables
        )
        if later:
            pieces, even_results = lax.optimization_barrier((pieces, even_results))
            attn_block = gather_rows_of(*[part[:, :width] for part in pieces])
        hidden, low, units_kept = units_forward(
            even_results, finish, unit_block, norm_set[2:]
        )
        if later:
            unit_pieces, low = lax.optimization_barrier(([part[:, width:] for part in pieces], low))
            unit_block = gather_rows_of(*unit_pieces)
        kept_list.append((*heads_kept, *units_kept))
    pool_part = pool(hidden, own_member)
    pool_part = pool_part + swap_core(pool_part)
    pooled_sum, sent = embed(pool_part, swap_near(pool_part), lengths, targets)
    far = swap_far(sent)
    pair = jnp.stack([jnp.where(z_pair == 0, sent, far), jnp.where(z_pair == 0, far, sent)])
    every = lax.all_gather(pair, "g", axis=0, tiled=True).reshape(-1, sent.shape[1])
    loss_total, gradient, low, second_params = loss_and_back(
        every,
        pooled_sum,
        lengths,
        member,
        (2 * column + z_pair).reshape(1, 1),
        kept_list[-1][-1],
        norm_params[LAYERS - 1, 2:],
    )
    norm_list = [None] * LAYERS
    pending = []
    for layer_index in reversed(range(LAYERS)):
        kept = kept_list[layer_index]
        attn_block, unit_block = weight_list[layer_index]
        grad_one, low, first_params, unit_grads = units_backward(
            kept, gradient, low, unit_block, norm_params[layer_index, :2]
        )
        norm_list[layer_index] = jnp.concatenate(
            [jnp.where(even, *first_params), jnp.where(even, *second_params)], axis=0
        )
        unit_pieces = scatter_rows_of(after(unit_grads, pending))
        pending, low = lax.optimization_barrier((pending, low))
        arriving = [from_working_block(*pieces) for pieces in pending]
        partial, attn_grads = heads_backward(kept, low, attn_block, layout, maps, tables)
        if layer_index > 0:
            sums, nears = [], []
            for chunk in range(2):
                own, leaving = core_sum_at_once(*partial[2 * chunk : 2 * chunk + 2])
                sums.append(own)
                nears.append(swap_near(leaving))
            nears, attn_grads = lax.optimization_barrier((nears, attn_grads))
            gradient, low, second_params = norm_back(
                grad_one,
                sums,
                nears,
                kept_list[layer_index - 1][-1],
                norm_params[layer_index - 1, 2:],
            )
            attn_pieces = scatter_rows_of(after(attn_grads, unit_pieces))
            pending = [
                tuple(
                    jnp.concatenate(halves, axis=1) for halves in zip(attn_pieces, unit_pieces)
                )
            ]
    partial, attn_grads = lax.optimization_barrier((partial, attn_grads))
    attn_halves = scatter_half(attn_grads)
    even_sum, even_low = core_sum(*partial[:2])
    odd_sum, odd_low = core_sum(*partial[2:])
    near = swap_near(jnp.where(even, odd_low, even_low))
    attn_halves, unit_pieces = lax.optimization_barrier((attn_halves, unit_pieces))
    unit_arrived = from_working_block(*unit_pieces)
    attn_arrived = from_working_block(*scatter_rest(*attn_halves))
    arrived = [attn_arrived, unit_arrived] + arriving
    arrived, near = lax.optimization_barrier((arrived, near))
    gradient = jnp.where(even, grad_one[0], grad_one[1])
    gradient = gradient + jnp.where(even, even_sum, odd_sum) + near.astype(jnp.float32)
    norm_stack = jnp.stack(norm_list).reshape(-1, width)
    gradient, norm_stack = after((gradient, norm_stack), attn_arrived)
    token_grad = turn(gradient.astype(jnp.bfloat16)).astype(jnp.float32)
    outgoing = jnp.zeros((OWN_MAX * owners, piece_rows, width), jnp.bfloat16)
    pieces = jnp.concatenate(arrived, axis=1).astype(jnp.bfloat16)
    for matrix in range(MATS):
        outgoing = lax.dynamic_update_index_in_dim(
            outgoing, pieces[:, matrix * width : (matrix + 1) * width], slot_of[matrix], 0
        )
    incoming = to_owners(outgoing.reshape(owners, OWN_MAX, piece_rows, width))
    slot_ids = (2 * column + core) * OWN_MAX + jnp.arange(OWN_MAX, dtype=jnp.int32)
    in_use = jnp.any(slot_of[None, :] == slot_ids[:, None], axis=1)
    norm_total = norm_stack + swap_core(norm_stack)
    norm_total = norm_total + swap_near(norm_total)
    norm_total = norm_total + swap_far(norm_total)
    if columns == 4:
        norm_total = norm_total + swap_x(norm_total)
        norm_total = norm_total + swap_y(norm_total)
    else:
        norm_total = jnp.sum(lax.all_gather(norm_total, "g", axis=0), axis=0)
    norm_total = norm_total.reshape(norm_params.shape)
    new_master, new_first, new_second, weight_copy = adam_slots(
        in_use, incoming, master, first_moment, second_moment
    )
    new_norm, new_norm_first, new_norm_second = adam_update(
        norm_params, norm_first, norm_second, norm_total, NORM_RATE
    )
    return (
        loss_total,
        token_grad,
        new_master,
        new_first,
        new_second,
        weight_copy,
        new_norm,
        new_norm_first,
        new_norm_second,
    )


def solution(mesh):
    owners, model_parts = mesh.devices.shape
    work_mesh = Mesh(mesh.devices.reshape(owners // 2, 2, model_parts // 2, 2), AXES)
    dp, mp = ("g", "c"), ("zp", "a")
    in_specs = (
        P(AXES, None),
        P(dp, None),
        P(dp, None),
        P(),
        P(dp, None, mp),
        P(dp, None, mp),
        P(dp, None, mp),
        P(),
        P(),
        P(),
    )
    out_specs = (
        P(),
        P(AXES, None),
        P(dp, None, mp),
        P(dp, None, mp),
        P(dp, None, mp),
        P(dp, None, mp),
        P(),
        P(),
        P(),
    )
    return jax.shard_map(
        per_device, mesh=work_mesh, in_specs=in_specs, out_specs=out_specs, check_vma=False
    )
```
